128 devices in a mesh: grp: 4 (over x_lo, core), blk: 32 (over z, x_hi, y).
Axes of the slice: x: 4 (x_hi: 2, x_lo: 2; x = x_hi * 2 + x_lo), y: 4, z: 4, core: 2. Of those that a mesh axis runs over, the one named last changes fastest.
Arguments:
- incident: float32 [768, 480], P(('grp', 'blk')), may hold values from -24 to 24
- sphere_site: int32 [768], replicated, may hold values from 0 to 767, each once
- jitter: float32 [3, 768], replicated, may hold values from -0.4 to 0.4
- rotation_table: bfloat16 [480, 480], replicated, may hold values from -0.25 to 0.25
- axial_tables: bfloat16 [2, 480, 480], replicated, may hold values from -0.25 to 0.25
- tmatrix: float32 [2, 240], replicated, may hold values from -0.3 to 0.3
- radius_factor: float32 [768], P(('grp', 'blk')), may hold values from 0.29 to 3.3
- probe_field: bfloat16 [32768, 480], P(('grp', 'blk')), may hold values from -0.25 to 0.25
- probe_group: int32 [32768], P(('grp', 'blk')), may hold values from 0 to 3
Outputs:
- solution: float32 [768, 480], P(('grp', 'blk'))
- sensitivity: float32 [768, 480], P(('grp', 'blk'))
- arnoldi: float32 [4], replicated
The draws below stay inside these ranges and needn't reach their ends.
Inputs may be any that keep to these rules, and one draw needn't show every extreme that they name: sphere_site is a permutation of the sites 0 to 767.
All inputs are finite; a program needn't handle non-finite values.
Results may differ from the reference program's by a relative error of at most 0.011.
Values sent between devices are 32-bit elements; how exact they have to be, the bound alone decides.
No kernel may reach another device: no remote copies, remote signals or barrier semaphores. Data moves between devices by JAX's collectives and lax.ppermute only.
A program may use at most 128 MiB of HBM per device.

```python
import jax
import jax.numpy as jnp
import numpy as np
from jax import lax

ORDER = 10
COEFF = 480
SPHERES = 768
PROBES = 32768
N_GRP = 4


def draw_incident(key, part):
    key = jax.random.fold_in(key, 11)
    position = jnp.arange(SPHERES, dtype=jnp.float32) / (SPHERES - 1)
    values = jnp.clip(jax.random.normal(key, (SPHERES, COEFF), jnp.float32), -6.0, 6.0)
    scales = 0.5 * jnp.exp(jnp.log(8.0) * position)
    return (values * scales[:, None]).astype(jnp.float32)


def draw_radius_factor(key, part):
    key = jax.random.fold_in(key, 12)
    position = jnp.arange(SPHERES, dtype=jnp.float32) / (SPHERES - 1)
    spread = jax.random.uniform(key, (SPHERES,), jnp.float32, 0.85, 1.15)
    scales = 0.5 * jnp.exp(jnp.log(4.0) * position)
    return (scales * spread).astype(jnp.float32)


def place_ends(drawn, rng, least, high):
    longest = drawn.shape.index(max(drawn.shape))
    spots = []
    for shift in (0, 1):
        where = [jax.random.randint(jax.random.fold_in(rng, axis), (), 0, length) for axis, length in enumerate(drawn.shape)]
        where[longest] = (where[longest] + shift) % drawn.shape[longest]
        spots.append(tuple(where))
    return drawn.at[spots[0]].set(least).at[spots[1]].set(high)


def shard_levels(key, dims, shards, least, high):
    level = 1.0
    for dim, parts in shards:
        draws = jax.random.uniform(jax.random.fold_in(jax.random.fold_in(key, 6), dim), (parts,), jnp.float32, least / len(shards), high / len(shards))
        level = level * jnp.repeat(jnp.exp(draws), dims[dim] // parts).reshape((-1,) + (1,) * (len(dims) - 1 - dim))
    return level


def centred(own_key, shape, width, bound, cuts=(), held_as=jnp.bfloat16):
    loudness = shard_levels(own_key, shape, cuts, -0.22, 0.18) if cuts else 1.0
    drawn = jax.random.normal(own_key, shape, jnp.float32) * width * loudness
    return jnp.minimum(jnp.maximum(drawn, -bound), bound).astype(held_as)


def setup_inputs(seed: int = 0) -> dict:
    arg_keys = jax.random.split(jax.random.key(seed), 10)
    return {
        "incident": draw_incident(jax.random.fold_in(arg_keys[9], 71), 0),
        "sphere_site": jax.random.permutation(arg_keys[1], SPHERES).astype(jnp.int32),
        "jitter": jnp.clip(jax.random.uniform(arg_keys[2], (3, SPHERES), jnp.float32, -0.4, 0.4), -0.4, 0.4),
        "rotation_table": centred(arg_keys[3], (COEFF, COEFF), COEFF ** -0.5, 0.25),
        "axial_tables": centred(arg_keys[4], (2, COEFF, COEFF), COEFF ** -0.5, 0.25),
        "tmatrix": jnp.clip(jax.random.uniform(arg_keys[5], (2, COEFF // 2), jnp.float32, -0.3, 0.3), -0.3, 0.3),
        "radius_factor": draw_radius_factor(jax.random.fold_in(arg_keys[9], 71), 0),
        "probe_field": centred(arg_keys[7], (PROBES, COEFF), COEFF ** -0.5, 0.25, ((0, 128),)),
        "probe_group": place_ends(jax.random.randint(arg_keys[8], (PROBES,), 0, N_GRP), jax.random.fold_in(arg_keys[8], 1), 0, N_GRP - 1).astype(jnp.int32),
    }


WAVENUMBER = 1.3
LATTICE_STEP = 2.5

def order_table(degree_max):
    entries = np.arange(degree_max * (degree_max + 2))
    degree = np.floor(np.sqrt(entries + 1.0) + 1e-09)
    orders = entries + 1 - degree * degree - degree
    return np.concatenate([orders, orders]).astype(np.float32)

def positions(sphere_site, jitter):
    lattice_xyz = jnp.stack([sphere_site % 8, sphere_site // 8 % 8, sphere_site // 64]).astype(jnp.float32)
    return lattice_xyz * LATTICE_STEP + jitter

def geometry(out_places, out_ids, src_places, src_ids, flip, orders):
    factor = -1.0 if flip else 1.0
    offset = (out_places[:, :, None] - src_places[:, None, :]) * factor
    self_pair = out_ids[:, None] == src_ids[None, :]
    dist_sq = lax.optimization_barrier(jnp.sum(offset * offset, axis=0))
    distance = jnp.sqrt(jnp.where(self_pair, 1.0, dist_sq))
    azimuth = jnp.arctan2(offset[1], offset[0])
    phase_arg = WAVENUMBER * distance
    radial_cos = jnp.where(self_pair, 0.0, jnp.cos(phase_arg) / phase_arg)
    radial_sin = jnp.where(self_pair, 0.0, jnp.sin(phase_arg) / phase_arg)
    phase = azimuth[:, :, None] * orders
    return (jnp.cos(phase), jnp.sin(phase), radial_cos, radial_sin)

def translate(source, pair_geometry, rotation_table, axial_pair):
    cos_rot, sin_rot, radial_cos, radial_sin = pair_geometry
    out_count, src_count, half_width = cos_rot.shape
    full_width = 2 * half_width
    source_real = source[None, :, :half_width]
    source_imag = source[None, :, half_width:]
    rotated = jnp.concatenate([cos_rot * source_real - sin_rot * source_imag, sin_rot * source_real + cos_rot * source_imag], axis=2).astype(jnp.bfloat16)
    flattened = rotated.reshape(out_count * src_count, full_width)
    turned = jnp.dot(flattened, rotation_table, preferred_element_type=jnp.float32).astype(jnp.bfloat16)
    axial_out = jnp.dot(turned, axial_pair, preferred_element_type=jnp.float32)
    shifted = (radial_cos.reshape(-1, 1) * axial_out[:, :full_width] + radial_sin.reshape(-1, 1) * axial_out[:, full_width:]).astype(jnp.bfloat16)
    returned = lax.dot_general(shifted, rotation_table, (((1,), (1,)), ((), ())), preferred_element_type=jnp.float32).reshape(out_count, src_count, full_width)
    back_real = returned[:, :, :half_width]
    back_imag = returned[:, :, half_width:]
    return jnp.concatenate([lax.optimization_barrier(jnp.sum(cos_rot * back_real + sin_rot * back_imag, axis=1)), lax.optimization_barrier(jnp.sum(cos_rot * back_imag - sin_rot * back_real, axis=1))], axis=1)

def scatter_apply(field, tmatrix, radius):
    half_width = tmatrix.shape[1]
    real_part, imag_part = (tmatrix[0], tmatrix[1])
    field_real, field_imag = (field[:, :half_width], field[:, half_width:])
    return jnp.concatenate([real_part * field_real - imag_part * field_imag, imag_part * field_real + real_part * field_imag], axis=1) * radius[:, None]

def scatter_adjoint(field, tmatrix, radius):
    half_width = tmatrix.shape[1]
    real_part, imag_part = (tmatrix[0], tmatrix[1])
    field_real, field_imag = (field[:, :half_width], field[:, half_width:])
    return jnp.concatenate([real_part * field_real + imag_part * field_imag, real_part * field_imag - imag_part * field_real], axis=1) * radius[:, None]

def field_all(source, places, flip, rotation_table, axial_pair, orders):
    sphere_count = places.shape[1]
    everyone = jnp.arange(sphere_count, dtype=jnp.int32)

    def block_field(first):
        out_ids = first + jnp.arange(16, dtype=jnp.int32)
        out_places = lax.dynamic_slice_in_dim(places, first, 16, 1)
        pair_geometry = geometry(out_places, out_ids, places, everyone, flip, orders)
        return translate(source, pair_geometry, rotation_table, axial_pair)
    starts = jnp.arange(0, sphere_count, 16, dtype=jnp.int32)
    return lax.map(block_field, starts).reshape(sphere_count, -1)

def reference(incident, sphere_site, jitter, rotation_table, axial_tables, tmatrix, radius_factor, probe_field, probe_group):
    orders = jnp.asarray(order_table(ORDER))
    places = positions(sphere_site, jitter)
    forward_pair = jnp.concatenate([axial_tables[0], axial_tables[1]], axis=1)
    adjoint_pair = jnp.concatenate([axial_tables[0].T, axial_tables[1].T], axis=1)

    def forward(vector):
        return vector - scatter_apply(field_all(vector, places, False, rotation_table, forward_pair, orders), tmatrix, radius_factor)

    def adjoint(vector):
        return vector - field_all(scatter_adjoint(vector, tmatrix, radius_factor), places, True, rotation_table, adjoint_pair, orders)
    initial_norm = jnp.sqrt(jnp.sum(incident * incident))
    basis_first = incident / initial_norm
    image_first = forward(basis_first)
    diag_first = jnp.sum(basis_first * image_first)
    ortho_first = image_first - diag_first * basis_first
    below_first = jnp.sqrt(jnp.sum(ortho_first * ortho_first))
    basis_second = ortho_first / below_first
    image_second = forward(basis_second)
    upper_second = jnp.sum(basis_first * image_second)
    diag_second = jnp.sum(basis_second * image_second)
    ortho_second = image_second - upper_second * basis_first - diag_second * basis_second
    rest_second = jnp.sum(ortho_second * ortho_second)
    gram_first = diag_first * diag_first + below_first * below_first
    gram_cross = diag_first * upper_second + below_first * diag_second
    gram_second = upper_second * upper_second + diag_second * diag_second + rest_second
    determinant = gram_first * gram_second - gram_cross * gram_cross
    coeff_first = initial_norm * (diag_first * gram_second - upper_second * gram_cross) / determinant
    coeff_second = initial_norm * (gram_first * upper_second - gram_cross * diag_first) / determinant
    solution = coeff_first * basis_first + coeff_second * basis_second
    arnoldi = jnp.stack([diag_first, below_first, diag_second, rest_second]).astype(jnp.float32)
    groups = N_GRP
    per_group = SPHERES // groups
    totals = lax.optimization_barrier(jnp.sum(solution.reshape(groups, per_group, -1), axis=1)) / jnp.sqrt(jnp.float32(per_group))
    totals_low = totals.astype(jnp.bfloat16)
    probe_values = lax.dot_general(probe_field, totals_low, (((1,), (1,)), ((), ())), preferred_element_type=jnp.float32)
    selector = (probe_group[:, None] == jnp.arange(groups, dtype=jnp.int32)[None, :]).astype(jnp.float32)
    weighted = (selector * probe_values).astype(jnp.bfloat16)
    gradient = lax.dot_general(weighted, probe_field, (((0,), (0,)), ((), ())), preferred_element_type=jnp.float32) * (COEFF * groups / PROBES)
    source = jnp.repeat(gradient, per_group, axis=0)
    sensitivity = adjoint(source)
    return (solution, sensitivity, arnoldi)
```

```python
import jax
import jax.numpy as jnp
import numpy as np
from jax import lax
from jax.experimental import pallas as pl
from jax.experimental.pallas import tpu as pltpu
from jax.sharding import Mesh
from jax.sharding import PartitionSpec as P

ORDER = 10
WAVENUMBER = 1.3
LATTICE_STEP = 2.5

SPHERES = 768
COEFF = 480
HALF = 240
GROUPS = 4
PER_GROUP = SPHERES // GROUPS
PROBES = 32768
OWN = 6
PROBES_OWN = 256
LANES = 128
WIDE = 256
FULL = 2 * WIDE
ROWS = 8
BLOCK = 2 * ROWS
BLOCKS = 4 * ORDER + 1
TOP = 2 * ORDER
CHUNK = OWN * FULL // LANES
FAR = 64
SCALE = 2.0**-14
PAD = HALF
BF = jnp.bfloat16
F32 = jnp.float32

FAR_AXES = ("xl", "z", "xh", "y")
ALL_AXES = ("xl", "co", "z", "xh", "y")


def order_table(degree_max):
    entries = np.arange(degree_max * (degree_max + 2))
    degree = np.floor(np.sqrt(entries + 1.0) + 1e-09)
    orders = entries + 1 - degree * degree - degree
    return np.concatenate([orders, orders]).astype(np.int32)


_ORDERS = order_table(ORDER)
_SORTED = np.lexsort((_ORDERS, np.abs(_ORDERS)))
_SOURCE = np.full((1, FULL), -1, np.int32)
_SOURCE[0, :HALF] = _SORTED
_SOURCE[0, WIDE : WIDE + HALF] = _SORTED + HALF
_LANE_ORDER = np.full((1, WIDE), 99, np.int32)
_LANE_ORDER[0, :HALF] = _ORDERS[_SORTED]
_SIGN = np.zeros((1, WIDE), np.float32)
_SIGN[0, :HALF] = np.sign(_ORDERS[_SORTED])


def classes_of(half):
    part = _LANE_ORDER[0, half * LANES : (half + 1) * LANES]
    return [int(m) for m in np.unique(part[part < 99])]


CLASSES = (classes_of(0), classes_of(1))


def dot(a, b):
    return jnp.dot(a, b, preferred_element_type=F32)


def dot_t(a, b):
    return lax.dot_general(a, b, (((1,), (1,)), ((), ())), preferred_element_type=F32)


def split(x):
    high = x.astype(BF)
    return high, (x - high.astype(F32)).astype(BF)


def exact_dot(x, onehot):
    high = x.astype(BF)
    rest = x - high.astype(F32)
    mid = rest.astype(BF)
    low = (rest - mid.astype(F32)).astype(BF)
    return dot(high, onehot) + dot(mid, onehot) + dot(low, onehot)


def onehot_in(source):
    rows = lax.broadcasted_iota(jnp.int32, (COEFF, FULL), 0)
    return jnp.where(rows == source, 1.0, 0.0).astype(BF)


def onehot_out(source_column):
    lanes = lax.broadcasted_iota(jnp.int32, (FULL, COEFF), 1)
    return jnp.where(lanes == source_column, 1.0, 0.0).astype(BF)


def own_group():
    return lax.axis_index("xl") * 2 + lax.axis_index("co")


def send_body(incident, source, radius, chunk, rows_out, radius_out, lines):
    value = jnp.concatenate([incident[...], jnp.zeros((ROWS - OWN, COEFF), F32)], axis=0) * SCALE
    rows = exact_dot(value, onehot_in(source[...]))
    rows_out[...] = rows
    lane = lax.broadcasted_iota(jnp.int32, (ROWS, FULL), 1)
    line = lax.broadcasted_iota(jnp.int32, (ROWS, LANES), 0)
    column = jnp.zeros((ROWS, LANES), F32)
    for r in range(OWN):
        column = jnp.where(line == r, radius[r], column)
    radius_out[...] = column
    marked = jnp.where(lane == PAD + own_group(), jnp.concatenate([column] * 4, axis=1), rows)
    write_chunks(marked, chunk, lines)


def write_chunks(rows, chunk, lines):
    for part in range(4):
        lines[pl.ds(part, ROWS, stride=4), :] = rows[:, part * LANES : (part + 1) * LANES]
    once = lines[:CHUNK, :]
    for far in range(FAR):
        chunk[far] = once


def prepare_body(
    site, jitter, rotation, axial, probes, tmat, source, source_column,
    pairs, tables, tables_t, probes_out, tmat_out,
):
    own = (
        (lax.axis_index("co") * 2 + lax.axis_index("xl")) * PER_GROUP
        + ((lax.axis_index("z") * 2 + lax.axis_index("xh")) * 4 + lax.axis_index("y")) * OWN
    )
    sites = site[...]
    place_x = (sites & 7).astype(F32) * LATTICE_STEP + jitter[0:1, :]
    place_y = ((sites >> 3) & 7).astype(F32) * LATTICE_STEP + jitter[1:2, :]
    place_z = (sites >> 6).astype(F32) * LATTICE_STEP + jitter[2:3, :]
    lane = lax.broadcasted_iota(jnp.int32, (ROWS, SPHERES), 1)
    line = lax.broadcasted_iota(jnp.int32, (ROWS, SPHERES), 0)
    same = lane == line + own

    def offset(place):
        here = jnp.sum(jnp.where(same, place, 0.0), axis=1, keepdims=True)
        return here - place

    dx, dy, dz = offset(place_x), offset(place_y), offset(place_z)
    distance = jnp.sqrt(jnp.where(same, 1.0, dx * dx + dy * dy + dz * dz))
    phase = WAVENUMBER * distance
    none = same | (line >= OWN)
    radial_cos = jnp.where(none, 0.0, jnp.cos(phase) / phase)
    radial_sin = jnp.where(none, 0.0, jnp.sin(phase) / phase)
    larger = jnp.maximum(jnp.abs(dx), jnp.abs(dy))
    apart = larger > 0.0
    inverse = 1.0 / jnp.where(apart, larger, 1.0)
    ax, ay = dx * inverse, dy * inverse
    length = jnp.sqrt(jnp.where(apart, ax * ax + ay * ay, 1.0))
    cos_one = jnp.where(apart, ax / length, 1.0)
    sin_one = jnp.where(apart, ay / length, 0.0)

    def put(block, factor):
        value = jnp.concatenate([radial_cos * factor, radial_sin * factor], axis=0)
        pairs[block * BLOCK : (block + 1) * BLOCK, :] = value.astype(BF)

    pairs[0:BLOCK, :] = jnp.concatenate([radial_cos, radial_sin], axis=0).astype(BF)
    cos_k, sin_k = cos_one, sin_one
    for k in range(1, TOP + 1):
        put(k, cos_k)
        put(TOP + k, sin_k)
        if k < TOP:
            cos_k, sin_k = (
                cos_k * cos_one - sin_k * sin_one,
                sin_k * cos_one + cos_k * sin_one,
            )

    inwards = onehot_in(source[...])
    outwards = onehot_out(source_column[...])
    turned = dot(outwards, rotation[...]).astype(BF)
    for radial in range(2):
        mixed_high, mixed_low = split(0.5 * dot(turned, axial[radial]))
        tables[radial] = (dot_t(mixed_high, turned) + dot_t(mixed_low, turned)).astype(BF)
        tables_t[radial] = (dot_t(turned, mixed_high) + dot_t(turned, mixed_low)).astype(BF)
    probes_out[...] = dot(probes[...], inwards).astype(BF)
    tmat_rows = jnp.concatenate([tmat[...], jnp.zeros((ROWS - 2, HALF), F32)], axis=0)
    tmat_out[...] = exact_dot(tmat_rows, inwards[:HALF, :WIDE])


def load_rows(gathered, rows):
    for part in range(4):
        lines = gathered[pl.ds(part, SPHERES, stride=4), :]
        rows[:, part * LANES : (part + 1) * LANES] = lines.astype(BF)


def group_sums(gathered):
    groups = []
    for place in (0, 2, 1, 3):
        parts = []
        for part in range(4):
            lines = gathered[pl.ds(place * PER_GROUP * 4 + part, PER_GROUP, stride=4), :]
            parts.append(jnp.sum(lines, axis=0, keepdims=True))
        groups.append(jnp.concatenate(parts, axis=1))
    return jnp.concatenate(groups, axis=0)


def mix(sums, shifted, tables, lane_order, sign):
    for k in range(1, TOP + 1):
        at_cos, at_sin = pl.ds(k * BLOCK, BLOCK), pl.ds((TOP + k) * BLOCK, BLOCK)
        cos_re, cos_im = sums[at_cos, :WIDE], sums[at_cos, WIDE:]
        sin_re, sin_im = sums[at_sin, :WIDE], sums[at_sin, WIDE:]
        sums[at_cos, :WIDE] = cos_re - sin_im
        sums[at_cos, WIDE:] = cos_im + sin_re
        sums[at_sin, :WIDE] = cos_re + sin_im
        sums[at_sin, WIDE:] = cos_im - sin_re

    def block_of(k):
        return (k if k >= 0 else TOP - k) * BLOCK

    for half in range(2):
        orders = jnp.broadcast_to(lane_order[:, half * LANES : (half + 1) * LANES], (BLOCK, LANES))
        masks = [orders == m for m in CLASSES[half]]

        def pick(out_order, start):
            columns = slice(start + half * LANES, start + (half + 1) * LANES)
            value = None
            for m, mask in zip(CLASSES[half], masks):
                row = block_of(m - out_order)
                here = sums[row : row + BLOCK, columns]
                value = here if value is None else jnp.where(mask, here, value)
            return value

        for out_order in range(ORDER + 1):
            minus_re, minus_im = pick(out_order, 0), pick(out_order, WIDE)
            if out_order:
                plus_re, plus_im = pick(-out_order, 0), pick(-out_order, WIDE)
            else:
                plus_re, plus_im = minus_re, minus_im
            cos_part = (minus_re + plus_re, minus_im + plus_im)
            sin_part = (plus_im - minus_im, minus_re - plus_re)
            for which, start in ((0, 0), (1, WIDE)):
                columns = slice(start + half * LANES, start + (half + 1) * LANES)
                for radial in range(2):
                    lines = slice(radial * ROWS, (radial + 1) * ROWS)
                    value = jnp.concatenate([cos_part[which][lines], sin_part[which][lines]], axis=0)
                    shifted[radial, out_order * BLOCK : (out_order + 1) * BLOCK, columns] = value.astype(BF)

    back = dot(shifted[0], tables[0]) + dot(shifted[1], tables[1])
    parts_re, parts_im = [], []
    for half in range(2):
        columns = slice(half * LANES, (half + 1) * LANES)
        orders = jnp.abs(jnp.broadcast_to(lane_order[:, columns], (ROWS, LANES)))
        signs = sign[:, columns]
        field_re = field_im = None
        for m in sorted({abs(c) for c in CLASSES[half]}):
            cos_lines = slice(m * BLOCK, m * BLOCK + ROWS)
            sin_lines = slice(m * BLOCK + ROWS, (m + 1) * BLOCK)
            real, imag = columns, slice(WIDE + half * LANES, WIDE + (half + 1) * LANES)
            value_re = back[cos_lines, real] + signs * back[sin_lines, imag]
            value_im = back[cos_lines, imag] - signs * back[sin_lines, real]
            field_re = value_re if field_re is None else jnp.where(orders == m, value_re, field_re)
            field_im = value_im if field_im is None else jnp.where(orders == m, value_im, field_im)
        parts_re.append(field_re)
        parts_im.append(field_im)
    return jnp.concatenate(parts_re + parts_im, axis=1)


def scatter(field, tmat, radius):
    real, imag = tmat[0:1, :], tmat[1:2, :]
    field_re, field_im = field[:, :WIDE], field[:, WIDE:]
    wide = jnp.concatenate([radius, radius], axis=1)
    return jnp.concatenate(
        [
            wide * (imag * field_im - real * field_re),
            -wide * (imag * field_re + real * field_im),
        ],
        axis=1,
    )


def first_body(
    gathered, pairs, tables, tmat, radius, lane_order, sign,
    chunk, rows_out, weights_out, totals_out, rows, sums, shifted, lines,
):
    load_rows(gathered, rows)
    totals_out[...] = group_sums(gathered)
    sums[...] = dot(pairs[...], rows[...])
    for block in range(BLOCKS):
        k = block if block <= TOP else block - TOP
        at = pl.ds(block * BLOCK, BLOCK)
        value = sums[at, LANES:WIDE]
        weights_out[at, :] = (value if k % 2 == 0 else -value).astype(BF)
    field = mix(sums, shifted, tables, lane_order, sign)
    image = scatter(field, tmat, radius[...])
    rows_out[...] = image
    write_chunks(image, chunk, lines)


def gradient_body(gathered, totals_first, probes, probe_group, keep, send):
    totals = jnp.concatenate([totals_first[...], group_sums(gathered)], axis=0)
    lane = lax.broadcasted_iota(jnp.int32, (2 * GROUPS, FULL), 1)
    totals = jnp.where((lane & (WIDE - 1)) < HALF, totals, 0.0)
    total_high, total_low = split(totals)
    values = dot_t(total_high, probes[...]) + dot_t(total_low, probes[...])
    line = lax.broadcasted_iota(jnp.int32, (2 * GROUPS, PROBES_OWN), 0)
    values = jnp.where((line & (GROUPS - 1)) == probe_group[...], values, 0.0)
    value_high, value_low = split(values)
    gradient = dot(value_high, probes[...]) + dot(value_low, probes[...])
    core = lax.axis_index("co")
    first, second = gradient[:GROUPS], gradient[GROUPS:]
    keep[...] = jnp.where(core == 0, first, second)
    send[...] = jnp.where(core == 0, second, first)


def second_body(
    gathered, pairs, tables, tmat, radius, lane_order, sign, base, image,
    scalars, rows, sums, shifted,
):
    load_rows(gathered, rows)
    sums[...] = dot(pairs[...], rows[...])
    field = mix(sums, shifted, tables, lane_order, sign)
    last = scatter(field, tmat, radius[...])
    zero, one = base[...], image[...]
    line = lax.broadcasted_iota(jnp.int32, (GROUPS, FULL), 0)
    lane = lax.broadcasted_iota(jnp.int32, (GROUPS, FULL), 1)
    out = jnp.zeros((GROUPS, FULL), F32)
    pairs_of = ((zero, zero), (zero, one), (one, one), (zero, last), (one, last), (last, last))
    for index, (a, b) in enumerate(pairs_of):
        out = jnp.where((line == 0) & (lane == PAD + index), jnp.sum(a * b), out)
    scalars[...] = out


def finish_body(
    parts, weights, tables_t, tmat, lane_order, sign, source_column, incident, image,
    solution_out, sensitivity_out, arnoldi_out, places, sums, shifted,
):
    first = jnp.sum(parts[0], axis=0)
    second = jnp.sum(parts[1], axis=0)
    scal = (first + second)[0:1, :]
    g00, s01, s11, s02, s12, s22 = [scal[:, PAD + i : PAD + i + 1] for i in range(6)]
    g01, g11, g02, g12, g22 = s01 / g00, s11 / g00, s02 / g00, s12 / g00, s22 / g00
    diag_first = 1.0 + g01
    below_sq = g11 - g01 * g01
    below_first = jnp.sqrt(below_sq)
    upper_second = (g02 - g01 * g01) / below_first
    shift_second = (g12 - g01 * g11 - g01 * g02 + g01 * g01 * g01) / below_sq
    diag_second = 1.0 + shift_second
    norm_sq = (g22 - 2.0 * g01 * g12 + g01 * g01 * g11) / below_sq
    rest_second = norm_sq - upper_second * upper_second - shift_second * shift_second
    gram_first = diag_first * diag_first + below_sq
    gram_cross = diag_first * upper_second + below_first * diag_second
    gram_second = upper_second * upper_second + diag_second * diag_second + rest_second
    determinant = gram_first * gram_second - gram_cross * gram_cross
    step_first = (diag_first * gram_second - upper_second * gram_cross) / determinant
    step_second = (gram_first * upper_second - gram_cross * diag_first) / determinant
    for_image = step_second / below_first
    for_base = step_first - for_image * g01
    arnoldi_out[0] = diag_first[0, 0]
    arnoldi_out[1] = below_first[0, 0]
    arnoldi_out[2] = diag_second[0, 0]
    arnoldi_out[3] = rest_second[0, 0]

    factor = COEFF * GROUPS / PROBES / SCALE / float(np.sqrt(np.float32(PER_GROUP)))
    gradient = (for_base * first + for_image * second) * factor
    real, imag = tmat[0:1, :], tmat[1:2, :]
    grad_re, grad_im = gradient[:, :WIDE], gradient[:, WIDE:]
    places[...] = jnp.zeros((LANES, FULL), F32)
    at = pl.ds(PAD - LANES, GROUPS)
    places[at, :WIDE] = real * grad_re + imag * grad_im
    places[at, WIDE:] = real * grad_im - imag * grad_re
    sums[...] = dot(weights[...], places[...].astype(BF))
    field = mix(sums, shifted, tables_t, lane_order, sign)
    group = own_group()
    own = jnp.zeros((1, FULL), F32)
    for g in range(GROUPS):
        own = jnp.where(group == g, gradient[g : g + 1, :], own)
    lane = lax.broadcasted_iota(jnp.int32, (1, FULL), 1)
    own = jnp.where((lane & (WIDE - 1)) < HALF, own, 0.0)
    both = jnp.concatenate([image[...], own - field], axis=0)
    result = exact_dot(both, onehot_out(source_column[...]))
    image_rows = result[:OWN]
    solution_out[...] = for_base * incident[...] + (for_image / SCALE) * image_rows
    sensitivity_out[...] = result[ROWS : ROWS + OWN]


def call(body, outs, scratch=(), operands=(), smem=(), smem_outs=(), cost=None):
    vmem = pl.BlockSpec(memory_space=pltpu.VMEM)
    scalar = pl.BlockSpec(memory_space=pltpu.SMEM)
    return pl.pallas_call(
        body,
        out_shape=[jax.ShapeDtypeStruct(shape, kind) for shape, kind in outs],
        in_specs=[scalar if i in smem else vmem for i in range(len(operands))],
        out_specs=[scalar if i in smem_outs else vmem for i in range(len(outs))],
        scratch_shapes=list(scratch),
        compiler_params=pltpu.CompilerParams(vmem_limit_bytes=40 * 1024 * 1024),
        cost_estimate=cost,
    )(*operands)


def exchange(chunk):
    far = lax.all_to_all(chunk, FAR_AXES, 0, 0)
    return lax.all_gather(far, "co").reshape(2 * FAR * CHUNK, LANES)


def on_device(
    incident,
    sphere_site,
    jitter,
    rotation_table,
    axial_tables,
    tmatrix,
    radius_factor,
    probe_field,
    probe_group,
):
    source = jnp.asarray(_SOURCE)
    source_column = jnp.asarray(_SOURCE.reshape(FULL, 1))
    lane_order = jnp.asarray(_LANE_ORDER)
    sign = jnp.asarray(_SIGN)

    chunk, base, radius = call(
        send_body,
        [((FAR, CHUNK, LANES), F32), ((ROWS, FULL), F32), ((ROWS, LANES), F32)],
        [pltpu.VMEM((4 * ROWS, LANES), F32)],
        (incident, source, radius_factor),
        smem=(2,),
    )
    gathered_base = exchange(chunk)

    def by_core(array):
        lead = array.shape[:-1]
        return jnp.swapaxes(array.reshape(lead + (2, 2, PER_GROUP)), -3, -2).reshape(lead + (SPHERES,))

    pairs, tables, tables_t, probes, tmat = call(
        prepare_body,
        [
            ((BLOCKS * BLOCK, SPHERES), BF),
            ((2, FULL, FULL), BF),
            ((2, FULL, FULL), BF),
            ((PROBES_OWN, FULL), BF),
            ((ROWS, WIDE), F32),
        ],
        operands=(
            by_core(sphere_site[None, :]),
            by_core(jitter),
            rotation_table,
            axial_tables,
            probe_field,
            tmatrix,
            source,
            source_column,
        ),
        cost=pl.CostEstimate(flops=6_000_000_000, bytes_accessed=8_000_000, transcendentals=20_000),
    )

    row_scratch = pltpu.VMEM((SPHERES, FULL), BF)
    sum_scratch = pltpu.VMEM((BLOCKS * BLOCK, FULL), F32)
    shift_scratch = pltpu.VMEM((2, (ORDER + 1) * BLOCK, FULL), BF)
    line_scratch = pltpu.VMEM((4 * ROWS, LANES), F32)

    chunk, image, weights, totals_first = call(
        first_body,
        [
            ((FAR, CHUNK, LANES), F32),
            ((ROWS, FULL), F32),
            ((BLOCKS * BLOCK, LANES), BF),
            ((GROUPS, FULL), F32),
        ],
        [row_scratch, sum_scratch, shift_scratch, line_scratch],
        (gathered_base, pairs, tables, tmat, radius, lane_order, sign),
    )
    gathered_image = exchange(chunk)

    keep, send = call(
        gradient_body,
        [((GROUPS, FULL), F32), ((GROUPS, FULL), F32)],
        operands=(gathered_image, totals_first, probes, probe_group.reshape(1, PROBES_OWN)),
    )
    received = lax.ppermute(send, "co", [(0, 1), (1, 0)])
    (scalars,) = call(
        second_body,
        [((GROUPS, FULL), F32)],
        [row_scratch, sum_scratch, shift_scratch],
        (gathered_image, pairs, tables, tmat, radius, lane_order, sign, base, image),
        cost=pl.CostEstimate(flops=1_000_000_000, bytes_accessed=8_000_000, transcendentals=0),
    )
    lane = jnp.arange(FULL, dtype=jnp.int32)
    share = jnp.where((lane & (WIDE - 1)) < HALF, keep + received, scalars)
    spread = jnp.broadcast_to(share[None], (FAR, GROUPS, FULL))
    parts = lax.all_gather(lax.all_to_all(spread, FAR_AXES, 0, 0), "co")
    solution_rows, sensitivity_rows, arnoldi = call(
        finish_body,
        [((OWN, COEFF), F32), ((OWN, COEFF), F32), ((4,), F32)],
        [pltpu.VMEM((LANES, FULL), F32), sum_scratch, shift_scratch],
        (parts, weights, tables_t, tmat, lane_order, sign, source_column, incident, image),
        smem_outs=(2,),
    )
    return solution_rows, sensitivity_rows, arnoldi


def solution(mesh):
    fine = Mesh(mesh.devices.reshape(2, 2, 4, 2, 4), ALL_AXES)
    split_rows = P(ALL_AXES)
    return jax.shard_map(
        on_device,
        mesh=fine,
        in_specs=(
            P(ALL_AXES, None),
            P(),
            P(),
            P(),
            P(),
            P(),
            split_rows,
            P(ALL_AXES, None),
            split_rows,
        ),
        out_specs=(P(ALL_AXES, None), P(ALL_AXES, None), P()),
        check_vma=False,
    )
```

```python
import jax
import jax.numpy as jnp
import numpy as np
from jax import lax
from jax.experimental import pallas as pl
from jax.experimental.pallas import tpu as pltpu
from jax.sharding import Mesh
from jax.sharding import PartitionSpec as P

ORDER = 10
WAVENUMBER = 1.3
LATTICE_STEP = 2.5

SPHERES = 768
COEFF = 480
HALF = 240
GROUPS = 4
PER_GROUP = SPHERES // GROUPS
PROBES = 32768
OWN = 6
PROBES_OWN = 256
LANES = 128
WIDE = 256
FULL = 2 * WIDE
ROWS = 8
BLOCK = 2 * ROWS
BLOCKS = 4 * ORDER + 1
TOP = 2 * ORDER
CHUNK = OWN * FULL // LANES
FAR = 64
SCALE = 2.0**-14
PAD = HALF
BF = jnp.bfloat16
F32 = jnp.float32

FAR_AXES = ("xl", "z", "xh", "y")
ALL_AXES = ("xl", "co", "z", "xh", "y")


def order_table(degree_max):
    entries = np.arange(degree_max * (degree_max + 2))
    degree = np.floor(np.sqrt(entries + 1.0) + 1e-09)
    orders = entries + 1 - degree * degree - degree
    return np.concatenate([orders, orders]).astype(np.int32)


_ORDERS = order_table(ORDER)
_SORTED = np.lexsort((_ORDERS, np.abs(_ORDERS)))
_SOURCE = np.full((1, FULL), -1, np.int32)
_SOURCE[0, :HALF] = _SORTED
_SOURCE[0, WIDE : WIDE + HALF] = _SORTED + HALF


def spans(half):
    part = _ORDERS[_SORTED][half * LANES : (half + 1) * LANES]
    found = []
    for order in dict.fromkeys(int(m) for m in part):
        lanes = np.flatnonzero(part == order)
        found.append((order, int(lanes[0]), int(lanes[-1]) + 1))
    return found


SPANS = (spans(0), spans(1))


def by_lane(lane, entries):
    chosen = entries[-1][0]
    for value, end in reversed(entries[:-1]):
        chosen = jnp.where(lane < end, value, chosen)
    return chosen


def dot(a, b):
    return jnp.dot(a, b, preferred_element_type=F32)


def dot_t(a, b):
    return lax.dot_general(a, b, (((1,), (1,)), ((), ())), preferred_element_type=F32)


def split(x):
    high = x.astype(BF)
    return high, (x - high.astype(F32)).astype(BF)


def exact_dot(x, onehot, dot=dot):
    high = x.astype(BF)
    rest = x - high.astype(F32)
    mid = rest.astype(BF)
    low = (rest - mid.astype(F32)).astype(BF)
    return dot(high, onehot) + dot(mid, onehot) + dot(low, onehot)


def onehot_in(source):
    rows = lax.broadcasted_iota(jnp.int32, (COEFF, FULL), 0)
    return jnp.where(rows == source, 1.0, 0.0).astype(BF)


def own_group():
    return lax.axis_index("xl") * 2 + lax.axis_index("co")


def send_body(incident, source, radius, chunk, rows_out, radius_out, lines, held, held_source, held_radius, sems):
    copies = [
        pltpu.make_async_copy(incident, held.at[pl.ds(0, OWN), :], sems.at[0]),
        pltpu.make_async_copy(source, held_source, sems.at[1]),
        pltpu.make_async_copy(radius, held_radius, sems.at[2]),
    ]
    for copy in copies:
        copy.start()
    for copy in copies:
        copy.wait()
    value = jnp.concatenate([held[:OWN, :], jnp.zeros((ROWS - OWN, COEFF), F32)], axis=0) * SCALE
    rows = exact_dot(value, onehot_in(held_source[...]))
    rows_out[...] = rows
    lane = lax.broadcasted_iota(jnp.int32, (ROWS, FULL), 1)
    line = lax.broadcasted_iota(jnp.int32, (ROWS, LANES), 0)
    column = jnp.zeros((ROWS, LANES), F32)
    for r in range(OWN):
        column = jnp.where(line == r, held_radius[r], column)
    radius_out[...] = column
    marked = jnp.where(lane == PAD + own_group(), jnp.concatenate([column] * 4, axis=1), rows)
    write_chunks(marked, chunk, lines)


def write_chunks(rows, chunk, lines):
    for part in range(4):
        lines[pl.ds(part, ROWS, stride=4), :] = rows[:, part * LANES : (part + 1) * LANES]
    once = lines[:CHUNK, :]
    for far in range(FAR):
        chunk[far] = once


def prepare_body(
    site, jitter, rotation, axial, probes, tmat, source,
    pairs, tables, tables_t, probes_out, tmat_out, inwards_out,
):
    own = (
        lax.axis_index("xl") * PER_GROUP
        + ((lax.axis_index("z") * 2 + lax.axis_index("xh")) * 4 + lax.axis_index("y")) * OWN
    )
    sites = site[...]
    core = lax.axis_index("co")

    def own_core_first(place):
        other = jnp.concatenate([place[:, SPHERES // 2 :], place[:, : SPHERES // 2]], axis=1)
        return jnp.where(core == 0, place, other)

    place_x = own_core_first((sites & 7).astype(F32) * LATTICE_STEP + jitter[0:1, :])
    place_y = own_core_first(((sites >> 3) & 7).astype(F32) * LATTICE_STEP + jitter[1:2, :])
    place_z = own_core_first((sites >> 6).astype(F32) * LATTICE_STEP + jitter[2:3, :])
    lane = lax.broadcasted_iota(jnp.int32, (ROWS, SPHERES), 1)
    line = lax.broadcasted_iota(jnp.int32, (ROWS, SPHERES), 0)
    same = lane == line + own

    def offset(place):
        here = jnp.sum(jnp.where(same, place, 0.0), axis=1, keepdims=True)
        return here - place

    dx, dy, dz = offset(place_x), offset(place_y), offset(place_z)
    distance = jnp.sqrt(jnp.where(same, 1.0, dx * dx + dy * dy + dz * dz))
    phase = WAVENUMBER * distance
    none = same | (line >= OWN)
    radial_cos = jnp.where(none, 0.0, jnp.cos(phase) / phase)
    radial_sin = jnp.where(none, 0.0, jnp.sin(phase) / phase)
    larger = jnp.maximum(jnp.abs(dx), jnp.abs(dy))
    apart = larger > 0.0
    inverse = 1.0 / jnp.where(apart, larger, 1.0)
    ax, ay = dx * inverse, dy * inverse
    length = jnp.sqrt(jnp.where(apart, ax * ax + ay * ay, 1.0))
    cos_one = jnp.where(apart, ax / length, 1.0)
    sin_one = jnp.where(apart, ay / length, 0.0)

    def put(block, factor):
        value = jnp.concatenate([radial_cos * factor, radial_sin * factor], axis=0)
        pairs[block * BLOCK : (block + 1) * BLOCK, :] = value.astype(BF)

    pairs[0:BLOCK, :] = jnp.concatenate([radial_cos, radial_sin], axis=0).astype(BF)
    cos_k, sin_k = cos_one, sin_one
    for k in range(1, TOP + 1):
        put(k, cos_k)
        put(TOP + k, sin_k)
        if k < TOP:
            cos_k, sin_k = (
                cos_k * cos_one - sin_k * sin_one,
                sin_k * cos_one + cos_k * sin_one,
            )

    inwards = onehot_in(source[...])
    inwards_out[...] = inwards
    outwards = inwards.astype(F32).T.astype(BF)
    turned = dot(outwards, rotation[...]).astype(BF)
    for radial in range(2):
        mixed_high, mixed_low = split(0.5 * dot(turned, axial[radial]))
        tables[radial] = (dot_t(mixed_high, turned) + dot_t(mixed_low, turned)).astype(BF)
        tables_t[radial] = (dot_t(turned, mixed_high) + dot_t(turned, mixed_low)).astype(BF)
    probes_out[...] = dot(outwards, probes[...]).astype(BF)
    tmat_rows = jnp.concatenate([tmat[...], jnp.zeros((ROWS - 2, HALF), F32)], axis=0)
    tmat_out[...] = exact_dot(tmat_rows, inwards[:HALF, :WIDE])


def load_rows(near, peer, rows):
    for which, lines in enumerate((near, peer)):
        at = pl.ds(which * SPHERES // 2, SPHERES // 2)
        for part in range(4):
            value = lines[pl.ds(part, SPHERES // 2, stride=4), :]
            rows[at, part * LANES : (part + 1) * LANES] = value.astype(BF)


def group_sums(near, peer):
    def total(lines, place):
        parts = []
        for part in range(4):
            value = lines[pl.ds(place * PER_GROUP * 4 + part, PER_GROUP, stride=4), :]
            parts.append(jnp.sum(value, axis=0, keepdims=True))
        return jnp.concatenate(parts, axis=1)

    core = lax.axis_index("co")
    groups = []
    for place in range(2):
        mine, other = total(near, place), total(peer, place)
        groups.append(jnp.where(core == 0, mine, other))
        groups.append(jnp.where(core == 0, other, mine))
    return jnp.concatenate(groups, axis=0)


def mix(sums, shifted, tables):
    for k in range(1, TOP + 1):
        at_cos, at_sin = pl.ds(k * BLOCK, BLOCK), pl.ds((TOP + k) * BLOCK, BLOCK)
        cos_re, cos_im = sums[at_cos, :WIDE], sums[at_cos, WIDE:]
        sin_re, sin_im = sums[at_sin, :WIDE], sums[at_sin, WIDE:]
        sums[at_cos, :WIDE] = cos_re - sin_im
        sums[at_cos, WIDE:] = cos_im + sin_re
        sums[at_sin, :WIDE] = cos_re + sin_im
        sums[at_sin, WIDE:] = cos_im - sin_re

    def block_of(k):
        return (k if k >= 0 else TOP - k) * BLOCK

    for half in range(2):
        lane = lax.broadcasted_iota(jnp.int32, (BLOCK, LANES), 1)

        def pick(out_order, start):
            columns = slice(start + half * LANES, start + (half + 1) * LANES)
            entries = []
            for order, _, end in SPANS[half]:
                row = block_of(order - out_order)
                entries.append((sums[row : row + BLOCK, columns], end))
            return by_lane(lane, entries)

        for out_order in range(ORDER + 1):
            minus_re, minus_im = pick(out_order, 0), pick(out_order, WIDE)
            if out_order:
                plus_re, plus_im = pick(-out_order, 0), pick(-out_order, WIDE)
            else:
                plus_re, plus_im = minus_re, minus_im
            cos_part = (minus_re + plus_re, minus_im + plus_im)
            sin_part = (plus_im - minus_im, minus_re - plus_re)
            for which, start in ((0, 0), (1, WIDE)):
                columns = slice(start + half * LANES, start + (half + 1) * LANES)
                for radial in range(2):
                    lines = slice(radial * ROWS, (radial + 1) * ROWS)
                    value = jnp.concatenate([cos_part[which][lines], sin_part[which][lines]], axis=0)
                    shifted[radial, out_order * BLOCK : (out_order + 1) * BLOCK, columns] = value.astype(BF)

    back = dot(shifted[0], tables[0]) + dot(shifted[1], tables[1])
    parts_re, parts_im = [], []
    lane = lax.broadcasted_iota(jnp.int32, (ROWS, LANES), 1)
    for half in range(2):
        real = slice(half * LANES, (half + 1) * LANES)
        imag = slice(WIDE + half * LANES, WIDE + (half + 1) * LANES)
        entries_re, entries_im = [], []
        for order, _, end in SPANS[half]:
            m = abs(order)
            cos_lines = slice(m * BLOCK, m * BLOCK + ROWS)
            sin_lines = slice(m * BLOCK + ROWS, (m + 1) * BLOCK)
            value_re, value_im = back[cos_lines, real], back[cos_lines, imag]
            if order > 0:
                value_re, value_im = value_re + back[sin_lines, imag], value_im - back[sin_lines, real]
            if order < 0:
                value_re, value_im = value_re - back[sin_lines, imag], value_im + back[sin_lines, real]
            entries_re.append((value_re, end))
            entries_im.append((value_im, end))
        parts_re.append(by_lane(lane, entries_re))
        parts_im.append(by_lane(lane, entries_im))
    return jnp.concatenate(parts_re + parts_im, axis=1)


def scatter(field, tmat, radius):
    real, imag = tmat[0:1, :], tmat[1:2, :]
    field_re, field_im = field[:, :WIDE], field[:, WIDE:]
    wide = jnp.concatenate([radius, radius], axis=1)
    return jnp.concatenate(
        [
            wide * (imag * field_im - real * field_re),
            -wide * (imag * field_re + real * field_im),
        ],
        axis=1,
    )


def first_body(
    near, peer, pairs, tables, tmat, radius,
    chunk, rows_out, weights_out, totals_out, rows, sums, shifted, lines,
):
    load_rows(near, peer, rows)
    totals_out[...] = group_sums(near, peer)
    sums[...] = dot(pairs[...], rows[...])
    for block in range(BLOCKS):
        k = block if block <= TOP else block - TOP
        at = pl.ds(block * BLOCK, BLOCK)
        value = sums[at, LANES:WIDE]
        weights_out[at, :] = (value if k % 2 == 0 else -value).astype(BF)
    field = mix(sums, shifted, tables)
    image = scatter(field, tmat, radius[...])
    rows_out[...] = image
    write_chunks(image, chunk, lines)


def gradient_body(near, peer, totals_first, probes, probe_group, keep, send):
    totals = jnp.concatenate([totals_first[...], group_sums(near, peer)], axis=0)
    lane = lax.broadcasted_iota(jnp.int32, (2 * GROUPS, FULL), 1)
    totals = jnp.where((lane & (WIDE - 1)) < HALF, totals, 0.0)
    total_high, total_low = split(totals)
    values = dot(total_high, probes[...]) + dot(total_low, probes[...])
    line = lax.broadcasted_iota(jnp.int32, (2 * GROUPS, PROBES_OWN), 0)
    values = jnp.where((line & (GROUPS - 1)) == probe_group[...], values, 0.0)
    value_high, value_low = split(values)
    gradient = dot_t(value_high, probes[...]) + dot_t(value_low, probes[...])
    core = lax.axis_index("co")
    first, second = gradient[:GROUPS], gradient[GROUPS:]
    keep[...] = jnp.where(core == 0, first, second)
    send[...] = jnp.where(core == 0, second, first)


def second_body(
    near, peer, pairs, tables, tmat, radius, base, image,
    scalars, rows, sums, shifted,
):
    load_rows(near, peer, rows)
    sums[...] = dot(pairs[...], rows[...])
    field = mix(sums, shifted, tables)
    last = scatter(field, tmat, radius[...])
    zero, one = base[...], image[...]
    line = lax.broadcasted_iota(jnp.int32, (GROUPS, FULL), 0)
    lane = lax.broadcasted_iota(jnp.int32, (GROUPS, FULL), 1)
    out = jnp.zeros((GROUPS, FULL), F32)
    pairs_of = ((zero, zero), (zero, one), (one, one), (zero, last), (one, last), (last, last))
    for index, (a, b) in enumerate(pairs_of):
        out = jnp.where((line == 0) & (lane == PAD + index), jnp.sum(a * b), out)
    scalars[...] = out


def finish_body(
    near, peer, weights, tables_t, tmat, inwards, incident, image,
    solution_out, sensitivity_out, arnoldi_out, places, sums, shifted,
):
    mine, other = jnp.sum(near[...], axis=0), jnp.sum(peer[...], axis=0)
    core = lax.axis_index("co")
    first, second = jnp.where(core == 0, mine, other), jnp.where(core == 0, other, mine)
    scal = (first + second)[0:1, :]
    g00, s01, s11, s02, s12, s22 = [scal[:, PAD + i : PAD + i + 1] for i in range(6)]
    g01, g11, g02, g12, g22 = s01 / g00, s11 / g00, s02 / g00, s12 / g00, s22 / g00
    diag_first = 1.0 + g01
    below_sq = g11 - g01 * g01
    below_first = jnp.sqrt(below_sq)
    upper_second = (g02 - g01 * g01) / below_first
    shift_second = (g12 - g01 * g11 - g01 * g02 + g01 * g01 * g01) / below_sq
    diag_second = 1.0 + shift_second
    norm_sq = (g22 - 2.0 * g01 * g12 + g01 * g01 * g11) / below_sq
    rest_second = norm_sq - upper_second * upper_second - shift_second * shift_second
    gram_first = diag_first * diag_first + below_sq
    gram_cross = diag_first * upper_second + below_first * diag_second
    gram_second = upper_second * upper_second + diag_second * diag_second + rest_second
    determinant = gram_first * gram_second - gram_cross * gram_cross
    step_first = (diag_first * gram_second - upper_second * gram_cross) / determinant
    step_second = (gram_first * upper_second - gram_cross * diag_first) / determinant
    for_image = step_second / below_first
    for_base = step_first - for_image * g01
    arnoldi_out[0] = diag_first[0, 0]
    arnoldi_out[1] = below_first[0, 0]
    arnoldi_out[2] = diag_second[0, 0]
    arnoldi_out[3] = rest_second[0, 0]

    factor = COEFF * GROUPS / PROBES / SCALE / float(np.sqrt(np.float32(PER_GROUP)))
    gradient = (for_base * first + for_image * second) * factor
    real, imag = tmat[0:1, :], tmat[1:2, :]
    grad_re, grad_im = gradient[:, :WIDE], gradient[:, WIDE:]
    places[...] = jnp.zeros((LANES, FULL), F32)
    at = pl.ds(PAD - LANES, GROUPS)
    places[at, :WIDE] = real * grad_re + imag * grad_im
    places[at, WIDE:] = real * grad_im - imag * grad_re
    sums[...] = dot(weights[...], places[...].astype(BF))
    field = mix(sums, shifted, tables_t)
    group = own_group()
    own = jnp.zeros((1, FULL), F32)
    for g in range(GROUPS):
        own = jnp.where(group == g, gradient[g : g + 1, :], own)
    lane = lax.broadcasted_iota(jnp.int32, (1, FULL), 1)
    own = jnp.where((lane & (WIDE - 1)) < HALF, own, 0.0)
    both = jnp.concatenate([image[...], own - field], axis=0)
    result = exact_dot(both, inwards[...], dot_t)
    image_rows = result[:OWN]
    solution_out[...] = for_base * incident[...] + (for_image / SCALE) * image_rows
    sensitivity_out[...] = result[ROWS : ROWS + OWN]


def call(body, outs, scratch=(), operands=(), spaces=None, smem_outs=(), cost=None):
    spaces = spaces or {}
    return pl.pallas_call(
        body,
        out_shape=[jax.ShapeDtypeStruct(shape, kind) for shape, kind in outs],
        in_specs=[pl.BlockSpec(memory_space=spaces.get(i, pltpu.VMEM)) for i in range(len(operands))],
        out_specs=[
            pl.BlockSpec(memory_space=pltpu.SMEM if i in smem_outs else pltpu.VMEM) for i in range(len(outs))
        ],
        scratch_shapes=list(scratch),
        compiler_params=pltpu.CompilerParams(vmem_limit_bytes=16 * 1024 * 1024),
        cost_estimate=cost,
    )(*operands)


def swap_cores(array):
    return lax.ppermute(array, "co", [(0, 1), (1, 0)])


def exchange(chunk):
    near = lax.all_to_all(chunk, FAR_AXES, 0, 0)
    peer = swap_cores(near)
    return near.reshape(FAR * CHUNK, LANES), peer.reshape(FAR * CHUNK, LANES)


def on_device(
    incident,
    sphere_site,
    jitter,
    rotation_table,
    axial_tables,
    tmatrix,
    radius_factor,
    probe_field,
    probe_group,
):
    source = jnp.asarray(_SOURCE)
    line_scratch = pltpu.VMEM((4 * ROWS, LANES), F32)
    chunk, base, radius = call(
        send_body,
        [((FAR, CHUNK, LANES), F32), ((ROWS, FULL), F32), ((ROWS, LANES), F32)],
        [
            line_scratch,
            pltpu.VMEM((ROWS, COEFF), F32),
            pltpu.VMEM((1, FULL), jnp.int32),
            pltpu.SMEM((OWN,), F32),
            pltpu.SemaphoreType.DMA((3,)),
        ],
        (incident, source, radius_factor),
        {0: pl.ANY, 1: pl.ANY, 2: pl.ANY},
    )
    near, peer = exchange(chunk)

    def by_core(array):
        lead = array.shape[:-1]
        return jnp.swapaxes(array.reshape(lead + (2, 2, PER_GROUP)), -3, -2).reshape(lead + (SPHERES,))

    pairs, tables, tables_t, probes, tmat, inwards = call(
        prepare_body,
        [
            ((BLOCKS * BLOCK, SPHERES), BF),
            ((2, FULL, FULL), BF),
            ((2, FULL, FULL), BF),
            ((FULL, PROBES_OWN), BF),
            ((ROWS, WIDE), F32),
            ((COEFF, FULL), BF),
        ],
        operands=(
            by_core(sphere_site[None, :]),
            by_core(jitter),
            rotation_table,
            axial_tables,
            probe_field.T,
            tmatrix,
            source,
        ),
        cost=pl.CostEstimate(flops=6_000_000_000, bytes_accessed=8_000_000, transcendentals=20_000),
    )

    row_scratch = pltpu.VMEM((SPHERES, FULL), BF)
    sum_scratch = pltpu.VMEM((BLOCKS * BLOCK, FULL), F32)
    shift_scratch = pltpu.VMEM((2, (ORDER + 1) * BLOCK, FULL), BF)

    chunk, image, weights, totals_first = call(
        first_body,
        [
            ((FAR, CHUNK, LANES), F32),
            ((ROWS, FULL), F32),
            ((BLOCKS * BLOCK, LANES), BF),
            ((GROUPS, FULL), F32),
        ],
        [row_scratch, sum_scratch, shift_scratch, line_scratch],
        (near, peer, pairs, tables, tmat, radius),
    )
    near, peer = exchange(chunk)

    keep, send = call(
        gradient_body,
        [((GROUPS, FULL), F32), ((GROUPS, FULL), F32)],
        operands=(near, peer, totals_first, probes, probe_group.reshape(1, PROBES_OWN)),
    )
    received = swap_cores(send)
    (scalars,) = call(
        second_body,
        [((GROUPS, FULL), F32)],
        [row_scratch, sum_scratch, shift_scratch],
        (near, peer, pairs, tables, tmat, radius, base, image),
        cost=pl.CostEstimate(flops=1_000_000_000, bytes_accessed=8_000_000, transcendentals=0),
    )
    lane = lax.broadcasted_iota(jnp.int32, (GROUPS, FULL), 1)
    share = jnp.where((lane & (WIDE - 1)) < HALF, keep + received, scalars)
    spread = jnp.broadcast_to(share[None], (FAR, GROUPS, FULL))
    near = lax.all_to_all(spread, FAR_AXES, 0, 0)
    peer = swap_cores(near)
    solution_rows, sensitivity_rows, arnoldi = call(
        finish_body,
        [((OWN, COEFF), F32), ((OWN, COEFF), F32), ((4,), F32)],
        [pltpu.VMEM((LANES, FULL), F32), sum_scratch, shift_scratch],
        (near, peer, weights, tables_t, tmat, inwards, incident, image),
        smem_outs=(2,),
    )
    return solution_rows, sensitivity_rows, arnoldi


def solution(mesh):
    fine = Mesh(mesh.devices.reshape(2, 2, 4, 2, 4), ALL_AXES)
    split_rows = P(ALL_AXES)
    return jax.shard_map(
        on_device,
        mesh=fine,
        in_specs=(
            P(ALL_AXES, None),
            P(),
            P(),
            P(),
            P(),
            P(),
            split_rows,
            P(ALL_AXES, None),
            split_rows,
        ),
        out_specs=(P(ALL_AXES, None), P(ALL_AXES, None), P()),
        check_vma=False,
    )
```

```python
import jax
import jax.numpy as jnp
import numpy as np
from jax import lax
from jax.experimental import pallas as pl
from jax.experimental.pallas import tpu as pltpu
from jax.sharding import Mesh
from jax.sharding import PartitionSpec as P

ORDER = 10
WAVENUMBER = 1.3
LATTICE_STEP = 2.5

SPHERES = 768
COEFF = 480
HALF = 240
GROUPS = 4
PER_GROUP = SPHERES // GROUPS
PROBES = 32768
OWN = 6
PROBES_OWN = 256
LANES = 128
WIDE = 256
FULL = 2 * WIDE
ROWS = 8
BLOCK = 2 * ROWS
BLOCKS = 4 * ORDER + 1
TOP = 2 * ORDER
CHUNK = OWN * FULL // LANES
FAR = 64
SCALE = 2.0**-14
PAD = HALF
BF = jnp.bfloat16
F32 = jnp.float32

FAR_AXES = ("xl", "z", "xh", "y")
ALL_AXES = ("xl", "co", "z", "xh", "y")


def order_table(degree_max):
    entries = np.arange(degree_max * (degree_max + 2))
    degree = np.floor(np.sqrt(entries + 1.0) + 1e-09)
    orders = entries + 1 - degree * degree - degree
    return np.concatenate([orders, orders]).astype(np.int32)


_ORDERS = order_table(ORDER)
_SORTED = np.lexsort((_ORDERS, np.abs(_ORDERS)))
_SOURCE = np.full((1, FULL), -1, np.int32)
_SOURCE[0, :HALF] = _SORTED
_SOURCE[0, WIDE : WIDE + HALF] = _SORTED + HALF


def spans(half):
    part = _ORDERS[_SORTED][half * LANES : (half + 1) * LANES]
    found = []
    for order in dict.fromkeys(int(m) for m in part):
        lanes = np.flatnonzero(part == order)
        found.append((order, int(lanes[0]), int(lanes[-1]) + 1))
    return found


SPANS = (spans(0), spans(1))


def by_lane(lane, entries):
    chosen = entries[-1][0]
    for value, end in reversed(entries[:-1]):
        chosen = jnp.where(lane < end, value, chosen)
    return chosen


def dot(a, b):
    return jnp.dot(a, b, preferred_element_type=F32)


def dot_t(a, b):
    return lax.dot_general(a, b, (((1,), (1,)), ((), ())), preferred_element_type=F32)


def fine_dot(x, y, dot=dot, parts=3):
    rows = x.shape[0]
    padded = -(-rows // 16) * 16
    if padded > rows:
        x = jnp.concatenate([x, jnp.zeros((padded - rows, x.shape[1]), F32)], axis=0)
    terms = []
    for _ in range(parts):
        terms.append(x.astype(BF))
        x = x - terms[-1].astype(F32)
    product = dot(jnp.concatenate(terms, axis=0), y)
    total = product[:rows]
    for part in range(1, parts):
        total = total + product[part * padded : part * padded + rows]
    return total


def onehot_in(source):
    rows = lax.broadcasted_iota(jnp.int32, (COEFF, FULL), 0)
    return jnp.where(rows == source, 1.0, 0.0).astype(BF)


def own_group():
    return lax.axis_index("xl") * 2 + lax.axis_index("co")


def send_body(incident, chunk, lines):
    value = jnp.concatenate([incident[...], jnp.zeros((ROWS - OWN, COEFF), F32)], axis=0) * SCALE
    value = jnp.concatenate([value, jnp.zeros((ROWS, FULL - COEFF), F32)], axis=1)
    write_chunks(value, chunk, lines)


def write_chunks(rows, chunk, lines):
    for part in range(4):
        lines[pl.ds(part, ROWS, stride=4), :] = rows[:, part * LANES : (part + 1) * LANES]
    once = lines[:CHUNK, :]
    for far in range(FAR):
        chunk[far] = once


def prepare_body(
    site, jitter, rotation, axial, probe_group, tmat, source, incident, radius,
    pairs, tables, seen_out, tmat_out, inwards_out, base_out, radius_out,
):
    own = (
        lax.axis_index("xl") * PER_GROUP
        + ((lax.axis_index("z") * 2 + lax.axis_index("xh")) * 4 + lax.axis_index("y")) * OWN
    )
    sites = site[...]
    core = lax.axis_index("co")

    def own_core_first(place):
        other = jnp.concatenate([place[:, SPHERES // 2 :], place[:, : SPHERES // 2]], axis=1)
        return jnp.where(core == 0, place, other)

    place_x = own_core_first((sites & 7).astype(F32) * LATTICE_STEP + jitter[0:1, :])
    place_y = own_core_first(((sites >> 3) & 7).astype(F32) * LATTICE_STEP + jitter[1:2, :])
    place_z = own_core_first((sites >> 6).astype(F32) * LATTICE_STEP + jitter[2:3, :])
    lane = lax.broadcasted_iota(jnp.int32, (ROWS, SPHERES), 1)
    line = lax.broadcasted_iota(jnp.int32, (ROWS, SPHERES), 0)
    same = lane == line + own

    def offset(place):
        here = jnp.sum(jnp.where(same, place, 0.0), axis=1, keepdims=True)
        return here - place

    dx, dy, dz = offset(place_x), offset(place_y), offset(place_z)
    distance = jnp.sqrt(jnp.where(same, 1.0, dx * dx + dy * dy + dz * dz))
    phase = WAVENUMBER * distance
    none = same | (line >= OWN)
    radial_cos = jnp.where(none, 0.0, jnp.cos(phase) / phase)
    radial_sin = jnp.where(none, 0.0, jnp.sin(phase) / phase)
    larger = jnp.maximum(jnp.abs(dx), jnp.abs(dy))
    apart = larger > 0.0
    inverse = 1.0 / jnp.where(apart, larger, 1.0)
    ax, ay = dx * inverse, dy * inverse
    length = jnp.sqrt(jnp.where(apart, ax * ax + ay * ay, 1.0))
    cos_one = jnp.where(apart, ax / length, 1.0)
    sin_one = jnp.where(apart, ay / length, 0.0)

    def put(block, factor):
        value = jnp.concatenate([radial_cos * factor, radial_sin * factor], axis=0)
        pairs[block * BLOCK : (block + 1) * BLOCK, :] = value.astype(BF)

    pairs[0:BLOCK, :] = jnp.concatenate([radial_cos, radial_sin], axis=0).astype(BF)
    cos_k, sin_k = cos_one, sin_one
    for k in range(1, TOP + 1):
        put(k, cos_k)
        put(TOP + k, sin_k)
        if k < TOP:
            cos_k, sin_k = (
                cos_k * cos_one - sin_k * sin_one,
                sin_k * cos_one + cos_k * sin_one,
            )

    inwards = onehot_in(source[...])
    inwards_out[...] = inwards
    outwards = inwards.astype(F32).T.astype(BF)
    turned = dot(outwards, rotation[...]).astype(BF)
    for radial in range(2):
        tables[radial] = fine_dot(0.5 * dot(turned, axial[radial]), turned, dot_t, 2).astype(BF)
    line = lax.broadcasted_iota(jnp.int32, (GROUPS, PROBES_OWN), 0)
    seen_out[...] = jnp.where(line == probe_group[...], 1.0, 0.0)
    tmat_rows = jnp.concatenate([tmat[...], jnp.zeros((ROWS - 2, HALF), F32)], axis=0)
    tmat_out[...] = fine_dot(tmat_rows, inwards[:HALF, :WIDE])
    value = jnp.concatenate([incident[...], jnp.zeros((ROWS - OWN, COEFF), F32)], axis=0) * SCALE
    base_out[...] = fine_dot(value, inwards)
    line = lax.broadcasted_iota(jnp.int32, (ROWS, LANES), 0)
    column = jnp.zeros((ROWS, LANES), F32)
    for r in range(OWN):
        column = jnp.where(line == r, radius[r], column)
    radius_out[...] = column


def load_rows(lines):
    parts = [lines[pl.ds(part, SPHERES // 2, stride=4), :].astype(BF) for part in range(4)]
    return jnp.concatenate(parts, axis=1)


def half_sums(lines):
    groups = []
    for place in range(2):
        parts = []
        for part in range(4):
            value = lines[pl.ds(place * PER_GROUP * 4 + part, PER_GROUP, stride=4), :]
            parts.append(jnp.sum(value, axis=0, keepdims=True))
        groups.append(jnp.concatenate(parts, axis=1))
    return jnp.concatenate(groups, axis=0)


def all_groups(mine, other):
    core = lax.axis_index("co")
    first, second = jnp.where(core == 0, mine, other), jnp.where(core == 0, other, mine)
    return jnp.concatenate([first[0:1], second[0:1], first[1:2], second[1:2]], axis=0)


def order_body(near_in, pairs, near_out):
    del near_in, pairs, near_out


def mix(sums, shifted, tables, dot=dot):
    for k in range(1, TOP + 1):
        at_cos, at_sin = pl.ds(k * BLOCK, BLOCK), pl.ds((TOP + k) * BLOCK, BLOCK)
        cos_re, cos_im = sums[at_cos, :WIDE], sums[at_cos, WIDE:]
        sin_re, sin_im = sums[at_sin, :WIDE], sums[at_sin, WIDE:]
        sums[at_cos, :WIDE] = cos_re - sin_im
        sums[at_cos, WIDE:] = cos_im + sin_re
        sums[at_sin, :WIDE] = cos_re + sin_im
        sums[at_sin, WIDE:] = cos_im - sin_re

    def block_of(k):
        return (k if k >= 0 else TOP - k) * BLOCK

    for half in range(2):
        lane = lax.broadcasted_iota(jnp.int32, (BLOCK, LANES), 1)

        def pick(out_order, start):
            columns = slice(start + half * LANES, start + (half + 1) * LANES)
            entries = []
            for order, _, end in SPANS[half]:
                row = block_of(order - out_order)
                entries.append((sums[row : row + BLOCK, columns], end))
            return by_lane(lane, entries)

        for out_order in range(ORDER + 1):
            minus_re, minus_im = pick(out_order, 0), pick(out_order, WIDE)
            if out_order:
                plus_re, plus_im = pick(-out_order, 0), pick(-out_order, WIDE)
            else:
                plus_re, plus_im = minus_re, minus_im
            cos_part = (minus_re + plus_re, minus_im + plus_im)
            sin_part = (plus_im - minus_im, minus_re - plus_re)
            for which, start in ((0, 0), (1, WIDE)):
                columns = slice(start + half * LANES, start + (half + 1) * LANES)
                for radial in range(2):
                    lines = slice(radial * ROWS, (radial + 1) * ROWS)
                    value = jnp.concatenate([cos_part[which][lines], sin_part[which][lines]], axis=0)
                    shifted[radial, out_order * BLOCK : (out_order + 1) * BLOCK, columns] = value.astype(BF)

    back = dot(shifted[0], tables[0]) + dot(shifted[1], tables[1])
    parts_re, parts_im = [], []
    lane = lax.broadcasted_iota(jnp.int32, (ROWS, LANES), 1)
    for half in range(2):
        real = slice(half * LANES, (half + 1) * LANES)
        imag = slice(WIDE + half * LANES, WIDE + (half + 1) * LANES)
        entries_re, entries_im = [], []
        for order, _, end in SPANS[half]:
            m = abs(order)
            cos_lines = slice(m * BLOCK, m * BLOCK + ROWS)
            sin_lines = slice(m * BLOCK + ROWS, (m + 1) * BLOCK)
            value_re, value_im = back[cos_lines, real], back[cos_lines, imag]
            if order > 0:
                value_re, value_im = value_re + back[sin_lines, imag], value_im - back[sin_lines, real]
            if order < 0:
                value_re, value_im = value_re - back[sin_lines, imag], value_im + back[sin_lines, real]
            entries_re.append((value_re, end))
            entries_im.append((value_im, end))
        parts_re.append(by_lane(lane, entries_re))
        parts_im.append(by_lane(lane, entries_im))
    return jnp.concatenate(parts_re + parts_im, axis=1)


def scatter(field, tmat, radius):
    real, imag = tmat[0:1, :], tmat[1:2, :]
    field_re, field_im = field[:, :WIDE], field[:, WIDE:]
    wide = jnp.concatenate([radius, radius], axis=1)
    return jnp.concatenate(
        [
            wide * (imag * field_im - real * field_re),
            -wide * (imag * field_re + real * field_im),
        ],
        axis=1,
    )


def first_body(
    near, peer, pairs, inwards, tables, tmat, radius,
    chunk, rows_out, totals_out, sums, shifted, lines,
):
    totals_out[...] = all_groups(half_sums(near), half_sums(peer))
    rows = jnp.concatenate([load_rows(near), load_rows(peer)], axis=0)[:, :COEFF]
    sums[...] = dot(pairs[...], dot(rows, inwards[...]).astype(BF))
    field = mix(sums, shifted, tables)
    image = scatter(field, tmat, radius[...])
    rows_out[...] = image
    lane = lax.broadcasted_iota(jnp.int32, (ROWS, FULL), 1)
    marked = jnp.where(lane == PAD + own_group(), jnp.concatenate([radius[...]] * 4, axis=1), image)
    write_chunks(marked, chunk, lines)


def gradient_of(totals, probes, seen):
    lane = lax.broadcasted_iota(jnp.int32, totals.shape, 1)
    totals = jnp.where((lane & (WIDE - 1)) < HALF, totals, 0.0)
    values = fine_dot(totals, probes[...], parts=2) * seen[...]
    return fine_dot(values, probes[...], dot_t, 2)


def first_gradient_body(totals, inwards, probes, seen, gradient_out, probes_out):
    outwards = inwards[...].astype(F32).T.astype(BF)
    probes_out[...] = dot(outwards, probes[...]).astype(BF)
    gradient_out[...] = gradient_of(fine_dot(totals[:, :COEFF], inwards[...]), probes_out, seen)


def second_gradient_body(near, peer, first, probes, seen, keep, send):
    second = gradient_of(all_groups(half_sums(near), half_sums(peer)), probes, seen)
    core = lax.axis_index("co")
    keep[...] = jnp.where(core == 0, first[...], second)
    send[...] = jnp.where(core == 0, second, first[...])


def second_body(
    near, peer, pairs, tables, tmat, radius, base, image,
    scalars, weights_out, sums, shifted,
):
    sums[...] = dot(pairs[...], jnp.concatenate([load_rows(near), load_rows(peer)], axis=0))
    for block in range(BLOCKS):
        k = block if block <= TOP else block - TOP
        at = pl.ds(block * BLOCK, BLOCK)
        value = sums[at, LANES:WIDE]
        weights_out[at, :] = (value if k % 2 == 0 else -value).astype(BF)
    field = mix(sums, shifted, tables)
    last = scatter(field, tmat, radius[...])
    zero, one = base[...], image[...]
    line = lax.broadcasted_iota(jnp.int32, (GROUPS, FULL), 0)
    lane = lax.broadcasted_iota(jnp.int32, (GROUPS, FULL), 1)
    out = jnp.zeros((GROUPS, FULL), F32)
    pairs_of = ((zero, zero), (zero, one), (one, one), (zero, last), (one, last), (last, last))
    for index, (a, b) in enumerate(pairs_of):
        out = jnp.where((line == 0) & (lane == PAD + index), jnp.sum(a * b), out)
    scalars[...] = out


def finish_body(
    near, peer, weights, tables, tmat, inwards, incident, image,
    solution_out, sensitivity_out, arnoldi_out, places, sums, shifted,
):
    mine, other = jnp.sum(near[...], axis=0), jnp.sum(peer[...], axis=0)
    core = lax.axis_index("co")
    first, second = jnp.where(core == 0, mine, other), jnp.where(core == 0, other, mine)
    scal = (first + second)[0:1, :]
    g00, s01, s11, s02, s12, s22 = [scal[:, PAD + i : PAD + i + 1] for i in range(6)]
    g01, g11, g02, g12, g22 = s01 / g00, s11 / g00, s02 / g00, s12 / g00, s22 / g00
    diag_first = 1.0 + g01
    below_sq = g11 - g01 * g01
    below_first = jnp.sqrt(below_sq)
    upper_second = (g02 - g01 * g01) / below_first
    shift_second = (g12 - g01 * g11 - g01 * g02 + g01 * g01 * g01) / below_sq
    diag_second = 1.0 + shift_second
    norm_sq = (g22 - 2.0 * g01 * g12 + g01 * g01 * g11) / below_sq
    rest_second = norm_sq - upper_second * upper_second - shift_second * shift_second
    gram_first = diag_first * diag_first + below_sq
    gram_cross = diag_first * upper_second + below_first * diag_second
    gram_second = upper_second * upper_second + diag_second * diag_second + rest_second
    determinant = gram_first * gram_second - gram_cross * gram_cross
    step_first = (diag_first * gram_second - upper_second * gram_cross) / determinant
    step_second = (gram_first * upper_second - gram_cross * diag_first) / determinant
    for_image = step_second / below_first
    for_base = step_first - for_image * g01
    arnoldi_out[0] = diag_first[0, 0]
    arnoldi_out[1] = below_first[0, 0]
    arnoldi_out[2] = diag_second[0, 0]
    arnoldi_out[3] = rest_second[0, 0]

    factor = COEFF * GROUPS / PROBES / SCALE / float(np.sqrt(np.float32(PER_GROUP)))
    gradient = (for_base * first + for_image * second) * factor
    real, imag = tmat[0:1, :], tmat[1:2, :]
    grad_re, grad_im = gradient[:, :WIDE], gradient[:, WIDE:]
    places[...] = jnp.zeros((LANES, FULL), F32)
    at = pl.ds(PAD - LANES, GROUPS)
    places[at, :WIDE] = real * grad_re + imag * grad_im
    places[at, WIDE:] = real * grad_im - imag * grad_re
    sums[...] = dot(weights[...], places[...].astype(BF))
    field = mix(sums, shifted, tables, dot_t)
    group = own_group()
    own = jnp.zeros((1, FULL), F32)
    for g in range(GROUPS):
        own = jnp.where(group == g, gradient[g : g + 1, :], own)
    lane = lax.broadcasted_iota(jnp.int32, (1, FULL), 1)
    own = jnp.where((lane & (WIDE - 1)) < HALF, own, 0.0)
    both = jnp.concatenate([image[...], own - field], axis=0)
    result = fine_dot(both, inwards[...], dot_t)
    image_rows = result[:OWN]
    solution_out[...] = for_base * incident[...] + (for_image / SCALE) * image_rows
    sensitivity_out[...] = result[ROWS : ROWS + OWN]


def call(body, outs, scratch=(), operands=(), spaces=None, out_spaces=None, cost=None, aliases=None):
    spaces, out_spaces = spaces or {}, out_spaces or {}
    return pl.pallas_call(
        body,
        out_shape=[jax.ShapeDtypeStruct(shape, kind) for shape, kind in outs],
        in_specs=[pl.BlockSpec(memory_space=spaces.get(i, pltpu.VMEM)) for i in range(len(operands))],
        out_specs=[pl.BlockSpec(memory_space=out_spaces.get(i, pltpu.VMEM)) for i in range(len(outs))],
        scratch_shapes=list(scratch),
        compiler_params=pltpu.CompilerParams(vmem_limit_bytes=16 * 1024 * 1024),
        cost_estimate=cost,
        input_output_aliases=aliases or {},
    )(*operands)


def swap_cores(array):
    return lax.ppermute(array, "co", [(0, 1), (1, 0)])


def as_lines(chunk):
    return chunk.reshape(FAR * CHUNK, LANES)


def on_device(
    incident,
    sphere_site,
    jitter,
    rotation_table,
    axial_tables,
    tmatrix,
    radius_factor,
    probe_field,
    probe_group,
):
    line_scratch = pltpu.VMEM((4 * ROWS, LANES), F32)
    sum_scratch = pltpu.VMEM((BLOCKS * BLOCK, FULL), F32)
    shift_scratch = pltpu.VMEM((2, (ORDER + 1) * BLOCK, FULL), BF)
    rows_shape = ((ROWS, FULL), F32)
    chunk_shape = ((FAR, CHUNK, LANES), F32)
    gradient_shape = ((GROUPS, FULL), F32)
    half_cost = pl.CostEstimate(flops=8_000_000_000, bytes_accessed=4_000_000, transcendentals=0)

    (chunk,) = call(send_body, [chunk_shape], [line_scratch], (incident,))

    def by_core(array):
        lead = array.shape[:-1]
        return jnp.swapaxes(array.reshape(lead + (2, 2, PER_GROUP)), -3, -2).reshape(lead + (SPHERES,))

    pairs, tables, seen, tmat, inwards, base, radius = call(
        prepare_body,
        [
            ((BLOCKS * BLOCK, SPHERES), BF),
            ((2, FULL, FULL), BF),
            ((GROUPS, PROBES_OWN), F32),
            ((ROWS, WIDE), F32),
            ((COEFF, FULL), BF),
            rows_shape,
            ((ROWS, LANES), F32),
        ],
        operands=(
            by_core(sphere_site[None, :]),
            by_core(jitter),
            rotation_table,
            axial_tables,
            probe_group.reshape(1, PROBES_OWN),
            tmatrix,
            jnp.asarray(_SOURCE),
            incident,
            radius_factor,
        ),
        spaces={8: pltpu.SMEM},
        cost=pl.CostEstimate(flops=8_000_000_000, bytes_accessed=8_000_000, transcendentals=20_000),
    )

    near = lax.all_to_all(chunk, FAR_AXES, 0, 0)
    (near,) = call(order_body, [chunk_shape], operands=(near, pairs), spaces={1: pl.ANY}, aliases={0: 0})
    chunk, image, totals = call(
        first_body,
        [chunk_shape, rows_shape, gradient_shape],
        [sum_scratch, shift_scratch, line_scratch],
        (as_lines(near), as_lines(swap_cores(near)), pairs, inwards, tables, tmat, radius),
    )

    gradient, probes = call(
        first_gradient_body,
        [gradient_shape, ((FULL, PROBES_OWN), BF)],
        operands=(totals, inwards, probe_field.T, seen),
        cost=half_cost,
    )

    near = lax.all_to_all(chunk, FAR_AXES, 0, 0)
    near, peer = as_lines(near), as_lines(swap_cores(near))
    keep, send = call(
        second_gradient_body,
        [gradient_shape, gradient_shape],
        operands=(near, peer, gradient, probes, seen),
    )
    received = swap_cores(send)
    scalars, weights = call(
        second_body,
        [gradient_shape, ((BLOCKS * BLOCK, LANES), BF)],
        [sum_scratch, shift_scratch],
        (near, peer, pairs, tables, tmat, radius, base, image),
        cost=half_cost,
    )
    lane = lax.broadcasted_iota(jnp.int32, (GROUPS, FULL), 1)
    share = jnp.where((lane & (WIDE - 1)) < HALF, keep + received, scalars)
    spread = jnp.broadcast_to(share[None], (FAR, GROUPS, FULL))
    near = lax.all_to_all(spread, FAR_AXES, 0, 0)
    peer = swap_cores(near)
    solution_rows, sensitivity_rows, arnoldi = call(
        finish_body,
        [((OWN, COEFF), F32), ((OWN, COEFF), F32), ((4,), F32)],
        [pltpu.VMEM((LANES, FULL), F32), sum_scratch, shift_scratch],
        (near, peer, weights, tables, tmat, inwards, incident, image),
        out_spaces={2: pltpu.SMEM},
    )
    return solution_rows, sensitivity_rows, arnoldi


def solution(mesh):
    fine = Mesh(mesh.devices.reshape(2, 2, 4, 2, 4), ALL_AXES)
    split_rows = P(ALL_AXES)
    return jax.shard_map(
        on_device,
        mesh=fine,
        in_specs=(
            P(ALL_AXES, None),
            P(),
            P(),
            P(),
            P(),
            P(),
            split_rows,
            P(ALL_AXES, None),
            split_rows,
        ),
        out_specs=(P(ALL_AXES, None), P(ALL_AXES, None), P()),
        check_vma=False,
    )
```

```python
import jax
import jax.numpy as jnp
import numpy as np
from jax import lax
from jax.experimental import pallas as pl
from jax.experimental.pallas import tpu as pltpu
from jax.sharding import Mesh
from jax.sharding import PartitionSpec as P

ORDER = 10
WAVENUMBER = 1.3
LATTICE_STEP = 2.5

SPHERES = 768
COEFF = 480
HALF = 240
GROUPS = 4
PER_GROUP = SPHERES // GROUPS
PROBES = 32768
OWN = 6
PROBES_OWN = 256
LANES = 128
WIDE = 256
FULL = 2 * WIDE
ROWS = 8
BLOCK = 2 * ROWS
BLOCKS = 4 * ORDER + 1
TOP = 2 * ORDER
CHUNK = OWN * FULL // LANES
FAR = 64
SCALE = 2.0**-14
PAD = HALF
SHARE = 2 * FULL // LANES
SCALAR_LINE = 2
PIECE_LINES = (6, 7)
SLICE_LINES = (3, 7)
BF = jnp.bfloat16
F32 = jnp.float32

FAR_AXES = ("xl", "z", "xh", "y")
ALL_AXES = ("xl", "co", "z", "xh", "y")


def order_table(degree_max):
    entries = np.arange(degree_max * (degree_max + 2))
    degree = np.floor(np.sqrt(entries + 1.0) + 1e-09)
    orders = entries + 1 - degree * degree - degree
    return np.concatenate([orders, orders]).astype(np.int32)


_ORDERS = order_table(ORDER)
_SORTED = np.lexsort((_ORDERS, np.abs(_ORDERS)))
_SOURCE = np.full((1, FULL), -1, np.int32)
_SOURCE[0, :HALF] = _SORTED
_SOURCE[0, WIDE : WIDE + HALF] = _SORTED + HALF


def spans(half):
    part = _ORDERS[_SORTED][half * LANES : (half + 1) * LANES]
    found = []
    for order in dict.fromkeys(int(m) for m in part):
        lanes = np.flatnonzero(part == order)
        found.append((order, int(lanes[0]), int(lanes[-1]) + 1))
    return found


SPANS = (spans(0), spans(1))


def by_lane(lane, entries):
    chosen = entries[-1][0]
    for value, end in reversed(entries[:-1]):
        chosen = jnp.where(lane < end, value, chosen)
    return chosen


def dot(a, b):
    return jnp.dot(a, b, preferred_element_type=F32)


def dot_t(a, b):
    return lax.dot_general(a, b, (((1,), (1,)), ((), ())), preferred_element_type=F32)


def fine_dot(x, y, dot=dot, parts=3):
    rows = x.shape[0]
    padded = -(-rows // 16) * 16
    if padded > rows:
        x = jnp.concatenate([x, jnp.zeros((padded - rows, x.shape[1]), F32)], axis=0)
    terms = []
    for _ in range(parts):
        terms.append(x.astype(BF))
        x = x - terms[-1].astype(F32)
    product = dot(jnp.concatenate(terms, axis=0), y)
    total = product[:rows]
    for part in range(1, parts):
        total = total + product[part * padded : part * padded + rows]
    return total


def onehot_in(source):
    rows = lax.broadcasted_iota(jnp.int32, (COEFF, FULL), 0)
    return jnp.where(rows == source, 1.0, 0.0).astype(BF)


def own_group():
    return lax.axis_index("xl") * 2 + lax.axis_index("co")


def send_body(incident, chunk, lines):
    value = jnp.concatenate([incident[...], jnp.zeros((ROWS - OWN, COEFF), F32)], axis=0) * SCALE
    value = jnp.concatenate([value, jnp.zeros((ROWS, FULL - COEFF), F32)], axis=1)
    write_chunks(value, chunk, lines)


def write_chunks(rows, chunk, lines):
    for part in range(4):
        lines[pl.ds(part, ROWS, stride=4), :] = rows[:, part * LANES : (part + 1) * LANES]
    once = lines[:CHUNK, :]
    for far in range(FAR):
        chunk[far * CHUNK : (far + 1) * CHUNK, :] = once


def prepare_body(
    site, jitter, rotation, axial, probes, probe_group, tmat, source, incident, radius,
    pairs, tables, probes_out, seen_out, tmat_out, inwards_out, outwards_out, base_out, radius_out,
):
    own = (
        lax.axis_index("xl") * PER_GROUP
        + ((lax.axis_index("z") * 2 + lax.axis_index("xh")) * 4 + lax.axis_index("y")) * OWN
    )
    sites = site[...]
    core = lax.axis_index("co")

    def own_core_first(place):
        other = jnp.concatenate([place[:, SPHERES // 2 :], place[:, : SPHERES // 2]], axis=1)
        return jnp.where(core == 0, place, other)

    place_x = own_core_first((sites & 7).astype(F32) * LATTICE_STEP + jitter[0:1, :])
    place_y = own_core_first(((sites >> 3) & 7).astype(F32) * LATTICE_STEP + jitter[1:2, :])
    place_z = own_core_first((sites >> 6).astype(F32) * LATTICE_STEP + jitter[2:3, :])
    lane = lax.broadcasted_iota(jnp.int32, (ROWS, SPHERES), 1)
    line = lax.broadcasted_iota(jnp.int32, (ROWS, SPHERES), 0)
    same = lane == line + own

    def offset(place):
        here = jnp.sum(jnp.where(same, place, 0.0), axis=1, keepdims=True)
        return here - place

    dx, dy, dz = offset(place_x), offset(place_y), offset(place_z)
    distance = jnp.sqrt(jnp.where(same, 1.0, dx * dx + dy * dy + dz * dz))
    phase = WAVENUMBER * distance
    none = same | (line >= OWN)
    radial_cos = jnp.where(none, 0.0, jnp.cos(phase) / phase)
    radial_sin = jnp.where(none, 0.0, jnp.sin(phase) / phase)
    larger = jnp.maximum(jnp.abs(dx), jnp.abs(dy))
    apart = larger > 0.0
    inverse = 1.0 / jnp.where(apart, larger, 1.0)
    ax, ay = dx * inverse, dy * inverse
    length = jnp.sqrt(jnp.where(apart, ax * ax + ay * ay, 1.0))
    cos_one = jnp.where(apart, ax / length, 1.0)
    sin_one = jnp.where(apart, ay / length, 0.0)

    def put(block, factor):
        value = jnp.concatenate([radial_cos * factor, radial_sin * factor], axis=0)
        pairs[block * BLOCK : (block + 1) * BLOCK, :] = value.astype(BF)

    pairs[0:BLOCK, :] = jnp.concatenate([radial_cos, radial_sin], axis=0).astype(BF)
    cos_k, sin_k = cos_one, sin_one
    for k in range(1, TOP + 1):
        put(k, cos_k)
        put(TOP + k, sin_k)
        if k < TOP:
            cos_k, sin_k = (
                cos_k * cos_one - sin_k * sin_one,
                sin_k * cos_one + cos_k * sin_one,
            )

    inwards = onehot_in(source[...])
    inwards_out[...] = inwards
    outwards = inwards.astype(F32).T.astype(BF)
    outwards_out[...] = outwards
    probes_out[...] = dot(outwards, probes[...]).astype(BF)
    turned = dot(outwards, rotation[...]).astype(BF)
    for radial in range(2):
        tables[radial] = fine_dot(0.5 * dot(turned, axial[radial]), turned, dot_t, 2).astype(BF)
    line = lax.broadcasted_iota(jnp.int32, (GROUPS, PROBES_OWN), 0)
    seen_out[...] = jnp.where(line == probe_group[...], 1.0, 0.0)
    tmat_rows = jnp.concatenate([tmat[...], jnp.zeros((ROWS - 2, HALF), F32)], axis=0)
    tmat_out[...] = fine_dot(tmat_rows, inwards[:HALF, :WIDE])
    value = jnp.concatenate([incident[...], jnp.zeros((ROWS - OWN, COEFF), F32)], axis=0) * SCALE
    base_out[...] = fine_dot(value, inwards)
    line = lax.broadcasted_iota(jnp.int32, (ROWS, LANES), 0)
    column = jnp.zeros((ROWS, LANES), F32)
    for r in range(OWN):
        column = jnp.where(line == r, radius[r], column)
    radius_out[...] = column


def load_rows(lines):
    parts = [lines[pl.ds(part, SPHERES // 2, stride=4), :].astype(BF) for part in range(4)]
    return jnp.concatenate(parts, axis=1)


def half_sums(lines):
    groups = []
    for place in range(2):
        parts = []
        for part in range(4):
            value = lines[pl.ds(place * PER_GROUP * 4 + part, PER_GROUP, stride=4), :]
            parts.append(jnp.sum(value, axis=0, keepdims=True))
        groups.append(jnp.concatenate(parts, axis=1))
    return jnp.concatenate(groups, axis=0)


def all_groups(mine, other):
    core = lax.axis_index("co")
    first, second = jnp.where(core == 0, mine, other), jnp.where(core == 0, other, mine)
    return jnp.concatenate([first[0:1], second[0:1], first[1:2], second[1:2]], axis=0)


def order_body(near_in, pairs, near_out):
    del near_in, pairs, near_out


def mix(sums, shifted, tables, dot=dot):
    for k in range(1, TOP + 1):
        at_cos, at_sin = pl.ds(k * BLOCK, BLOCK), pl.ds((TOP + k) * BLOCK, BLOCK)
        cos_re, cos_im = sums[at_cos, :WIDE], sums[at_cos, WIDE:]
        sin_re, sin_im = sums[at_sin, :WIDE], sums[at_sin, WIDE:]
        sums[at_cos, :WIDE] = cos_re - sin_im
        sums[at_cos, WIDE:] = cos_im + sin_re
        sums[at_sin, :WIDE] = cos_re + sin_im
        sums[at_sin, WIDE:] = cos_im - sin_re

    def block_of(k):
        return (k if k >= 0 else TOP - k) * BLOCK

    for half in range(2):
        lane = lax.broadcasted_iota(jnp.int32, (BLOCK, LANES), 1)

        def pick(out_order, start):
            columns = slice(start + half * LANES, start + (half + 1) * LANES)
            entries = []
            for order, _, end in SPANS[half]:
                row = block_of(order - out_order)
                entries.append((sums[row : row + BLOCK, columns], end))
            return by_lane(lane, entries)

        for out_order in range(ORDER + 1):
            minus_re, minus_im = pick(out_order, 0), pick(out_order, WIDE)
            if out_order:
                plus_re, plus_im = pick(-out_order, 0), pick(-out_order, WIDE)
            else:
                plus_re, plus_im = minus_re, minus_im
            cos_part = (minus_re + plus_re, minus_im + plus_im)
            sin_part = (plus_im - minus_im, minus_re - plus_re)
            for which, start in ((0, 0), (1, WIDE)):
                columns = slice(start + half * LANES, start + (half + 1) * LANES)
                for radial in range(2):
                    lines = slice(radial * ROWS, (radial + 1) * ROWS)
                    value = jnp.concatenate([cos_part[which][lines], sin_part[which][lines]], axis=0)
                    shifted[radial, out_order * BLOCK : (out_order + 1) * BLOCK, columns] = value.astype(BF)

    back = dot(shifted[0], tables[0]) + dot(shifted[1], tables[1])
    parts_re, parts_im = [], []
    lane = lax.broadcasted_iota(jnp.int32, (ROWS, LANES), 1)
    for half in range(2):
        real = slice(half * LANES, (half + 1) * LANES)
        imag = slice(WIDE + half * LANES, WIDE + (half + 1) * LANES)
        entries_re, entries_im = [], []
        for order, _, end in SPANS[half]:
            m = abs(order)
            cos_lines = slice(m * BLOCK, m * BLOCK + ROWS)
            sin_lines = slice(m * BLOCK + ROWS, (m + 1) * BLOCK)
            value_re, value_im = back[cos_lines, real], back[cos_lines, imag]
            if order > 0:
                value_re, value_im = value_re + back[sin_lines, imag], value_im - back[sin_lines, real]
            if order < 0:
                value_re, value_im = value_re - back[sin_lines, imag], value_im + back[sin_lines, real]
            entries_re.append((value_re, end))
            entries_im.append((value_im, end))
        parts_re.append(by_lane(lane, entries_re))
        parts_im.append(by_lane(lane, entries_im))
    return jnp.concatenate(parts_re + parts_im, axis=1)


def scatter(field, tmat, radius):
    real, imag = tmat[0:1, :], tmat[1:2, :]
    field_re, field_im = field[:, :WIDE], field[:, WIDE:]
    wide = jnp.concatenate([radius, radius], axis=1)
    return jnp.concatenate(
        [
            wide * (imag * field_im - real * field_re),
            -wide * (imag * field_re + real * field_im),
        ],
        axis=1,
    )


def first_body(
    near, peer, pairs, inwards, tables, tmat, radius, plain_probes, probes, seen,
    chunk, rows_out, sums, shifted, lines,
):
    rows = jnp.concatenate([load_rows(near), load_rows(peer)], axis=0)[:, :COEFF]
    sums[...] = dot(pairs[...], dot(rows, inwards[...]).astype(BF))
    totals = all_groups(half_sums(near), half_sums(peer))[:, :COEFF]
    gradient = gradient_of(totals, plain_probes, probes, seen)
    field = mix(sums, shifted, tables)
    image = scatter(field, tmat, radius[...])
    rows_out[...] = image
    lane = lax.broadcasted_iota(jnp.int32, (ROWS, FULL), 1)
    marked = jnp.where(lane == PAD + own_group(), jnp.concatenate([radius[...]] * 4, axis=1), image)
    write_chunks(marked, chunk, lines)
    for piece in range(2):
        line = SLICE_LINES[piece]
        chunk[pl.ds(line, FAR, stride=CHUNK), :] = lines[line : line + 1, :] + slices(gradient, piece)


def piece_mask(piece):
    lane = lax.broadcasted_iota(jnp.int32, (FAR, FULL), 1)
    far = lax.broadcasted_iota(jnp.int32, (FAR, FULL), 0)
    return (lane >> 4) == ((far & (FAR // GROUPS - 1)) * 2 + piece)


def slices(gradient, piece):
    rows = [jnp.broadcast_to(gradient[g : g + 1, :], (FAR // GROUPS, FULL)) for g in range(GROUPS)]
    rows = jnp.where(piece_mask(piece), jnp.concatenate(rows, axis=0), 0.0)
    lane = lax.broadcasted_iota(jnp.int32, (FULL, LANES), 1)
    source = lax.broadcasted_iota(jnp.int32, (FULL, LANES), 0)
    fold = jnp.where(lane - (LANES - 16) == (source & 15), 1.0, 0.0).astype(BF)
    return fine_dot(rows, fold, parts=2)


def unslice(parts):
    lane = lax.broadcasted_iota(jnp.int32, (LANES, FULL), 1)
    source = lax.broadcasted_iota(jnp.int32, (LANES, FULL), 0)
    spread = jnp.where(source - (LANES - 16) == (lane & 15), 1.0, 0.0).astype(BF)
    both = fine_dot(jnp.concatenate(parts, axis=0), spread, parts=2)
    total = jnp.where(piece_mask(0), both[:FAR], jnp.where(piece_mask(1), both[FAR:], 0.0))
    each = FAR // GROUPS
    return jnp.concatenate(
        [jnp.sum(total[g * each : (g + 1) * each], axis=0, keepdims=True) for g in range(GROUPS)], axis=0
    )


def gradient_of(totals, from_probes, to_probes, seen):
    values = fine_dot(totals, from_probes[...], parts=2) * seen[...]
    return fine_dot(values, to_probes[...], dot_t, 2)


def to_lines(rows):
    return jnp.concatenate([rows[:, part * LANES : (part + 1) * LANES] for part in range(4)], axis=0)


def from_lines(lines):
    each = lines.shape[0] // 4
    return jnp.concatenate([lines[part * each : (part + 1) * each, :] for part in range(4)], axis=1)


def second_gradient_body(near, peer, probes, seen, keep, send):
    totals = all_groups(half_sums(near), half_sums(peer))
    lane = lax.broadcasted_iota(jnp.int32, totals.shape, 1)
    totals = jnp.where((lane & (WIDE - 1)) < HALF, totals, 0.0)
    gradient = gradient_of(totals, probes, probes, seen)
    core = lax.axis_index("co")
    low, high = to_lines(gradient[:2]), to_lines(gradient[2:])
    keep[...] = jnp.where(core == 0, low, high)
    send[...] = jnp.where(core == 0, high, low)


def second_body(
    near, peer, pairs, tables, tmat, radius, base, image,
    extra, weights_out, sums, shifted,
):
    sums[...] = dot(pairs[...], jnp.concatenate([load_rows(near), load_rows(peer)], axis=0))
    for block in range(BLOCKS):
        k = block if block <= TOP else block - TOP
        at = pl.ds(block * BLOCK, BLOCK)
        value = sums[at, LANES:WIDE]
        weights_out[at, :] = (value if k % 2 == 0 else -value).astype(BF)
    field = mix(sums, shifted, tables)
    last = scatter(field, tmat, radius[...])
    zero, one = base[...], image[...]
    line = lax.broadcasted_iota(jnp.int32, (SHARE, LANES), 0)
    lane = lax.broadcasted_iota(jnp.int32, (SHARE, LANES), 1)
    out = jnp.zeros((SHARE, LANES), F32)
    pairs_of = ((zero, zero), (zero, one), (one, one), (zero, last), (one, last), (last, last))
    for index, (a, b) in enumerate(pairs_of):
        out = jnp.where((line == SCALAR_LINE) & (lane == PAD - LANES + index), jnp.sum(a * b), out)
    for piece in range(2):
        value = jnp.sum(near[pl.ds(SLICE_LINES[piece], FAR, stride=CHUNK), :], axis=0, keepdims=True)
        out = jnp.where((line == PIECE_LINES[piece]) & (lane >= LANES - 16), value, out)
    extra[...] = out


def sum_body(near, out):
    total = near[pl.ds(0, SHARE), :]
    for far in range(1, FAR):
        total = total + near[pl.ds(far * SHARE, SHARE), :]
    out[:SHARE, :] = total
    pieces = [near[pl.ds(PIECE_LINES[piece], FAR, stride=SHARE), :] for piece in range(2)]
    out[SHARE:, :] = to_lines(unslice(pieces))


def finish_body(
    near, peer, weights, tables, tmat, outwards, incident, image,
    solution_out, sensitivity_out, arnoldi_out, places, sums, shifted,
):
    scal = near[SCALAR_LINE : SCALAR_LINE + 1, :] + peer[SCALAR_LINE : SCALAR_LINE + 1, :]
    scal = scal / scal[:, PAD - LANES : PAD - LANES + 1]
    g01, g11, g02, g12, g22 = [scal[:, PAD - LANES + i : PAD - LANES + i + 1] for i in range(1, 6)]
    core = lax.axis_index("co")
    first = from_lines(near[SHARE:, :] + peer[SHARE:, :])
    mine, other = from_lines(near[:SHARE, :]), from_lines(peer[:SHARE, :])
    low, high = jnp.where(core == 0, mine, other), jnp.where(core == 0, other, mine)
    second = jnp.concatenate([low, high], axis=0)
    diag_first = 1.0 + g01
    below_sq = g11 - g01 * g01
    below_first = jnp.sqrt(below_sq)
    upper_second = (g02 - g01 * g01) / below_first
    shift_second = (g12 - g01 * g11 - g01 * g02 + g01 * g01 * g01) / below_sq
    diag_second = 1.0 + shift_second
    norm_sq = (g22 - 2.0 * g01 * g12 + g01 * g01 * g11) / below_sq
    rest_second = norm_sq - upper_second * upper_second - shift_second * shift_second
    gram_first = diag_first * diag_first + below_sq
    gram_cross = diag_first * upper_second + below_first * diag_second
    gram_second = upper_second * upper_second + diag_second * diag_second + rest_second
    determinant = gram_first * gram_second - gram_cross * gram_cross
    step_first = (diag_first * gram_second - upper_second * gram_cross) / determinant
    step_second = (gram_first * upper_second - gram_cross * diag_first) / determinant
    for_image = step_second / below_first
    for_base = step_first - for_image * g01
    arnoldi_out[0] = diag_first[0, 0]
    arnoldi_out[1] = below_first[0, 0]
    arnoldi_out[2] = diag_second[0, 0]
    arnoldi_out[3] = rest_second[0, 0]

    factor = COEFF * GROUPS / PROBES / SCALE / float(np.sqrt(np.float32(PER_GROUP)))
    gradient = (for_base * first + for_image * second) * factor
    real, imag = tmat[0:1, :], tmat[1:2, :]
    grad_re, grad_im = gradient[:, :WIDE], gradient[:, WIDE:]
    places[...] = jnp.zeros((LANES, FULL), F32)
    at = pl.ds(PAD - LANES, GROUPS)
    places[at, :WIDE] = real * grad_re + imag * grad_im
    places[at, WIDE:] = real * grad_im - imag * grad_re
    sums[...] = dot(weights[...], places[...].astype(BF))
    field = mix(sums, shifted, tables, dot_t)
    group = own_group()
    own = jnp.zeros((1, FULL), F32)
    for g in range(GROUPS):
        own = jnp.where(group == g, gradient[g : g + 1, :], own)
    lane = lax.broadcasted_iota(jnp.int32, (1, FULL), 1)
    own = jnp.where((lane & (WIDE - 1)) < HALF, own, 0.0)
    both = jnp.concatenate([image[...], own - field], axis=0)
    result = fine_dot(both, outwards[...])
    image_rows = result[:OWN]
    solution_out[...] = for_base * incident[...] + (for_image / SCALE) * image_rows
    sensitivity_out[...] = result[ROWS : ROWS + OWN]


def call(body, outs, scratch=(), operands=(), spaces=None, out_spaces=None, cost=None, aliases=None):
    spaces, out_spaces = spaces or {}, out_spaces or {}
    return pl.pallas_call(
        body,
        out_shape=[jax.ShapeDtypeStruct(shape, kind) for shape, kind in outs],
        in_specs=[pl.BlockSpec(memory_space=spaces.get(i, pltpu.VMEM)) for i in range(len(operands))],
        out_specs=[pl.BlockSpec(memory_space=out_spaces.get(i, pltpu.VMEM)) for i in range(len(outs))],
        scratch_shapes=list(scratch),
        compiler_params=pltpu.CompilerParams(vmem_limit_bytes=16 * 1024 * 1024),
        cost_estimate=cost,
        input_output_aliases=aliases or {},
    )(*operands)


def swap_cores(array):
    return lax.ppermute(array, "co", [(0, 1), (1, 0)])


def spread_far(lines):
    parts = lines.reshape(FAR, lines.shape[0] // FAR, LANES)
    return lax.all_to_all(parts, FAR_AXES, 0, 0).reshape(lines.shape)


def on_device(
    incident,
    sphere_site,
    jitter,
    rotation_table,
    axial_tables,
    tmatrix,
    radius_factor,
    probe_field,
    probe_group,
):
    line_scratch = pltpu.VMEM((4 * ROWS, LANES), F32)
    sum_scratch = pltpu.VMEM((BLOCKS * BLOCK, FULL), F32)
    shift_scratch = pltpu.VMEM((2, (ORDER + 1) * BLOCK, FULL), BF)
    rows_shape = ((ROWS, FULL), F32)
    chunk_shape = ((FAR * CHUNK, LANES), F32)
    share_shape = ((SHARE, LANES), F32)
    half_cost = pl.CostEstimate(flops=8_000_000_000, bytes_accessed=4_000_000, transcendentals=0)

    (chunk,) = call(send_body, [chunk_shape], [line_scratch], (incident,))

    def by_core(array):
        lead = array.shape[:-1]
        return jnp.swapaxes(array.reshape(lead + (2, 2, PER_GROUP)), -3, -2).reshape(lead + (SPHERES,))

    plain_probes = probe_field.T
    pairs, tables, probes, seen, tmat, inwards, outwards, base, radius = call(
        prepare_body,
        [
            ((BLOCKS * BLOCK, SPHERES), BF),
            ((2, FULL, FULL), BF),
            ((FULL, PROBES_OWN), BF),
            ((GROUPS, PROBES_OWN), F32),
            ((ROWS, WIDE), F32),
            ((COEFF, FULL), BF),
            ((FULL, COEFF), BF),
            rows_shape,
            ((ROWS, LANES), F32),
        ],
        operands=(
            by_core(sphere_site[None, :]),
            by_core(jitter),
            rotation_table,
            axial_tables,
            plain_probes,
            probe_group.reshape(1, PROBES_OWN),
            tmatrix,
            jnp.asarray(_SOURCE),
            incident,
            radius_factor,
        ),
        spaces={9: pltpu.SMEM},
        cost=pl.CostEstimate(flops=8_000_000_000, bytes_accessed=8_000_000, transcendentals=20_000),
    )

    near = spread_far(chunk)
    (near,) = call(order_body, [chunk_shape], operands=(near, pairs), spaces={1: pl.ANY}, aliases={0: 0})
    chunk, image = call(
        first_body,
        [chunk_shape, rows_shape],
        [sum_scratch, shift_scratch, line_scratch],
        (near, swap_cores(near), pairs, inwards, tables, tmat, radius, plain_probes, probes, seen),
    )

    near = spread_far(chunk)
    peer = swap_cores(near)
    keep, send = call(second_gradient_body, [share_shape, share_shape], operands=(near, peer, probes, seen))
    received = swap_cores(send)
    extra, weights = call(
        second_body,
        [share_shape, ((BLOCKS * BLOCK, LANES), BF)],
        [sum_scratch, shift_scratch],
        (near, peer, pairs, tables, tmat, radius, base, image),
        cost=half_cost,
    )
    share = keep + received + extra
    near = spread_far(jnp.broadcast_to(share[None], (FAR, SHARE, LANES)).reshape(FAR * SHARE, LANES))
    (near,) = call(sum_body, [((SHARE + GROUPS * 4, LANES), F32)], operands=(near,))
    peer = swap_cores(near)
    solution_rows, sensitivity_rows, arnoldi = call(
        finish_body,
        [((OWN, COEFF), F32), ((OWN, COEFF), F32), ((4,), F32)],
        [pltpu.VMEM((LANES, FULL), F32), sum_scratch, shift_scratch],
        (near, peer, weights, tables, tmat, outwards, incident, image),
        out_spaces={2: pltpu.SMEM},
    )
    return solution_rows, sensitivity_rows, arnoldi


def solution(mesh):
    fine = Mesh(mesh.devices.reshape(2, 2, 4, 2, 4), ALL_AXES)
    split_rows = P(ALL_AXES)
    return jax.shard_map(
        on_device,
        mesh=fine,
        in_specs=(
            P(ALL_AXES, None),
            P(),
            P(),
            P(),
            P(),
            P(),
            split_rows,
            P(ALL_AXES, None),
            split_rows,
        ),
        out_specs=(P(ALL_AXES, None), P(ALL_AXES, None), P()),
        check_vma=False,
    )
```

```python
import jax
import jax.numpy as jnp
import numpy as np
from jax import lax
from jax.experimental import pallas as pl
from jax.experimental.pallas import tpu as pltpu
from jax.sharding import Mesh
from jax.sharding import PartitionSpec as P

ORDER = 10
WAVENUMBER = 1.3
LATTICE_STEP = 2.5

SPHERES = 768
COEFF = 480
HALF = 240
GROUPS = 4
PER_GROUP = SPHERES // GROUPS
PROBES = 32768
OWN = 6
PROBES_OWN = 256
LANES = 128
WIDE = 256
FULL = 2 * WIDE
ROWS = 8
BLOCK = 2 * ROWS
BLOCKS = 4 * ORDER + 1
TOP = 2 * ORDER
CHUNK = OWN * FULL // LANES
FAR = 64
SCALE = 2.0**-14
PAD = HALF
SHARE = 2 * FULL // LANES
SCALAR_LINE = 2
SCALARS = SHARE + 4 * GROUPS
PIECE_LINES = (6, 7)
SLICE_LINES = (3, 7)
BF = jnp.bfloat16
F32 = jnp.float32

FAR_AXES = ("xl", "z", "xh", "y")
ALL_AXES = ("xl", "co", "z", "xh", "y")


def order_table(degree_max):
    entries = np.arange(degree_max * (degree_max + 2))
    degree = np.floor(np.sqrt(entries + 1.0) + 1e-09)
    orders = entries + 1 - degree * degree - degree
    return np.concatenate([orders, orders]).astype(np.int32)


_ORDERS = order_table(ORDER)
_SORTED = np.lexsort((_ORDERS, np.abs(_ORDERS)))
_SOURCE = np.full((1, FULL), -1, np.int32)
_SOURCE[0, :HALF] = _SORTED
_SOURCE[0, WIDE : WIDE + HALF] = _SORTED + HALF


def spans(half):
    part = _ORDERS[_SORTED][half * LANES : (half + 1) * LANES]
    found = []
    for order in dict.fromkeys(int(m) for m in part):
        lanes = np.flatnonzero(part == order)
        found.append((order, int(lanes[0]), int(lanes[-1]) + 1))
    return found


SPANS = (spans(0), spans(1))


def by_lane(lane, entries):
    chosen = entries[-1][0]
    for value, end in reversed(entries[:-1]):
        chosen = jnp.where(lane < end, value, chosen)
    return chosen


def dot(a, b):
    return jnp.dot(a, b, preferred_element_type=F32)


def dot_t(a, b):
    return lax.dot_general(a, b, (((1,), (1,)), ((), ())), preferred_element_type=F32)


def fine_dot(x, y, dot=dot, parts=3):
    rows = x.shape[0]
    padded = -(-rows // 16) * 16
    if padded > rows:
        x = jnp.concatenate([x, jnp.zeros((padded - rows, x.shape[1]), F32)], axis=0)
    terms = []
    for _ in range(parts):
        terms.append(x.astype(BF))
        x = x - terms[-1].astype(F32)
    product = dot(jnp.concatenate(terms, axis=0), y)
    total = product[:rows]
    for part in range(1, parts):
        total = total + product[part * padded : part * padded + rows]
    return total


def onehot_in(source):
    rows = lax.broadcasted_iota(jnp.int32, (COEFF, FULL), 0)
    return jnp.where(rows == source, 1.0, 0.0).astype(BF)


def own_group():
    return lax.axis_index("xl") * 2 + lax.axis_index("co")


def send_body(incident, chunk, lines):
    value = jnp.concatenate([incident[...], jnp.zeros((ROWS - OWN, COEFF), F32)], axis=0) * SCALE
    value = jnp.concatenate([value, jnp.zeros((ROWS, FULL - COEFF), F32)], axis=1)
    write_chunks(value, chunk, lines)


def write_chunks(rows, chunk, lines):
    for part in range(4):
        lines[pl.ds(part, ROWS, stride=4), :] = rows[:, part * LANES : (part + 1) * LANES]
    once = lines[:CHUNK, :]
    for far in range(FAR):
        chunk[far * CHUNK : (far + 1) * CHUNK, :] = once


def prepare_body(
    site, jitter, rotation, axial, probes, probe_group, tmat, source, incident, radius,
    pairs, tables, probes_out, seen_out, tmat_out, inwards_out, base_out, radius_out,
):
    own = (
        lax.axis_index("xl") * PER_GROUP
        + ((lax.axis_index("z") * 2 + lax.axis_index("xh")) * 4 + lax.axis_index("y")) * OWN
    )
    sites = site[...]
    core = lax.axis_index("co")

    def own_core_first(place):
        other = jnp.concatenate([place[:, SPHERES // 2 :], place[:, : SPHERES // 2]], axis=1)
        return jnp.where(core == 0, place, other)

    place_x = own_core_first((sites & 7).astype(F32) * LATTICE_STEP + jitter[0:1, :])
    place_y = own_core_first(((sites >> 3) & 7).astype(F32) * LATTICE_STEP + jitter[1:2, :])
    place_z = own_core_first((sites >> 6).astype(F32) * LATTICE_STEP + jitter[2:3, :])
    lane = lax.broadcasted_iota(jnp.int32, (ROWS, SPHERES), 1)
    line = lax.broadcasted_iota(jnp.int32, (ROWS, SPHERES), 0)
    same = lane == line + own

    def offset(place):
        here = jnp.sum(jnp.where(same, place, 0.0), axis=1, keepdims=True)
        return here - place

    dx, dy, dz = offset(place_x), offset(place_y), offset(place_z)
    distance = jnp.sqrt(jnp.where(same, 1.0, dx * dx + dy * dy + dz * dz))
    phase = WAVENUMBER * distance
    none = same | (line >= OWN)
    radial_cos = jnp.where(none, 0.0, jnp.cos(phase) / phase)
    radial_sin = jnp.where(none, 0.0, jnp.sin(phase) / phase)
    larger = jnp.maximum(jnp.abs(dx), jnp.abs(dy))
    apart = larger > 0.0
    inverse = 1.0 / jnp.where(apart, larger, 1.0)
    ax, ay = dx * inverse, dy * inverse
    length = jnp.sqrt(jnp.where(apart, ax * ax + ay * ay, 1.0))
    cos_one = jnp.where(apart, ax / length, 1.0)
    sin_one = jnp.where(apart, ay / length, 0.0)

    def put(block, factor):
        value = jnp.concatenate([radial_cos * factor, radial_sin * factor], axis=0)
        pairs[block * BLOCK : (block + 1) * BLOCK, :] = value.astype(BF)

    pairs[0:BLOCK, :] = jnp.concatenate([radial_cos, radial_sin], axis=0).astype(BF)
    cos_k, sin_k = cos_one, sin_one
    for k in range(1, TOP + 1):
        put(k, cos_k)
        put(TOP + k, sin_k)
        if k < TOP:
            cos_k, sin_k = (
                cos_k * cos_one - sin_k * sin_one,
                sin_k * cos_one + cos_k * sin_one,
            )

    inwards = onehot_in(source[...])
    inwards_out[...] = inwards
    outwards = inwards.astype(F32).T.astype(BF)
    probes_out[...] = dot(outwards, probes[...]).astype(BF)
    turned = dot(outwards, rotation[...]).astype(BF)
    for radial in range(2):
        tables[radial] = fine_dot(0.5 * dot(turned, axial[radial]), turned, dot_t, 2).astype(BF)
    line = lax.broadcasted_iota(jnp.int32, (GROUPS, PROBES_OWN), 0)
    seen_out[...] = jnp.where(line == probe_group[...], 1.0, 0.0)
    tmat_rows = jnp.concatenate([tmat[...], jnp.zeros((ROWS - 2, HALF), F32)], axis=0)
    tmat_out[...] = fine_dot(tmat_rows, inwards[:HALF, :WIDE])
    value = jnp.concatenate([incident[...], jnp.zeros((ROWS - OWN, COEFF), F32)], axis=0) * SCALE
    base_out[...] = fine_dot(value, inwards)
    line = lax.broadcasted_iota(jnp.int32, (ROWS, LANES), 0)
    column = jnp.zeros((ROWS, LANES), F32)
    for r in range(OWN):
        column = jnp.where(line == r, radius[r], column)
    radius_out[...] = column


def load_rows(lines):
    parts = [lines[pl.ds(part, SPHERES // 2, stride=4), :].astype(BF) for part in range(4)]
    return jnp.concatenate(parts, axis=1)


def half_sums(lines):
    groups = []
    for place in range(2):
        parts = []
        for part in range(4):
            value = lines[pl.ds(place * PER_GROUP * 4 + part, PER_GROUP, stride=4), :]
            parts.append(jnp.sum(value, axis=0, keepdims=True))
        groups.append(jnp.concatenate(parts, axis=1))
    return jnp.concatenate(groups, axis=0)


def all_groups(mine, other):
    core = lax.axis_index("co")
    first, second = jnp.where(core == 0, mine, other), jnp.where(core == 0, other, mine)
    return jnp.concatenate([first[0:1], second[0:1], first[1:2], second[1:2]], axis=0)


def order_body(near_in, pairs, near_out):
    del near_in, pairs, near_out


def near_body(near, inwards, rows_out, totals_out):
    rows_out[...] = dot(load_rows(near)[:, :COEFF], inwards[...]).astype(BF)
    totals_out[...] = half_sums(near)


def mix(sums, shifted, tables, dot=dot):
    for k in range(1, TOP + 1):
        at_cos, at_sin = pl.ds(k * BLOCK, BLOCK), pl.ds((TOP + k) * BLOCK, BLOCK)
        cos_re, cos_im = sums[at_cos, :WIDE], sums[at_cos, WIDE:]
        sin_re, sin_im = sums[at_sin, :WIDE], sums[at_sin, WIDE:]
        sums[at_cos, :WIDE] = cos_re - sin_im
        sums[at_cos, WIDE:] = cos_im + sin_re
        sums[at_sin, :WIDE] = cos_re + sin_im
        sums[at_sin, WIDE:] = cos_im - sin_re

    def block_of(k):
        return (k if k >= 0 else TOP - k) * BLOCK

    for half in range(2):
        lane = lax.broadcasted_iota(jnp.int32, (BLOCK, LANES), 1)

        def pick(out_order, start):
            columns = slice(start + half * LANES, start + (half + 1) * LANES)
            entries = []
            for order, _, end in SPANS[half]:
                row = block_of(order - out_order)
                entries.append((sums[row : row + BLOCK, columns], end))
            return by_lane(lane, entries)

        for out_order in range(ORDER + 1):
            minus_re, minus_im = pick(out_order, 0), pick(out_order, WIDE)
            if out_order:
                plus_re, plus_im = pick(-out_order, 0), pick(-out_order, WIDE)
            else:
                plus_re, plus_im = minus_re, minus_im
            cos_part = (minus_re + plus_re, minus_im + plus_im)
            sin_part = (plus_im - minus_im, minus_re - plus_re)
            for which, start in ((0, 0), (1, WIDE)):
                columns = slice(start + half * LANES, start + (half + 1) * LANES)
                for radial in range(2):
                    lines = slice(radial * ROWS, (radial + 1) * ROWS)
                    value = jnp.concatenate([cos_part[which][lines], sin_part[which][lines]], axis=0)
                    shifted[radial, out_order * BLOCK : (out_order + 1) * BLOCK, columns] = value.astype(BF)

    back = dot(shifted[0], tables[0]) + dot(shifted[1], tables[1])
    parts_re, parts_im = [], []
    lane = lax.broadcasted_iota(jnp.int32, (ROWS, LANES), 1)
    for half in range(2):
        real = slice(half * LANES, (half + 1) * LANES)
        imag = slice(WIDE + half * LANES, WIDE + (half + 1) * LANES)
        entries_re, entries_im = [], []
        for order, _, end in SPANS[half]:
            m = abs(order)
            cos_lines = slice(m * BLOCK, m * BLOCK + ROWS)
            sin_lines = slice(m * BLOCK + ROWS, (m + 1) * BLOCK)
            value_re, value_im = back[cos_lines, real], back[cos_lines, imag]
            if order > 0:
                value_re, value_im = value_re + back[sin_lines, imag], value_im - back[sin_lines, real]
            if order < 0:
                value_re, value_im = value_re - back[sin_lines, imag], value_im + back[sin_lines, real]
            entries_re.append((value_re, end))
            entries_im.append((value_im, end))
        parts_re.append(by_lane(lane, entries_re))
        parts_im.append(by_lane(lane, entries_im))
    return jnp.concatenate(parts_re + parts_im, axis=1)


def scatter(field, tmat, radius):
    real, imag = tmat[0:1, :], tmat[1:2, :]
    field_re, field_im = field[:, :WIDE], field[:, WIDE:]
    wide = jnp.concatenate([radius, radius], axis=1)
    return jnp.concatenate(
        [
            wide * (imag * field_im - real * field_re),
            -wide * (imag * field_re + real * field_im),
        ],
        axis=1,
    )


def first_body(
    near_rows, near_totals, peer, pairs, inwards, tables, tmat, radius, plain_probes, probes, seen,
    chunk, rows_out, sums, shifted, lines,
):
    rows = dot(load_rows(peer)[:, :COEFF], inwards[...]).astype(BF)
    sums[...] = dot(pairs[...], jnp.concatenate([near_rows[...], rows], axis=0))
    totals = all_groups(near_totals[...], half_sums(peer))[:, :COEFF]
    gradient = gradient_of(totals, plain_probes, probes, seen)
    field = mix(sums, shifted, tables)
    image = scatter(field, tmat, radius[...])
    rows_out[...] = image
    lane = lax.broadcasted_iota(jnp.int32, (ROWS, FULL), 1)
    marked = jnp.where(lane == PAD + own_group(), jnp.concatenate([radius[...]] * 4, axis=1), image)
    write_chunks(marked, chunk, lines)
    for piece in range(2):
        line = SLICE_LINES[piece]
        chunk[pl.ds(line, FAR, stride=CHUNK), :] = lines[line : line + 1, :] + slices(gradient, piece)


def piece_mask(piece):
    lane = lax.broadcasted_iota(jnp.int32, (FAR, FULL), 1)
    far = lax.broadcasted_iota(jnp.int32, (FAR, FULL), 0)
    return (lane >> 4) == ((far & (FAR // GROUPS - 1)) * 2 + piece)


def slices(gradient, piece):
    rows = [jnp.broadcast_to(gradient[g : g + 1, :], (FAR // GROUPS, FULL)) for g in range(GROUPS)]
    rows = jnp.where(piece_mask(piece), jnp.concatenate(rows, axis=0), 0.0)
    lane = lax.broadcasted_iota(jnp.int32, (FULL, LANES), 1)
    source = lax.broadcasted_iota(jnp.int32, (FULL, LANES), 0)
    fold = jnp.where(lane - (LANES - 16) == (source & 15), 1.0, 0.0).astype(BF)
    return fine_dot(rows, fold, parts=2)


def unslice(parts):
    lane = lax.broadcasted_iota(jnp.int32, (LANES, FULL), 1)
    source = lax.broadcasted_iota(jnp.int32, (LANES, FULL), 0)
    spread = jnp.where(source - (LANES - 16) == (lane & 15), 1.0, 0.0).astype(BF)
    both = fine_dot(jnp.concatenate(parts, axis=0), spread, parts=2)
    total = jnp.where(piece_mask(0), both[:FAR], jnp.where(piece_mask(1), both[FAR:], 0.0))
    each = FAR // GROUPS
    return jnp.concatenate(
        [jnp.sum(total[g * each : (g + 1) * each], axis=0, keepdims=True) for g in range(GROUPS)], axis=0
    )


def gradient_of(totals, from_probes, to_probes, seen):
    values = fine_dot(totals, from_probes[...], parts=2) * seen[...]
    return fine_dot(values, to_probes[...], dot_t, 2)


def to_lines(rows):
    return jnp.concatenate([rows[:, part * LANES : (part + 1) * LANES] for part in range(4)], axis=0)


def from_lines(lines):
    each = lines.shape[0] // 4
    return jnp.concatenate([lines[part * each : (part + 1) * each, :] for part in range(4)], axis=1)


def second_gradient_body(near, peer, probes, seen, keep, send):
    totals = all_groups(half_sums(near), half_sums(peer))
    lane = lax.broadcasted_iota(jnp.int32, totals.shape, 1)
    totals = jnp.where((lane & (WIDE - 1)) < HALF, totals, 0.0)
    gradient = gradient_of(totals, probes, probes, seen)
    core = lax.axis_index("co")
    low, high = to_lines(gradient[:2]), to_lines(gradient[2:])
    keep[...] = jnp.where(core == 0, low, high)
    send[...] = jnp.where(core == 0, high, low)


def second_body(
    near, peer, pairs, tables, tmat, radius, base, image,
    extra, weights_out, sums, shifted,
):
    sums[...] = dot(pairs[...], jnp.concatenate([load_rows(near), load_rows(peer)], axis=0))
    for block in range(BLOCKS):
        k = block if block <= TOP else block - TOP
        at = pl.ds(block * BLOCK, BLOCK)
        value = sums[at, LANES:WIDE]
        weights_out[at, :] = (value if k % 2 == 0 else -value).astype(BF)
    field = mix(sums, shifted, tables)
    last = scatter(field, tmat, radius[...])
    zero, one = base[...], image[...]
    line = lax.broadcasted_iota(jnp.int32, (SHARE, LANES), 0)
    lane = lax.broadcasted_iota(jnp.int32, (SHARE, LANES), 1)
    pairs_of = ((zero, zero), (zero, one), (one, one), (zero, last), (one, last), (last, last))
    sums_of = []
    for a, b in pairs_of:
        product = a * b
        parts = [product[:, part * LANES : (part + 1) * LANES] for part in range(4)]
        sums_of.append(jnp.sum((parts[0] + parts[1]) + (parts[2] + parts[3]), axis=0, keepdims=True))
    stacked = jnp.concatenate(sums_of + [jnp.zeros((SHARE - 6, LANES), F32)], axis=0)
    column = jnp.sum(stacked, axis=1, keepdims=True)
    row = jnp.sum(jnp.where(lane - (PAD - LANES) == line, column, 0.0), axis=0, keepdims=True)
    out = jnp.where(line == SCALAR_LINE, row, 0.0)
    for piece in range(2):
        value = jnp.sum(near[pl.ds(SLICE_LINES[piece], FAR, stride=CHUNK), :], axis=0, keepdims=True)
        out = jnp.where((line == PIECE_LINES[piece]) & (lane >= LANES - 16), value, out)
    extra[...] = out


def sum_body(near, out):
    total = near[pl.ds(0, SHARE), :]
    for far in range(1, FAR):
        total = total + near[pl.ds(far * SHARE, SHARE), :]
    out[:SHARE, :] = total
    pieces = [near[pl.ds(PIECE_LINES[piece], FAR, stride=SHARE), :] for piece in range(2)]
    out[SHARE:SCALARS, :] = to_lines(unslice(pieces))
    line = total[SCALAR_LINE : SCALAR_LINE + 1, :]
    for index in range(6):
        at = PAD - LANES + index
        out[SCALARS + index : SCALARS + index + 1, :] = jnp.broadcast_to(line[:, at : at + 1], (1, LANES))


def finish_body(
    near, peer, weights, tables, tmat, inwards, incident, image,
    solution_out, sensitivity_out, arnoldi_out, places, sums, shifted,
):
    g00, g01, g11, g02, g12, g22 = [near[at : at + 1, :] + peer[at : at + 1, :] for at in range(SCALARS, SCALARS + 6)]
    scale = 1.0 / g00
    g01, g11, g02, g12, g22 = g01 * scale, g11 * scale, g02 * scale, g12 * scale, g22 * scale
    core = lax.axis_index("co")
    first = from_lines(near[SHARE:SCALARS, :] + peer[SHARE:SCALARS, :])
    mine, other = from_lines(near[:SHARE, :]), from_lines(peer[:SHARE, :])
    low, high = jnp.where(core == 0, mine, other), jnp.where(core == 0, other, mine)
    second = jnp.concatenate([low, high], axis=0)
    diag_first = 1.0 + g01
    below_sq = g11 - g01 * g01
    inverse = 1.0 / below_sq
    upper = g02 - g01 * g01
    shift = g12 - g01 * (g11 + g02 - g01 * g01)
    norm_sq = g22 - g01 * (2.0 * g12 - g01 * g11)
    cross = diag_first * upper + below_sq + shift
    gram_first = diag_first * diag_first + below_sq
    gram_second = (below_sq + 2.0 * shift + norm_sq) * inverse
    cross_scaled = cross * inverse
    determinant = gram_first * gram_second - cross * cross_scaled
    for_image = (upper - diag_first * (1.0 + shift * inverse)) / determinant
    for_base = (diag_first * gram_second - upper * cross_scaled) / determinant - for_image * g01
    below_first = jnp.sqrt(below_sq)
    shift_second = shift * inverse
    diag_second = 1.0 + shift_second
    rest_second = (norm_sq - upper * upper) * inverse - shift_second * shift_second
    arnoldi_out[0] = diag_first[0, 0]
    arnoldi_out[1] = below_first[0, 0]
    arnoldi_out[2] = diag_second[0, 0]
    arnoldi_out[3] = rest_second[0, 0]

    for_base, for_image = [jnp.concatenate([part] * 4, axis=1) for part in (for_base, for_image)]
    factor = COEFF * GROUPS / PROBES / SCALE / float(np.sqrt(np.float32(PER_GROUP)))
    gradient = (for_base * first + for_image * second) * factor
    real, imag = tmat[0:1, :], tmat[1:2, :]
    grad_re, grad_im = gradient[:, :WIDE], gradient[:, WIDE:]
    places[...] = jnp.zeros((LANES, FULL), F32)
    at = pl.ds(PAD - LANES, GROUPS)
    places[at, :WIDE] = real * grad_re + imag * grad_im
    places[at, WIDE:] = real * grad_im - imag * grad_re
    sums[...] = dot(weights[...], places[...].astype(BF))
    field = mix(sums, shifted, tables, dot_t)
    group = own_group()
    own = jnp.zeros((1, FULL), F32)
    for g in range(GROUPS):
        own = jnp.where(group == g, gradient[g : g + 1, :], own)
    lane = lax.broadcasted_iota(jnp.int32, (1, FULL), 1)
    own = jnp.where((lane & (WIDE - 1)) < HALF, own, 0.0)
    both = jnp.concatenate([image[...], own - field], axis=0)
    result = fine_dot(both, inwards[...], dot_t)
    image_rows = result[:OWN]
    solution_out[...] = for_base[:, :COEFF] * incident[...] + (for_image[:, :COEFF] / SCALE) * image_rows
    sensitivity_out[...] = result[ROWS : ROWS + OWN]


def call(body, outs, scratch=(), operands=(), spaces=None, out_spaces=None, cost=None, aliases=None):
    spaces, out_spaces = spaces or {}, out_spaces or {}
    return pl.pallas_call(
        body,
        out_shape=[jax.ShapeDtypeStruct(shape, kind) for shape, kind in outs],
        in_specs=[pl.BlockSpec(memory_space=spaces.get(i, pltpu.VMEM)) for i in range(len(operands))],
        out_specs=[pl.BlockSpec(memory_space=out_spaces.get(i, pltpu.VMEM)) for i in range(len(outs))],
        scratch_shapes=list(scratch),
        compiler_params=pltpu.CompilerParams(vmem_limit_bytes=16 * 1024 * 1024),
        cost_estimate=cost,
        input_output_aliases=aliases or {},
    )(*operands)


def swap_cores(array):
    return lax.ppermute(array, "co", [(0, 1), (1, 0)])


def spread_far(lines):
    parts = lines.reshape(FAR, lines.shape[0] // FAR, LANES)
    return lax.all_to_all(parts, FAR_AXES, 0, 0).reshape(lines.shape)


def on_device(
    incident,
    sphere_site,
    jitter,
    rotation_table,
    axial_tables,
    tmatrix,
    radius_factor,
    probe_field,
    probe_group,
):
    line_scratch = pltpu.VMEM((4 * ROWS, LANES), F32)
    sum_scratch = pltpu.VMEM((BLOCKS * BLOCK, FULL), F32)
    shift_scratch = pltpu.VMEM((2, (ORDER + 1) * BLOCK, FULL), BF)
    rows_shape = ((ROWS, FULL), F32)
    chunk_shape = ((FAR * CHUNK, LANES), F32)
    share_shape = ((SHARE, LANES), F32)
    half_cost = pl.CostEstimate(flops=8_000_000_000, bytes_accessed=4_000_000, transcendentals=0)

    (chunk,) = call(send_body, [chunk_shape], [line_scratch], (incident,))

    def by_core(array):
        lead = array.shape[:-1]
        return jnp.swapaxes(array.reshape(lead + (2, 2, PER_GROUP)), -3, -2).reshape(lead + (SPHERES,))

    plain_probes = probe_field.T
    pairs, tables, probes, seen, tmat, inwards, base, radius = call(
        prepare_body,
        [
            ((BLOCKS * BLOCK, SPHERES), BF),
            ((2, FULL, FULL), BF),
            ((FULL, PROBES_OWN), BF),
            ((GROUPS, PROBES_OWN), F32),
            ((ROWS, WIDE), F32),
            ((COEFF, FULL), BF),
            rows_shape,
            ((ROWS, LANES), F32),
        ],
        operands=(
            by_core(sphere_site[None, :]),
            by_core(jitter),
            rotation_table,
            axial_tables,
            plain_probes,
            probe_group.reshape(1, PROBES_OWN),
            tmatrix,
            jnp.asarray(_SOURCE),
            incident,
            radius_factor,
        ),
        spaces={9: pltpu.SMEM},
        cost=pl.CostEstimate(flops=8_000_000_000, bytes_accessed=8_000_000, transcendentals=20_000),
    )

    near = spread_far(chunk)
    (near,) = call(order_body, [chunk_shape], operands=(near, pairs), spaces={1: pl.ANY}, aliases={0: 0})
    near_rows, near_totals = call(
        near_body,
        [((SPHERES // 2, FULL), BF), ((2, FULL), F32)],
        operands=(near, inwards),
        cost=half_cost,
    )
    chunk, image = call(
        first_body,
        [chunk_shape, rows_shape],
        [sum_scratch, shift_scratch, line_scratch],
        (near_rows, near_totals, swap_cores(near), pairs, inwards, tables, tmat, radius, plain_probes, probes, seen),
    )

    near = spread_far(chunk)
    peer = swap_cores(near)
    keep, send = call(second_gradient_body, [share_shape, share_shape], operands=(near, peer, probes, seen))
    received = swap_cores(send)
    extra, weights = call(
        second_body,
        [share_shape, ((BLOCKS * BLOCK, LANES), BF)],
        [sum_scratch, shift_scratch],
        (near, peer, pairs, tables, tmat, radius, base, image),
        cost=half_cost,
    )
    share = keep + received + extra
    near = spread_far(jnp.broadcast_to(share[None], (FAR, SHARE, LANES)).reshape(FAR * SHARE, LANES))
    (near,) = call(sum_body, [((SCALARS + 8, LANES), F32)], operands=(near,))
    peer = swap_cores(near)
    solution_rows, sensitivity_rows, arnoldi = call(
        finish_body,
        [((OWN, COEFF), F32), ((OWN, COEFF), F32), ((4,), F32)],
        [pltpu.VMEM((LANES, FULL), F32), sum_scratch, shift_scratch],
        (near, peer, weights, tables, tmat, inwards, incident, image),
        out_spaces={2: pltpu.SMEM},
    )
    return solution_rows, sensitivity_rows, arnoldi


def solution(mesh):
    fine = Mesh(mesh.devices.reshape(2, 2, 4, 2, 4), ALL_AXES)
    split_rows = P(ALL_AXES)
    return jax.shard_map(
        on_device,
        mesh=fine,
        in_specs=(
            P(ALL_AXES, None),
            P(),
            P(),
            P(),
            P(),
            P(),
            split_rows,
            P(ALL_AXES, None),
            split_rows,
        ),
        out_specs=(P(ALL_AXES, None), P(ALL_AXES, None), P()),
        check_vma=False,
    )
```

```python
import jax
import jax.numpy as jnp
import numpy as np
from jax import lax
from jax.experimental import pallas as pl
from jax.experimental.pallas import tpu as pltpu
from jax.sharding import Mesh
from jax.sharding import PartitionSpec as P

ORDER = 10
WAVENUMBER = 1.3
LATTICE_STEP = 2.5

SPHERES = 768
COEFF = 480
HALF = 240
GROUPS = 4
PER_GROUP = SPHERES // GROUPS
PROBES = 32768
OWN = 6
PROBES_OWN = 256
LANES = 128
WIDE = 256
FULL = 2 * WIDE
ROWS = 8
BLOCK = 2 * ROWS
BLOCKS = 4 * ORDER + 1
TOP = 2 * ORDER
CHUNK = OWN * FULL // LANES
FAR = 64
SCALE = 2.0**-14
PAD = HALF
SIN_ROWS = (ORDER + 2) * ROWS
SHARE = 2 * FULL // LANES
SCALAR_LINE = 2
SCALARS = SHARE + 4 * GROUPS
PIECE_LINES = (6, 7)
SLICE_LINES = (3, 7)
BF = jnp.bfloat16
F32 = jnp.float32

FAR_AXES = ("xl", "z", "xh", "y")
ALL_AXES = ("xl", "co", "z", "xh", "y")


def order_table(degree_max):
    entries = np.arange(degree_max * (degree_max + 2))
    degree = np.floor(np.sqrt(entries + 1.0) + 1e-09)
    orders = entries + 1 - degree * degree - degree
    return np.concatenate([orders, orders]).astype(np.int32)


_ORDERS = np.zeros((1, WIDE), np.int32)
_ORDERS[0, :HALF] = order_table(ORDER)


def dot(a, b):
    return jnp.dot(a, b, preferred_element_type=F32)


def dot_t(a, b):
    return lax.dot_general(a, b, (((1,), (1,)), ((), ())), preferred_element_type=F32)


def fine_dot(x, y, dot=dot, parts=3):
    rows = x.shape[0]
    padded = -(-rows // 16) * 16
    if padded > rows:
        x = jnp.concatenate([x, jnp.zeros((padded - rows, x.shape[1]), F32)], axis=0)
    terms = []
    for _ in range(parts):
        terms.append(x.astype(BF))
        x = x - terms[-1].astype(F32)
    product = dot(jnp.concatenate(terms, axis=0), y)
    total = product[:rows]
    for part in range(1, parts):
        total = total + product[part * padded : part * padded + rows]
    return total


def padded(x, axis):
    zeros = jnp.zeros((x.shape[0], WIDE - HALF) if axis else (WIDE - HALF, x.shape[1]), x.dtype)
    low, high = (x[:, :HALF], x[:, HALF:]) if axis else (x[:HALF, :], x[HALF:, :])
    return jnp.concatenate([low, zeros, high, zeros], axis=axis)


def own_rows(incident):
    value = jnp.concatenate([incident[...], jnp.zeros((ROWS - OWN, COEFF), F32)], axis=0) * SCALE
    return padded(value, 1)


def own_group():
    return lax.axis_index("xl") * 2 + lax.axis_index("co")


def send_body(incident, chunk, lines):
    write_chunks(own_rows(incident), chunk, lines)


def write_chunks(rows, chunk, lines):
    for part in range(4):
        lines[pl.ds(part, ROWS, stride=4), :] = rows[:, part * LANES : (part + 1) * LANES]
    once = lines[:CHUNK, :]
    for far in range(FAR):
        chunk[far * CHUNK : (far + 1) * CHUNK, :] = once


def prepare_body(
    site, jitter, rotation, axial, probes, probe_group, tmat, orders, incident, radius,
    pairs, tables, probes_out, seen_out, tmat_out, orders_out, base_out, radius_out,
):
    own = (
        lax.axis_index("xl") * PER_GROUP
        + ((lax.axis_index("z") * 2 + lax.axis_index("xh")) * 4 + lax.axis_index("y")) * OWN
    )
    sites = site[...]
    core = lax.axis_index("co")

    def own_core_first(place):
        other = jnp.concatenate([place[:, SPHERES // 2 :], place[:, : SPHERES // 2]], axis=1)
        return jnp.where(core == 0, place, other)

    place_x = own_core_first((sites & 7).astype(F32) * LATTICE_STEP + jitter[0:1, :])
    place_y = own_core_first(((sites >> 3) & 7).astype(F32) * LATTICE_STEP + jitter[1:2, :])
    place_z = own_core_first((sites >> 6).astype(F32) * LATTICE_STEP + jitter[2:3, :])
    lane = lax.broadcasted_iota(jnp.int32, (ROWS, SPHERES), 1)
    line = lax.broadcasted_iota(jnp.int32, (ROWS, SPHERES), 0)
    same = lane == line + own

    def offset(place):
        here = jnp.sum(jnp.where(same, place, 0.0), axis=1, keepdims=True)
        return here - place

    dx, dy, dz = offset(place_x), offset(place_y), offset(place_z)
    distance = jnp.sqrt(jnp.where(same, 1.0, dx * dx + dy * dy + dz * dz))
    phase = WAVENUMBER * distance
    none = same | (line >= OWN)
    radial_cos = jnp.where(none, 0.0, jnp.cos(phase) / phase)
    radial_sin = jnp.where(none, 0.0, jnp.sin(phase) / phase)
    larger = jnp.maximum(jnp.abs(dx), jnp.abs(dy))
    apart = larger > 0.0
    inverse = 1.0 / jnp.where(apart, larger, 1.0)
    ax, ay = dx * inverse, dy * inverse
    length = jnp.sqrt(jnp.where(apart, ax * ax + ay * ay, 1.0))
    cos_one = jnp.where(apart, ax / length, 1.0)
    sin_one = jnp.where(apart, ay / length, 0.0)

    def put(block, factor):
        value = jnp.concatenate([radial_cos * factor, radial_sin * factor], axis=0)
        pairs[block * BLOCK : (block + 1) * BLOCK, :] = value.astype(BF)

    pairs[0:BLOCK, :] = jnp.concatenate([radial_cos, radial_sin], axis=0).astype(BF)
    cos_k, sin_k = cos_one, sin_one
    for k in range(1, TOP + 1):
        put(k, cos_k)
        put(TOP + k, sin_k)
        if k < TOP:
            cos_k, sin_k = (
                cos_k * cos_one - sin_k * sin_one,
                sin_k * cos_one + cos_k * sin_one,
            )

    probes_out[...] = padded(probes[...], 0)
    turned = padded(rotation[...], 0)
    for radial in range(2):
        tables[radial] = fine_dot(0.5 * dot(turned, axial[radial]), turned, dot_t, 2).astype(BF)
    line = lax.broadcasted_iota(jnp.int32, (GROUPS, PROBES_OWN), 0)
    seen_out[...] = jnp.where(line == probe_group[...], 1.0, 0.0)
    tmat_rows = jnp.concatenate([tmat[...], jnp.zeros((2, WIDE - HALF), F32)], axis=1)
    tmat_out[...] = jnp.concatenate([tmat_rows, jnp.zeros((ROWS - 2, WIDE), F32)], axis=0)
    orders_out[...] = jnp.broadcast_to(orders[...], (ROWS, WIDE))
    base_out[...] = own_rows(incident)
    line = lax.broadcasted_iota(jnp.int32, (ROWS, LANES), 0)
    column = jnp.zeros((ROWS, LANES), F32)
    for r in range(OWN):
        column = jnp.where(line == r, radius[r], column)
    radius_out[...] = column


def load_rows(lines):
    parts = [lines[pl.ds(part, SPHERES // 2, stride=4), :].astype(BF) for part in range(4)]
    return jnp.concatenate(parts, axis=1)


def half_sums(lines):
    groups = []
    for place in range(2):
        parts = []
        for part in range(4):
            value = lines[pl.ds(place * PER_GROUP * 4 + part, PER_GROUP, stride=4), :]
            parts.append(jnp.sum(value, axis=0, keepdims=True))
        groups.append(jnp.concatenate(parts, axis=1))
    return jnp.concatenate(groups, axis=0)


def all_groups(mine, other):
    core = lax.axis_index("co")
    first, second = jnp.where(core == 0, mine, other), jnp.where(core == 0, other, mine)
    return jnp.concatenate([first[0:1], second[0:1], first[1:2], second[1:2]], axis=0)


def order_body(near_in, pairs, near_out):
    del near_in, pairs, near_out


def first_near_body(near, pairs, sums_out, totals_out):
    sums_out[...] = dot(pairs[:, : SPHERES // 2], load_rows(near))
    totals_out[...] = half_sums(near)


def second_near_body(near, pairs, probes, seen, sums_out, gradient_out):
    sums_out[...] = dot(pairs[:, : SPHERES // 2], load_rows(near))
    gradient_out[...] = half_gradient(near, probes, seen, lax.axis_index("co"))


def half_gradient(lines, probes, seen, core):
    totals = half_sums(lines)
    lane = lax.broadcasted_iota(jnp.int32, totals.shape, 1)
    totals = jnp.where((lane & (WIDE - 1)) < HALF, totals, 0.0)
    first, second = seen[0:2, :], seen[2:4, :]
    mask = jnp.concatenate(
        [jnp.where(core == 0, part[0:1], part[1:2]) for part in (first, second)], axis=0
    )
    return gradient_of(totals, probes, mask)


def by_order(values, bits):
    for bit, mask in zip((16, 8, 4, 2, 1), bits):
        count = TOP + bit
        values = [
            jnp.where(mask, values[j + bit], values[j]) if j + bit < len(values) else values[j]
            for j in range(count)
        ]
    return values


def mix(sums, shifted, tables, orders, dot=dot):
    zeros = jnp.zeros((ROWS, LANES), F32)
    for half in range(2):
        code = orders[:, half * LANES : (half + 1) * LANES] + ORDER
        bits = [(code & bit) != 0 for bit in (16, 8, 4, 2, 1)]
        real = slice(half * LANES, (half + 1) * LANES)
        imag = slice(WIDE + half * LANES, WIDE + (half + 1) * LANES)
        for radial in range(2):

            def load(block, columns):
                at = block * BLOCK + radial * ROWS
                return sums[at : at + ROWS, columns]

            for is_imag, columns, others in ((0, real, imag), (1, imag, real)):
                plus, minus = [load(0, columns)], []
                for k in range(1, TOP + 1):
                    cos_sum, sin_sum = load(k, columns), load(TOP + k, others)
                    plus.append(cos_sum + sin_sum if is_imag else cos_sum - sin_sum)
                    minus.append(cos_sum - sin_sum if is_imag else cos_sum + sin_sum)
                chosen = by_order(minus[::-1] + plus, bits)
                cos_part, sin_part = [], []
                for m in range(ORDER + 1):
                    ahead, behind = chosen[ORDER - m], chosen[ORDER + m]
                    cos_part.append(ahead + behind)
                    sin_part.append(behind - ahead if is_imag else ahead - behind)
                cos_part.append(zeros)
                for m in range(0, ORDER + 1, 2):
                    value = jnp.concatenate(cos_part[m : m + 2], axis=0)
                    shifted[radial, m * ROWS : (m + 2) * ROWS, columns] = value.astype(BF)
                for m in range(1, ORDER + 1, 2):
                    value = jnp.concatenate(sin_part[m : m + 2], axis=0)
                    at = SIN_ROWS + (m - 1) * ROWS
                    shifted[radial, at : at + 2 * ROWS, others] = value.astype(BF)

    back = dot(shifted[0], tables[0]) + dot(shifted[1], tables[1])
    parts_re, parts_im = [], []
    for half in range(2):
        real = slice(half * LANES, (half + 1) * LANES)
        imag = slice(WIDE + half * LANES, WIDE + (half + 1) * LANES)
        order = orders[:, real]
        size = jnp.abs(order)
        sign = jnp.where(order > 0, 1.0, -1.0)
        field_re, field_im = back[0:ROWS, real], back[0:ROWS, imag]
        for m in range(1, ORDER + 1):
            cos_lines = slice(m * ROWS, (m + 1) * ROWS)
            sin_lines = slice(SIN_ROWS + (m - 1) * ROWS, SIN_ROWS + m * ROWS)
            field_re = jnp.where(size == m, back[cos_lines, real] + sign * back[sin_lines, imag], field_re)
            field_im = jnp.where(size == m, back[cos_lines, imag] - sign * back[sin_lines, real], field_im)
        parts_re.append(field_re)
        parts_im.append(field_im)
    return jnp.concatenate(parts_re + parts_im, axis=1)


def scatter(field, tmat, radius):
    real, imag = tmat[0:1, :], tmat[1:2, :]
    field_re, field_im = field[:, :WIDE], field[:, WIDE:]
    wide = jnp.concatenate([radius, radius], axis=1)
    return jnp.concatenate(
        [
            wide * (imag * field_im - real * field_re),
            -wide * (imag * field_re + real * field_im),
        ],
        axis=1,
    )


def first_body(
    near_sums, near_totals, peer, pairs, tables, tmat, radius, orders, probes, seen,
    chunk, rows_out, sums, shifted, lines,
):
    sums[...] = near_sums[...] + dot(pairs[:, SPHERES // 2 :], load_rows(peer))
    gradient = gradient_of(all_groups(near_totals[...], half_sums(peer)), probes, seen[...])
    field = mix(sums, shifted, tables, orders)
    image = scatter(field, tmat, radius[...])
    rows_out[...] = image
    lane = lax.broadcasted_iota(jnp.int32, (ROWS, FULL), 1)
    marked = jnp.where(lane == PAD + own_group(), jnp.concatenate([radius[...]] * 4, axis=1), image)
    write_chunks(marked, chunk, lines)
    for piece in range(2):
        line = SLICE_LINES[piece]
        chunk[pl.ds(line, FAR, stride=CHUNK), :] = lines[line : line + 1, :] + slices(gradient, piece)


def piece_mask(piece):
    lane = lax.broadcasted_iota(jnp.int32, (FAR, FULL), 1)
    far = lax.broadcasted_iota(jnp.int32, (FAR, FULL), 0)
    return (lane >> 4) == ((far & (FAR // GROUPS - 1)) * 2 + piece)


def slices(gradient, piece):
    rows = [jnp.broadcast_to(gradient[g : g + 1, :], (FAR // GROUPS, FULL)) for g in range(GROUPS)]
    rows = jnp.where(piece_mask(piece), jnp.concatenate(rows, axis=0), 0.0)
    lane = lax.broadcasted_iota(jnp.int32, (FULL, LANES), 1)
    source = lax.broadcasted_iota(jnp.int32, (FULL, LANES), 0)
    fold = jnp.where(lane - (LANES - 16) == (source & 15), 1.0, 0.0).astype(BF)
    return fine_dot(rows, fold, parts=2)


def unslice(parts):
    lane = lax.broadcasted_iota(jnp.int32, (LANES, FULL), 1)
    source = lax.broadcasted_iota(jnp.int32, (LANES, FULL), 0)
    spread = jnp.where(source - (LANES - 16) == (lane & 15), 1.0, 0.0).astype(BF)
    both = fine_dot(jnp.concatenate(parts, axis=0), spread, parts=2)
    total = jnp.where(piece_mask(0), both[:FAR], jnp.where(piece_mask(1), both[FAR:], 0.0))
    each = FAR // GROUPS
    return jnp.concatenate(
        [jnp.sum(total[g * each : (g + 1) * each], axis=0, keepdims=True) for g in range(GROUPS)], axis=0
    )


def gradient_of(totals, probes, seen):
    values = fine_dot(totals, probes[...], parts=2) * seen
    return fine_dot(values, probes[...], dot_t, 2)


def to_lines(rows):
    return jnp.concatenate([rows[:, part * LANES : (part + 1) * LANES] for part in range(4)], axis=0)


def from_lines(lines):
    each = lines.shape[0] // 4
    return jnp.concatenate([lines[part * each : (part + 1) * each, :] for part in range(4)], axis=1)


def second_gradient_body(peer, probes, seen, send):
    send[...] = to_lines(half_gradient(peer, probes, seen, 1 - lax.axis_index("co")))


def second_body(
    near, near_sums, near_gradient, peer, pairs, tables, tmat, radius, orders, base, image,
    extra, weights_out, sums, shifted,
):
    sums[...] = near_sums[...] + dot(pairs[:, SPHERES // 2 :], load_rows(peer))
    for block in range(BLOCKS):
        k = block if block <= TOP else block - TOP
        at = pl.ds(block * BLOCK, BLOCK)
        value = sums[at, LANES:WIDE]
        weights_out[at, :] = (value if k % 2 == 0 else -value).astype(BF)
    field = mix(sums, shifted, tables, orders)
    last = scatter(field, tmat, radius[...])
    zero, one = base[...], image[...]
    line = lax.broadcasted_iota(jnp.int32, (SHARE, LANES), 0)
    lane = lax.broadcasted_iota(jnp.int32, (SHARE, LANES), 1)
    pairs_of = ((zero, zero), (zero, one), (one, one), (zero, last), (one, last), (last, last))
    sums_of = []
    for a, b in pairs_of:
        product = a * b
        parts = [product[:, part * LANES : (part + 1) * LANES] for part in range(4)]
        sums_of.append(jnp.sum((parts[0] + parts[1]) + (parts[2] + parts[3]), axis=0, keepdims=True))
    stacked = jnp.concatenate(sums_of + [jnp.zeros((SHARE - 6, LANES), F32)], axis=0)
    column = jnp.sum(stacked, axis=1, keepdims=True)
    row = jnp.sum(jnp.where(lane - (PAD - LANES) == line, column, 0.0), axis=0, keepdims=True)
    out = jnp.where(line == SCALAR_LINE, row, 0.0)
    for piece in range(2):
        value = jnp.sum(near[pl.ds(SLICE_LINES[piece], FAR, stride=CHUNK), :], axis=0, keepdims=True)
        out = jnp.where((line == PIECE_LINES[piece]) & (lane >= LANES - 16), value, out)
    extra[...] = out + to_lines(near_gradient[...])


def sum_body(near, out):
    total = near[pl.ds(0, SHARE), :]
    for far in range(1, FAR):
        total = total + near[pl.ds(far * SHARE, SHARE), :]
    out[:SHARE, :] = total
    pieces = [near[pl.ds(PIECE_LINES[piece], FAR, stride=SHARE), :] for piece in range(2)]
    out[SHARE:SCALARS, :] = to_lines(unslice(pieces))
    line = total[SCALAR_LINE : SCALAR_LINE + 1, :]
    for index in range(6):
        at = PAD - LANES + index
        out[SCALARS + index : SCALARS + index + 1, :] = jnp.broadcast_to(line[:, at : at + 1], (1, LANES))


def finish_body(
    near, peer, weights, tables, tmat, orders, incident, image,
    solution_out, sensitivity_out, arnoldi_out, places, sums, shifted,
):
    g00, g01, g11, g02, g12, g22 = [near[at : at + 1, :] + peer[at : at + 1, :] for at in range(SCALARS, SCALARS + 6)]
    scale = 1.0 / g00
    g01, g11, g02, g12, g22 = g01 * scale, g11 * scale, g02 * scale, g12 * scale, g22 * scale
    core = lax.axis_index("co")
    first = from_lines(near[SHARE:SCALARS, :] + peer[SHARE:SCALARS, :])
    mine, other = from_lines(near[:SHARE, :]), from_lines(peer[:SHARE, :])
    even, odd = jnp.where(core == 0, mine, other), jnp.where(core == 0, other, mine)
    second = jnp.concatenate([even[0:1], odd[0:1], even[1:2], odd[1:2]], axis=0)
    diag_first = 1.0 + g01
    below_sq = g11 - g01 * g01
    inverse = 1.0 / below_sq
    upper = g02 - g01 * g01
    shift = g12 - g01 * (g11 + g02 - g01 * g01)
    norm_sq = g22 - g01 * (2.0 * g12 - g01 * g11)
    cross = diag_first * upper + below_sq + shift
    gram_first = diag_first * diag_first + below_sq
    gram_second = (below_sq + 2.0 * shift + norm_sq) * inverse
    cross_scaled = cross * inverse
    determinant = gram_first * gram_second - cross * cross_scaled
    for_image = (upper - diag_first * (1.0 + shift * inverse)) / determinant
    for_base = (diag_first * gram_second - upper * cross_scaled) / determinant - for_image * g01
    below_first = jnp.sqrt(below_sq)
    shift_second = shift * inverse
    diag_second = 1.0 + shift_second
    rest_second = (norm_sq - upper * upper) * inverse - shift_second * shift_second
    arnoldi_out[0] = diag_first[0, 0]
    arnoldi_out[1] = below_first[0, 0]
    arnoldi_out[2] = diag_second[0, 0]
    arnoldi_out[3] = rest_second[0, 0]

    for_base, for_image = [jnp.concatenate([part] * 4, axis=1) for part in (for_base, for_image)]
    factor = COEFF * GROUPS / PROBES / SCALE / float(np.sqrt(np.float32(PER_GROUP)))
    gradient = (for_base * first + for_image * second) * factor
    real, imag = tmat[0:1, :], tmat[1:2, :]
    grad_re, grad_im = gradient[:, :WIDE], gradient[:, WIDE:]
    places[...] = jnp.zeros((LANES, FULL), F32)
    at = pl.ds(PAD - LANES, GROUPS)
    places[at, :WIDE] = real * grad_re + imag * grad_im
    places[at, WIDE:] = real * grad_im - imag * grad_re
    sums[...] = dot(weights[...], places[...].astype(BF))
    field = mix(sums, shifted, tables, orders, dot_t)
    group = own_group()
    own = jnp.zeros((1, FULL), F32)
    for g in range(GROUPS):
        own = jnp.where(group == g, gradient[g : g + 1, :], own)
    lane = lax.broadcasted_iota(jnp.int32, (1, FULL), 1)
    own = jnp.where((lane & (WIDE - 1)) < HALF, own, 0.0)
    image_rows = unpadded(image[...])
    solution_out[...] = for_base[:, :COEFF] * incident[...] + (for_image[:, :COEFF] / SCALE) * image_rows
    sensitivity_out[...] = unpadded(own - field)


def unpadded(rows):
    return jnp.concatenate([rows[:OWN, :HALF], rows[:OWN, WIDE : WIDE + HALF]], axis=1)


def call(body, outs, scratch=(), operands=(), spaces=None, out_spaces=None, cost=None, aliases=None):
    spaces, out_spaces = spaces or {}, out_spaces or {}
    return pl.pallas_call(
        body,
        out_shape=[jax.ShapeDtypeStruct(shape, kind) for shape, kind in outs],
        in_specs=[pl.BlockSpec(memory_space=spaces.get(i, pltpu.VMEM)) for i in range(len(operands))],
        out_specs=[pl.BlockSpec(memory_space=out_spaces.get(i, pltpu.VMEM)) for i in range(len(outs))],
        scratch_shapes=list(scratch),
        compiler_params=pltpu.CompilerParams(vmem_limit_bytes=16 * 1024 * 1024),
        cost_estimate=cost,
        input_output_aliases=aliases or {},
    )(*operands)


def swap_cores(array):
    return lax.ppermute(array, "co", [(0, 1), (1, 0)])


def spread_far(lines):
    parts = lines.reshape(FAR, lines.shape[0] // FAR, LANES)
    return lax.all_to_all(parts, FAR_AXES, 0, 0).reshape(lines.shape)


def on_device(
    incident,
    sphere_site,
    jitter,
    rotation_table,
    axial_tables,
    tmatrix,
    radius_factor,
    probe_field,
    probe_group,
):
    line_scratch = pltpu.VMEM((4 * ROWS, LANES), F32)
    sum_scratch = pltpu.VMEM((BLOCKS * BLOCK, FULL), F32)
    shift_scratch = pltpu.VMEM((2, (ORDER + 1) * BLOCK, FULL), BF)
    rows_shape = ((ROWS, FULL), F32)
    chunk_shape = ((FAR * CHUNK, LANES), F32)
    share_shape = ((SHARE, LANES), F32)
    half_cost = pl.CostEstimate(flops=8_000_000_000, bytes_accessed=4_000_000, transcendentals=0)

    (chunk,) = call(send_body, [chunk_shape], [line_scratch], (incident,))

    def by_core(array):
        lead = array.shape[:-1]
        return jnp.swapaxes(array.reshape(lead + (2, 2, PER_GROUP)), -3, -2).reshape(lead + (SPHERES,))

    pairs, tables, probes, seen, tmat, orders, base, radius = call(
        prepare_body,
        [
            ((BLOCKS * BLOCK, SPHERES), BF),
            ((2, FULL, FULL), BF),
            ((FULL, PROBES_OWN), BF),
            ((GROUPS, PROBES_OWN), F32),
            ((ROWS, WIDE), F32),
            ((ROWS, WIDE), jnp.int32),
            rows_shape,
            ((ROWS, LANES), F32),
        ],
        operands=(
            by_core(sphere_site[None, :]),
            by_core(jitter),
            rotation_table,
            axial_tables,
            probe_field.T,
            probe_group.reshape(1, PROBES_OWN),
            tmatrix,
            jnp.asarray(_ORDERS),
            incident,
            radius_factor,
        ),
        spaces={9: pltpu.SMEM},
        cost=pl.CostEstimate(flops=8_000_000_000, bytes_accessed=8_000_000, transcendentals=20_000),
    )

    near = spread_far(chunk)
    (near,) = call(order_body, [chunk_shape], operands=(near, pairs), spaces={1: pl.ANY}, aliases={0: 0})
    sums_shape = ((BLOCKS * BLOCK, FULL), F32)
    near_sums, near_totals = call(
        first_near_body,
        [sums_shape, ((2, FULL), F32)],
        operands=(near, pairs),
        cost=half_cost,
    )
    chunk, image = call(
        first_body,
        [chunk_shape, rows_shape],
        [sum_scratch, shift_scratch, line_scratch],
        (near_sums, near_totals, swap_cores(near), pairs, tables, tmat, radius, orders, probes, seen),
    )

    near = spread_far(chunk)
    peer = swap_cores(near)
    near_sums, near_gradient = call(
        second_near_body,
        [sums_shape, ((2, FULL), F32)],
        operands=(near, pairs, probes, seen),
        cost=half_cost,
    )
    (send,) = call(second_gradient_body, [share_shape], operands=(peer, probes, seen))
    received = swap_cores(send)
    extra, weights = call(
        second_body,
        [share_shape, ((BLOCKS * BLOCK, LANES), BF)],
        [sum_scratch, shift_scratch],
        (near, near_sums, near_gradient, peer, pairs, tables, tmat, radius, orders, base, image),
        cost=half_cost,
    )
    share = received + extra
    near = spread_far(jnp.broadcast_to(share[None], (FAR, SHARE, LANES)).reshape(FAR * SHARE, LANES))
    (near,) = call(sum_body, [((SCALARS + 8, LANES), F32)], operands=(near,))
    peer = swap_cores(near)
    solution_rows, sensitivity_rows, arnoldi = call(
        finish_body,
        [((OWN, COEFF), F32), ((OWN, COEFF), F32), ((4,), F32)],
        [pltpu.VMEM((LANES, FULL), F32), sum_scratch, shift_scratch],
        (near, peer, weights, tables, tmat, orders, incident, image),
        out_spaces={2: pltpu.SMEM},
    )
    return solution_rows, sensitivity_rows, arnoldi


def solution(mesh):
    fine = Mesh(mesh.devices.reshape(2, 2, 4, 2, 4), ALL_AXES)
    split_rows = P(ALL_AXES)
    return jax.shard_map(
        on_device,
        mesh=fine,
        in_specs=(
            P(ALL_AXES, None),
            P(),
            P(),
            P(),
            P(),
            P(),
            split_rows,
            P(ALL_AXES, None),
            split_rows,
        ),
        out_specs=(P(ALL_AXES, None), P(ALL_AXES, None), P()),
        check_vma=False,
    )
```

```python
import jax
import jax.numpy as jnp
import numpy as np
from jax import lax
from jax.experimental import pallas as pl
from jax.experimental.pallas import tpu as pltpu
from jax.sharding import Mesh
from jax.sharding import PartitionSpec as P

ORDER = 10
WAVENUMBER = 1.3
LATTICE_STEP = 2.5

SPHERES = 768
COEFF = 480
HALF = 240
GROUPS = 4
PER_GROUP = SPHERES // GROUPS
PROBES = 32768
OWN = 6
PROBES_OWN = 256
LANES = 128
WIDE = 256
FULL = 2 * WIDE
ROWS = 8
BLOCK = 2 * ROWS
BLOCKS = 4 * ORDER + 1
TOP = 2 * ORDER
CHUNK = OWN * FULL // LANES
FAR = 64
SCALE = 2.0**-14
PAD = HALF
SIN_ROWS = (ORDER + 2) * ROWS
SHARE = 2 * FULL // LANES
SCALAR_LINE = 2
SCALARS = SHARE + 4 * GROUPS
PIECE_LINES = (6, 7)
SLICE_LINES = (3, 7)
BF = jnp.bfloat16
F32 = jnp.float32

FAR_AXES = ("xl", "z", "xh", "y")
ALL_AXES = ("xl", "co", "z", "xh", "y")


def order_table(degree_max):
    entries = np.arange(degree_max * (degree_max + 2))
    degree = np.floor(np.sqrt(entries + 1.0) + 1e-09)
    orders = entries + 1 - degree * degree - degree
    return np.concatenate([orders, orders]).astype(np.int32)


_ORDERS = np.zeros((1, WIDE), np.int32)
_ORDERS[0, :HALF] = order_table(ORDER)


def dot(a, b):
    return jnp.dot(a, b, preferred_element_type=F32)


def dot_t(a, b):
    return lax.dot_general(a, b, (((1,), (1,)), ((), ())), preferred_element_type=F32)


def fine_dot(x, y, dot=dot, parts=3):
    rows = x.shape[0]
    padded = -(-rows // 16) * 16
    if padded > rows:
        x = jnp.concatenate([x, jnp.zeros((padded - rows, x.shape[1]), F32)], axis=0)
    terms = []
    for _ in range(parts):
        terms.append(x.astype(BF))
        x = x - terms[-1].astype(F32)
    product = dot(jnp.concatenate(terms, axis=0), y)
    total = product[:rows]
    for part in range(1, parts):
        total = total + product[part * padded : part * padded + rows]
    return total


def padded(x, axis):
    zeros = jnp.zeros((x.shape[0], WIDE - HALF) if axis else (WIDE - HALF, x.shape[1]), x.dtype)
    low, high = (x[:, :HALF], x[:, HALF:]) if axis else (x[:HALF, :], x[HALF:, :])
    return jnp.concatenate([low, zeros, high, zeros], axis=axis)


def own_rows(incident):
    value = jnp.concatenate([incident[...], jnp.zeros((ROWS - OWN, COEFF), F32)], axis=0) * SCALE
    return padded(value, 1)


def own_group():
    return lax.axis_index("xl") * 2 + lax.axis_index("co")


def send_body(incident, chunk, lines):
    write_chunks(own_rows(incident), chunk, lines)


def write_chunks(rows, chunk, lines):
    for part in range(4):
        lines[pl.ds(part, ROWS, stride=4), :] = rows[:, part * LANES : (part + 1) * LANES]
    once = lines[:CHUNK, :]
    for far in range(FAR):
        chunk[far * CHUNK : (far + 1) * CHUNK, :] = once


def prepare_body(
    site, jitter, rotation, axial, probes, probe_group, tmat, orders, incident, radius,
    pairs, tables, probes_out, seen_out, tmat_out, orders_out, base_out, radius_out,
):
    own = (
        lax.axis_index("xl") * PER_GROUP
        + ((lax.axis_index("z") * 2 + lax.axis_index("xh")) * 4 + lax.axis_index("y")) * OWN
    )
    sites = site[...]
    core = lax.axis_index("co")

    def own_core_first(place):
        other = jnp.concatenate([place[:, SPHERES // 2 :], place[:, : SPHERES // 2]], axis=1)
        return jnp.where(core == 0, place, other)

    place_x = own_core_first((sites & 7).astype(F32) * LATTICE_STEP + jitter[0:1, :])
    place_y = own_core_first(((sites >> 3) & 7).astype(F32) * LATTICE_STEP + jitter[1:2, :])
    place_z = own_core_first((sites >> 6).astype(F32) * LATTICE_STEP + jitter[2:3, :])
    lane = lax.broadcasted_iota(jnp.int32, (ROWS, SPHERES), 1)
    line = lax.broadcasted_iota(jnp.int32, (ROWS, SPHERES), 0)
    same = lane == line + own

    def offset(place):
        here = jnp.sum(jnp.where(same, place, 0.0), axis=1, keepdims=True)
        return here - place

    dx, dy, dz = offset(place_x), offset(place_y), offset(place_z)
    distance = jnp.sqrt(jnp.where(same, 1.0, dx * dx + dy * dy + dz * dz))
    phase = WAVENUMBER * distance
    none = same | (line >= OWN)
    radial_cos = jnp.where(none, 0.0, jnp.cos(phase) / phase)
    radial_sin = jnp.where(none, 0.0, jnp.sin(phase) / phase)
    larger = jnp.maximum(jnp.abs(dx), jnp.abs(dy))
    apart = larger > 0.0
    inverse = 1.0 / jnp.where(apart, larger, 1.0)
    ax, ay = dx * inverse, dy * inverse
    length = jnp.sqrt(jnp.where(apart, ax * ax + ay * ay, 1.0))
    cos_one = jnp.where(apart, ax / length, 1.0)
    sin_one = jnp.where(apart, ay / length, 0.0)

    def put(block, factor):
        value = jnp.concatenate([radial_cos * factor, radial_sin * factor], axis=0)
        pairs[block * BLOCK : (block + 1) * BLOCK, :] = value.astype(BF)

    pairs[0:BLOCK, :] = jnp.concatenate([radial_cos, radial_sin], axis=0).astype(BF)
    cos_k, sin_k = cos_one, sin_one
    for k in range(1, TOP + 1):
        put(k, cos_k)
        put(TOP + k, sin_k)
        if k < TOP:
            cos_k, sin_k = (
                cos_k * cos_one - sin_k * sin_one,
                sin_k * cos_one + cos_k * sin_one,
            )

    probes_out[...] = padded(probes[...], 0)
    turned = padded(rotation[...], 0)
    for radial in range(2):
        tables[radial] = fine_dot(0.5 * dot(turned, axial[radial]), turned, dot_t, 2).astype(BF)
    line = lax.broadcasted_iota(jnp.int32, (GROUPS, PROBES_OWN), 0)
    seen_out[...] = jnp.where(line == probe_group[...], 1.0, 0.0)
    tmat_rows = jnp.concatenate([tmat[...], jnp.zeros((2, WIDE - HALF), F32)], axis=1)
    tmat_out[...] = jnp.concatenate([tmat_rows, jnp.zeros((ROWS - 2, WIDE), F32)], axis=0)
    orders_out[...] = jnp.broadcast_to(orders[...], (ROWS, WIDE))
    base_out[...] = own_rows(incident)
    line = lax.broadcasted_iota(jnp.int32, (ROWS, LANES), 0)
    column = jnp.zeros((ROWS, LANES), F32)
    for r in range(OWN):
        column = jnp.where(line == r, radius[r], column)
    radius_out[...] = column


def load_rows(lines):
    parts = [lines[pl.ds(part, SPHERES // 2, stride=4), :].astype(BF) for part in range(4)]
    return jnp.concatenate(parts, axis=1)


def half_sums(lines):
    groups = []
    for place in range(2):
        parts = []
        for part in range(4):
            value = lines[pl.ds(place * PER_GROUP * 4 + part, PER_GROUP, stride=4), :]
            parts.append(jnp.sum(value, axis=0, keepdims=True))
        groups.append(jnp.concatenate(parts, axis=1))
    return jnp.concatenate(groups, axis=0)


def all_groups(mine, other):
    core = lax.axis_index("co")
    first, second = jnp.where(core == 0, mine, other), jnp.where(core == 0, other, mine)
    return jnp.concatenate([first[0:1], second[0:1], first[1:2], second[1:2]], axis=0)


def order_body(near_in, pairs, near_out):
    del near_in, pairs, near_out


def first_near_body(near, pairs, sums_out, totals_out):
    sums_out[...] = dot(pairs[:, : SPHERES // 2], load_rows(near))
    totals_out[...] = half_sums(near)


def second_near_body(near, pairs, probes, seen, sums_out, gradient_out):
    sums_out[...] = dot(pairs[:, : SPHERES // 2], load_rows(near))
    gradient_out[...] = half_gradient(near, probes, seen, lax.axis_index("co"))


def half_gradient(lines, probes, seen, core):
    totals = half_sums(lines)
    lane = lax.broadcasted_iota(jnp.int32, totals.shape, 1)
    totals = jnp.where((lane & (WIDE - 1)) < HALF, totals, 0.0)
    first, second = seen[0:2, :], seen[2:4, :]
    mask = jnp.concatenate(
        [jnp.where(core == 0, part[0:1], part[1:2]) for part in (first, second)], axis=0
    )
    return gradient_of(totals, probes, mask)


def by_order(values, bits):
    for bit, mask in zip((16, 8, 4, 2, 1), bits):
        count = TOP + bit
        values = [
            jnp.where(mask, values[j + bit], values[j]) if j + bit < len(values) else values[j]
            for j in range(count)
        ]
    return values


def mix(sums, shifted, tables, orders, dot=dot):
    zeros = jnp.zeros((ROWS, LANES), F32)
    for half in range(2):
        code = orders[:, half * LANES : (half + 1) * LANES] + ORDER
        bits = [(code & bit) != 0 for bit in (16, 8, 4, 2, 1)]
        real = slice(half * LANES, (half + 1) * LANES)
        imag = slice(WIDE + half * LANES, WIDE + (half + 1) * LANES)
        for radial in range(2):

            def load(block, columns):
                at = block * BLOCK + radial * ROWS
                return sums[at : at + ROWS, columns]

            for is_imag, columns, others in ((0, real, imag), (1, imag, real)):
                plus, minus = [load(0, columns)], []
                for k in range(1, TOP + 1):
                    cos_sum, sin_sum = load(k, columns), load(TOP + k, others)
                    plus.append(cos_sum + sin_sum if is_imag else cos_sum - sin_sum)
                    minus.append(cos_sum - sin_sum if is_imag else cos_sum + sin_sum)
                chosen = by_order(minus[::-1] + plus, bits)
                cos_part, sin_part = [], []
                for m in range(ORDER + 1):
                    ahead, behind = chosen[ORDER - m], chosen[ORDER + m]
                    cos_part.append(ahead + behind)
                    sin_part.append(behind - ahead if is_imag else ahead - behind)
                cos_part.append(zeros)
                for m in range(0, ORDER + 1, 2):
                    value = jnp.concatenate(cos_part[m : m + 2], axis=0)
                    shifted[radial, m * ROWS : (m + 2) * ROWS, columns] = value.astype(BF)
                for m in range(1, ORDER + 1, 2):
                    value = jnp.concatenate(sin_part[m : m + 2], axis=0)
                    at = SIN_ROWS + (m - 1) * ROWS
                    shifted[radial, at : at + 2 * ROWS, others] = value.astype(BF)

    back = dot(shifted[0], tables[0]) + dot(shifted[1], tables[1])
    parts_re, parts_im = [], []
    for half in range(2):
        real = slice(half * LANES, (half + 1) * LANES)
        imag = slice(WIDE + half * LANES, WIDE + (half + 1) * LANES)
        order = orders[:, real]
        size = jnp.abs(order)
        sign = jnp.where(order > 0, 1.0, -1.0)
        field_re, field_im = back[0:ROWS, real], back[0:ROWS, imag]
        for m in range(1, ORDER + 1):
            cos_lines = slice(m * ROWS, (m + 1) * ROWS)
            sin_lines = slice(SIN_ROWS + (m - 1) * ROWS, SIN_ROWS + m * ROWS)
            field_re = jnp.where(size == m, back[cos_lines, real] + sign * back[sin_lines, imag], field_re)
            field_im = jnp.where(size == m, back[cos_lines, imag] - sign * back[sin_lines, real], field_im)
        parts_re.append(field_re)
        parts_im.append(field_im)
    return jnp.concatenate(parts_re + parts_im, axis=1)


def scatter(field, tmat, radius):
    real, imag = tmat[0:1, :], tmat[1:2, :]
    field_re, field_im = field[:, :WIDE], field[:, WIDE:]
    wide = jnp.concatenate([radius, radius], axis=1)
    return jnp.concatenate(
        [
            wide * (imag * field_im - real * field_re),
            -wide * (imag * field_re + real * field_im),
        ],
        axis=1,
    )


def first_body(
    near_sums, near_totals, peer, pairs, tables, tmat, radius, orders, probes, seen,
    chunk, rows_out, sums, shifted, lines,
):
    sums[...] = near_sums[...] + dot(pairs[:, SPHERES // 2 :], load_rows(peer))
    gradient = gradient_of(all_groups(near_totals[...], half_sums(peer)), probes, seen[...])
    field = mix(sums, shifted, tables, orders)
    image = scatter(field, tmat, radius[...])
    rows_out[...] = image
    lane = lax.broadcasted_iota(jnp.int32, (ROWS, FULL), 1)
    marked = jnp.where(lane == PAD + own_group(), jnp.concatenate([radius[...]] * 4, axis=1), image)
    write_chunks(marked, chunk, lines)
    for piece in range(2):
        line = SLICE_LINES[piece]
        chunk[pl.ds(line, FAR, stride=CHUNK), :] = lines[line : line + 1, :] + slices(gradient, piece)


def piece_mask(piece):
    lane = lax.broadcasted_iota(jnp.int32, (FAR, FULL), 1)
    far = lax.broadcasted_iota(jnp.int32, (FAR, FULL), 0)
    return (lane >> 4) == ((far & (FAR // GROUPS - 1)) * 2 + piece)


def slices(gradient, piece):
    rows = [jnp.broadcast_to(gradient[g : g + 1, :], (FAR // GROUPS, FULL)) for g in range(GROUPS)]
    rows = jnp.where(piece_mask(piece), jnp.concatenate(rows, axis=0), 0.0)
    lane = lax.broadcasted_iota(jnp.int32, (FULL, LANES), 1)
    source = lax.broadcasted_iota(jnp.int32, (FULL, LANES), 0)
    fold = jnp.where(lane - (LANES - 16) == (source & 15), 1.0, 0.0).astype(BF)
    return fine_dot(rows, fold, parts=2)


def unslice(parts):
    lane = lax.broadcasted_iota(jnp.int32, (LANES, FULL), 1)
    source = lax.broadcasted_iota(jnp.int32, (LANES, FULL), 0)
    spread = jnp.where(source - (LANES - 16) == (lane & 15), 1.0, 0.0).astype(BF)
    both = fine_dot(jnp.concatenate(parts, axis=0), spread, parts=2)
    total = jnp.where(piece_mask(0), both[:FAR], jnp.where(piece_mask(1), both[FAR:], 0.0))
    each = FAR // GROUPS
    return jnp.concatenate(
        [jnp.sum(total[g * each : (g + 1) * each], axis=0, keepdims=True) for g in range(GROUPS)], axis=0
    )


def gradient_of(totals, probes, seen):
    values = fine_dot(totals, probes[...], parts=2) * seen
    return fine_dot(values, probes[...], dot_t, 2)


def to_lines(rows):
    return jnp.concatenate([rows[:, part * LANES : (part + 1) * LANES] for part in range(4)], axis=0)


def from_lines(lines):
    each = lines.shape[0] // 4
    return jnp.concatenate([lines[part * each : (part + 1) * each, :] for part in range(4)], axis=1)


def second_gradient_body(peer, probes, seen, send):
    send[...] = to_lines(half_gradient(peer, probes, seen, 1 - lax.axis_index("co")))


def second_body(
    near, near_sums, near_gradient, peer, pairs, tables, tmat, radius, orders, base, image,
    extra, weights_out, sums, shifted,
):
    sums[...] = near_sums[...] + dot(pairs[:, SPHERES // 2 :], load_rows(peer))
    for block in range(BLOCKS):
        k = block if block <= TOP else block - TOP
        at = pl.ds(block * BLOCK, BLOCK)
        value = sums[at, LANES:WIDE]
        weights_out[at, :] = (value if k % 2 == 0 else -value).astype(BF)
    field = mix(sums, shifted, tables, orders)
    last = scatter(field, tmat, radius[...])
    zero, one = base[...], image[...]
    line = lax.broadcasted_iota(jnp.int32, (SHARE, LANES), 0)
    lane = lax.broadcasted_iota(jnp.int32, (SHARE, LANES), 1)
    pairs_of = ((zero, zero), (zero, one), (one, one), (zero, last), (one, last), (last, last))
    sums_of = []
    for a, b in pairs_of:
        product = a * b
        parts = [product[:, part * LANES : (part + 1) * LANES] for part in range(4)]
        sums_of.append(jnp.sum((parts[0] + parts[1]) + (parts[2] + parts[3]), axis=0, keepdims=True))
    stacked = jnp.concatenate(sums_of + [jnp.zeros((SHARE - 6, LANES), F32)], axis=0)
    column = jnp.sum(stacked, axis=1, keepdims=True)
    row = jnp.sum(jnp.where(lane - (PAD - LANES) == line, column, 0.0), axis=0, keepdims=True)
    out = jnp.where(line == SCALAR_LINE, row, 0.0)
    for piece in range(2):
        value = jnp.sum(near[pl.ds(SLICE_LINES[piece], FAR, stride=CHUNK), :], axis=0, keepdims=True)
        out = jnp.where((line == PIECE_LINES[piece]) & (lane >= LANES - 16), value, out)
    extra[...] = out + to_lines(near_gradient[...])


def sum_body(near, out):
    total = near[pl.ds(0, SHARE), :]
    for far in range(1, FAR):
        total = total + near[pl.ds(far * SHARE, SHARE), :]
    out[:SHARE, :] = total
    pieces = [near[pl.ds(PIECE_LINES[piece], FAR, stride=SHARE), :] for piece in range(2)]
    out[SHARE:SCALARS, :] = to_lines(unslice(pieces))
    line = total[SCALAR_LINE : SCALAR_LINE + 1, :]
    for index in range(6):
        at = PAD - LANES + index
        out[SCALARS + index : SCALARS + index + 1, :] = jnp.broadcast_to(line[:, at : at + 1], (1, LANES))


def finish_body(
    near, peer, weights, tables, tmat, orders, incident, image,
    solution_out, sensitivity_out, arnoldi_out, places, sums, shifted,
):
    g00, g01, g11, g02, g12, g22 = [near[at : at + 1, :] + peer[at : at + 1, :] for at in range(SCALARS, SCALARS + 6)]
    scale = 1.0 / g00
    g01, g11, g02, g12, g22 = g01 * scale, g11 * scale, g02 * scale, g12 * scale, g22 * scale
    core = lax.axis_index("co")
    first = from_lines(near[SHARE:SCALARS, :] + peer[SHARE:SCALARS, :])
    mine, other = from_lines(near[:SHARE, :]), from_lines(peer[:SHARE, :])
    even, odd = jnp.where(core == 0, mine, other), jnp.where(core == 0, other, mine)
    second = jnp.concatenate([even[0:1], odd[0:1], even[1:2], odd[1:2]], axis=0)
    diag_first = 1.0 + g01
    below_sq = g11 - g01 * g01
    full = below_sq > 0.0
    below_sq = jnp.where(full, below_sq, 0.0)
    inverse = 1.0 / jnp.where(full, below_sq, 1.0)
    upper = g02 - g01 * g01
    shift = g12 - g01 * (g11 + g02 - g01 * g01)
    norm_sq = g22 - g01 * (2.0 * g12 - g01 * g11)
    cross = diag_first * upper + below_sq + shift
    gram_first = diag_first * diag_first + below_sq
    gram_second = (below_sq + 2.0 * shift + norm_sq) * inverse
    cross_scaled = cross * inverse
    determinant = jnp.where(full, gram_first * gram_second - cross * cross_scaled, 1.0)
    for_image = (upper - diag_first * (1.0 + shift * inverse)) / determinant
    for_base = (diag_first * gram_second - upper * cross_scaled) / determinant - for_image * g01
    for_image = jnp.where(full, for_image, 0.0)
    for_base = jnp.where(full, for_base, diag_first / gram_first)
    below_first = jnp.sqrt(below_sq)
    shift_second = shift * inverse
    diag_second = 1.0 + shift_second
    rest_second = (norm_sq - upper * upper) * inverse - shift_second * shift_second
    arnoldi_out[0] = diag_first[0, 0]
    arnoldi_out[1] = below_first[0, 0]
    arnoldi_out[2] = diag_second[0, 0]
    arnoldi_out[3] = rest_second[0, 0]

    for_base, for_image = [jnp.concatenate([part] * 4, axis=1) for part in (for_base, for_image)]
    factor = COEFF * GROUPS / PROBES / SCALE / float(np.sqrt(np.float32(PER_GROUP)))
    gradient = (for_base * first + for_image * second) * factor
    real, imag = tmat[0:1, :], tmat[1:2, :]
    grad_re, grad_im = gradient[:, :WIDE], gradient[:, WIDE:]
    places[...] = jnp.zeros((LANES, FULL), F32)
    at = pl.ds(PAD - LANES, GROUPS)
    places[at, :WIDE] = real * grad_re + imag * grad_im
    places[at, WIDE:] = real * grad_im - imag * grad_re
    sums[...] = dot(weights[...], places[...].astype(BF))
    field = mix(sums, shifted, tables, orders, dot_t)
    group = own_group()
    own = jnp.zeros((1, FULL), F32)
    for g in range(GROUPS):
        own = jnp.where(group == g, gradient[g : g + 1, :], own)
    lane = lax.broadcasted_iota(jnp.int32, (1, FULL), 1)
    own = jnp.where((lane & (WIDE - 1)) < HALF, own, 0.0)
    image_rows = unpadded(image[...])
    solution_out[...] = for_base[:, :COEFF] * incident[...] + (for_image[:, :COEFF] / SCALE) * image_rows
    sensitivity_out[...] = unpadded(own - field)


def unpadded(rows):
    return jnp.concatenate([rows[:OWN, :HALF], rows[:OWN, WIDE : WIDE + HALF]], axis=1)


def call(body, outs, scratch=(), operands=(), spaces=None, out_spaces=None, cost=None, aliases=None):
    spaces, out_spaces = spaces or {}, out_spaces or {}
    return pl.pallas_call(
        body,
        out_shape=[jax.ShapeDtypeStruct(shape, kind) for shape, kind in outs],
        in_specs=[pl.BlockSpec(memory_space=spaces.get(i, pltpu.VMEM)) for i in range(len(operands))],
        out_specs=[pl.BlockSpec(memory_space=out_spaces.get(i, pltpu.VMEM)) for i in range(len(outs))],
        scratch_shapes=list(scratch),
        compiler_params=pltpu.CompilerParams(vmem_limit_bytes=8 * 1024 * 1024),
        cost_estimate=cost,
        input_output_aliases=aliases or {},
    )(*operands)


def swap_cores(array):
    return lax.ppermute(array, "co", [(0, 1), (1, 0)])


def spread_far(lines):
    parts = lines.reshape(FAR, lines.shape[0] // FAR, LANES)
    return lax.all_to_all(parts, FAR_AXES, 0, 0).reshape(lines.shape)


def on_device(
    incident,
    sphere_site,
    jitter,
    rotation_table,
    axial_tables,
    tmatrix,
    radius_factor,
    probe_field,
    probe_group,
):
    line_scratch = pltpu.VMEM((4 * ROWS, LANES), F32)
    sum_scratch = pltpu.VMEM((BLOCKS * BLOCK, FULL), F32)
    shift_scratch = pltpu.VMEM((2, (ORDER + 1) * BLOCK, FULL), BF)
    rows_shape = ((ROWS, FULL), F32)
    chunk_shape = ((FAR * CHUNK, LANES), F32)
    share_shape = ((SHARE, LANES), F32)
    half_cost = pl.CostEstimate(flops=8_000_000_000, bytes_accessed=4_000_000, transcendentals=0)

    (chunk,) = call(send_body, [chunk_shape], [line_scratch], (incident,))

    def by_core(array):
        lead = array.shape[:-1]
        return jnp.swapaxes(array.reshape(lead + (2, 2, PER_GROUP)), -3, -2).reshape(lead + (SPHERES,))

    pairs, tables, probes, seen, tmat, orders, base, radius = call(
        prepare_body,
        [
            ((BLOCKS * BLOCK, SPHERES), BF),
            ((2, FULL, FULL), BF),
            ((FULL, PROBES_OWN), BF),
            ((GROUPS, PROBES_OWN), F32),
            ((ROWS, WIDE), F32),
            ((ROWS, WIDE), jnp.int32),
            rows_shape,
            ((ROWS, LANES), F32),
        ],
        operands=(
            by_core(sphere_site[None, :]),
            by_core(jitter),
            rotation_table,
            axial_tables,
            probe_field.T,
            probe_group.reshape(1, PROBES_OWN),
            tmatrix,
            jnp.asarray(_ORDERS),
            incident,
            radius_factor,
        ),
        spaces={9: pltpu.SMEM},
        cost=pl.CostEstimate(flops=8_000_000_000, bytes_accessed=8_000_000, transcendentals=20_000),
    )

    near = spread_far(chunk)
    (near,) = call(order_body, [chunk_shape], operands=(near, pairs), spaces={1: pl.ANY}, aliases={0: 0})
    sums_shape = ((BLOCKS * BLOCK, FULL), F32)
    near_sums, near_totals = call(
        first_near_body,
        [sums_shape, ((2, FULL), F32)],
        operands=(near, pairs),
        cost=half_cost,
    )
    chunk, image = call(
        first_body,
        [chunk_shape, rows_shape],
        [sum_scratch, shift_scratch, line_scratch],
        (near_sums, near_totals, swap_cores(near), pairs, tables, tmat, radius, orders, probes, seen),
    )

    near = spread_far(chunk)
    peer = swap_cores(near)
    near_sums, near_gradient = call(
        second_near_body,
        [sums_shape, ((2, FULL), F32)],
        operands=(near, pairs, probes, seen),
        cost=half_cost,
    )
    (send,) = call(second_gradient_body, [share_shape], operands=(peer, probes, seen))
    received = swap_cores(send)
    extra, weights = call(
        second_body,
        [share_shape, ((BLOCKS * BLOCK, LANES), BF)],
        [sum_scratch, shift_scratch],
        (near, near_sums, near_gradient, peer, pairs, tables, tmat, radius, orders, base, image),
        cost=half_cost,
    )
    share = received + extra
    near = spread_far(jnp.broadcast_to(share[None], (FAR, SHARE, LANES)).reshape(FAR * SHARE, LANES))
    (near,) = call(sum_body, [((SCALARS + 8, LANES), F32)], operands=(near,))
    peer = swap_cores(near)
    solution_rows, sensitivity_rows, arnoldi = call(
        finish_body,
        [((OWN, COEFF), F32), ((OWN, COEFF), F32), ((4,), F32)],
        [pltpu.VMEM((LANES, FULL), F32), sum_scratch, shift_scratch],
        (near, peer, weights, tables, tmat, orders, incident, image),
        out_spaces={2: pltpu.SMEM},
    )
    return solution_rows, sensitivity_rows, arnoldi


def solution(mesh):
    fine = Mesh(mesh.devices.reshape(2, 2, 4, 2, 4), ALL_AXES)
    split_rows = P(ALL_AXES)
    return jax.shard_map(
        on_device,
        mesh=fine,
        in_specs=(
            P(ALL_AXES, None),
            P(),
            P(),
            P(),
            P(),
            P(),
            split_rows,
            P(ALL_AXES, None),
            split_rows,
        ),
        out_specs=(P(ALL_AXES, None), P(ALL_AXES, None), P()),
        check_vma=False,
    )
```

```python
import jax
import jax.numpy as jnp
import numpy as np
from jax import lax
from jax.experimental import pallas as pl
from jax.experimental.pallas import tpu as pltpu
from jax.sharding import Mesh
from jax.sharding import PartitionSpec as P

ORDER = 10
WAVENUMBER = 1.3
LATTICE_STEP = 2.5

SPHERES = 768
HALF_SPHERES = SPHERES // 2
COEFF = 480
HALF = 240
GROUPS = 4
PER_GROUP = SPHERES // GROUPS
PROBES = 32768
OWN = 6
PROBES_OWN = 256
LANES = 128
WIDE = 256
FULL = 2 * WIDE
ROWS = 8
BLOCK = 2 * ROWS
BLOCKS = 4 * ORDER + 1
TOP = 2 * ORDER
CHUNK = OWN * FULL // LANES
FAR = 64
SCALE = 2.0**-14
PAD = HALF
SIN_ROWS = (ORDER + 2) * ROWS
SHARE = 2 * FULL // LANES
SCALAR_LINE = 2
SCALARS = SHARE + 4 * GROUPS
PIECE_LINES = (6, 7)
SLICE_LINES = (3, 7)
BF = jnp.bfloat16
F32 = jnp.float32

FAR_AXES = ("xl", "z", "xh", "y")
ALL_AXES = ("xl", "co", "z", "xh", "y")


def order_table(degree_max):
    entries = np.arange(degree_max * (degree_max + 2))
    degree = np.floor(np.sqrt(entries + 1.0) + 1e-09)
    orders = entries + 1 - degree * degree - degree
    return np.concatenate([orders, orders]).astype(np.int32)


_ORDERS = np.zeros((1, WIDE), np.int32)
_ORDERS[0, :HALF] = order_table(ORDER)


def dot(a, b):
    return jnp.dot(a, b, preferred_element_type=F32)


def dot_t(a, b):
    return lax.dot_general(a, b, (((1,), (1,)), ((), ())), preferred_element_type=F32)


def fine_dot(x, y, dot=dot, parts=3):
    rows = x.shape[0]
    padded = -(-rows // 16) * 16
    if padded > rows:
        x = jnp.concatenate([x, jnp.zeros((padded - rows, x.shape[1]), F32)], axis=0)
    terms = []
    for _ in range(parts):
        terms.append(x.astype(BF))
        x = x - terms[-1].astype(F32)
    product = dot(jnp.concatenate(terms, axis=0), y)
    total = product[:rows]
    for part in range(1, parts):
        total = total + product[part * padded : part * padded + rows]
    return total


def padded(x, axis):
    zeros = jnp.zeros((x.shape[0], WIDE - HALF) if axis else (WIDE - HALF, x.shape[1]), x.dtype)
    low, high = (x[:, :HALF], x[:, HALF:]) if axis else (x[:HALF, :], x[HALF:, :])
    return jnp.concatenate([low, zeros, high, zeros], axis=axis)


def own_rows(incident):
    value = jnp.concatenate([incident[...], jnp.zeros((ROWS - OWN, COEFF), F32)], axis=0) * SCALE
    return padded(value, 1)


def own_group():
    return lax.axis_index("xl") * 2 + lax.axis_index("co")


def send_body(incident, chunk, lines):
    write_chunks(own_rows(incident), chunk, lines)


def write_chunks(rows, chunk, lines):
    for part in range(4):
        lines[pl.ds(part, ROWS, stride=4), :] = rows[:, part * LANES : (part + 1) * LANES]
    once = lines[:CHUNK, :]
    for far in range(FAR):
        chunk[far * CHUNK : (far + 1) * CHUNK, :] = once


def prepare_body(
    site, jitter, rotation, axial, probes, probe_group, tmat, orders, incident, radius,
    pairs, tables, probes_out, seen_out, tmat_out, orders_out, base_out, radius_out,
):
    own = (
        lax.axis_index("xl") * PER_GROUP
        + ((lax.axis_index("z") * 2 + lax.axis_index("xh")) * 4 + lax.axis_index("y")) * OWN
    )
    sites = site[...]
    core = lax.axis_index("co")

    def own_core_first(place):
        other = jnp.concatenate([place[:, HALF_SPHERES :], place[:, : HALF_SPHERES]], axis=1)
        return jnp.where(core == 0, place, other)

    place_x = own_core_first((sites & 7).astype(F32) * LATTICE_STEP + jitter[0:1, :])
    place_y = own_core_first(((sites >> 3) & 7).astype(F32) * LATTICE_STEP + jitter[1:2, :])
    place_z = own_core_first((sites >> 6).astype(F32) * LATTICE_STEP + jitter[2:3, :])
    lane = lax.broadcasted_iota(jnp.int32, (ROWS, SPHERES), 1)
    line = lax.broadcasted_iota(jnp.int32, (ROWS, SPHERES), 0)
    same = lane == line + own
    same_peer = lane == line + own + HALF_SPHERES

    def offset(place):
        here = jnp.sum(jnp.where(same, place, 0.0), axis=1, keepdims=True)
        peer = jnp.sum(jnp.where(same_peer, place, 0.0), axis=1, keepdims=True)
        return jnp.concatenate([here - place, peer - place[:, :HALF_SPHERES]], axis=1)

    dx, dy, dz = offset(place_x), offset(place_y), offset(place_z)
    line = lax.broadcasted_iota(jnp.int32, dx.shape, 0)
    same = lax.broadcasted_iota(jnp.int32, dx.shape, 1) == line + own
    distance = jnp.sqrt(jnp.where(same, 1.0, dx * dx + dy * dy + dz * dz))
    phase = WAVENUMBER * distance
    none = same | (line >= OWN)
    radial_cos = jnp.where(none, 0.0, jnp.cos(phase) / phase)
    radial_sin = jnp.where(none, 0.0, jnp.sin(phase) / phase)
    larger = jnp.maximum(jnp.abs(dx), jnp.abs(dy))
    apart = larger > 0.0
    inverse = 1.0 / jnp.where(apart, larger, 1.0)
    ax, ay = dx * inverse, dy * inverse
    length = jnp.sqrt(jnp.where(apart, ax * ax + ay * ay, 1.0))
    cos_one = jnp.where(apart, ax / length, 1.0)
    sin_one = jnp.where(apart, ay / length, 0.0)

    def put(block, factor):
        value = jnp.concatenate([radial_cos * factor, radial_sin * factor], axis=0)
        pairs[block * BLOCK : (block + 1) * BLOCK, :] = value.astype(BF)

    pairs[0:BLOCK, :] = jnp.concatenate([radial_cos, radial_sin], axis=0).astype(BF)
    cos_k, sin_k = cos_one, sin_one
    for k in range(1, TOP + 1):
        put(k, cos_k)
        put(TOP + k, sin_k)
        if k < TOP:
            cos_k, sin_k = (
                cos_k * cos_one - sin_k * sin_one,
                sin_k * cos_one + cos_k * sin_one,
            )

    probes_out[...] = padded(probes[...], 0)
    turned = padded(rotation[...], 0)
    for radial in range(2):
        tables[radial] = fine_dot(0.5 * dot(turned, axial[radial]), turned, dot_t, 2).astype(BF)
    line = lax.broadcasted_iota(jnp.int32, (GROUPS, PROBES_OWN), 0)
    seen_out[...] = jnp.where(line == probe_group[...], 1.0, 0.0)
    tmat_rows = jnp.concatenate([tmat[...], jnp.zeros((2, WIDE - HALF), F32)], axis=1)
    tmat_out[...] = jnp.concatenate([tmat_rows, jnp.zeros((ROWS - 2, WIDE), F32)], axis=0)
    orders_out[...] = jnp.broadcast_to(orders[...], (ROWS, WIDE))
    base_out[...] = own_rows(incident)
    line = lax.broadcasted_iota(jnp.int32, (ROWS, LANES), 0)
    column = jnp.zeros((ROWS, LANES), F32)
    for r in range(OWN):
        column = jnp.where(line == r, radius[r], column)
    radius_out[...] = column


def load_rows(lines):
    parts = [lines[pl.ds(part, HALF_SPHERES, stride=4), :].astype(BF) for part in range(4)]
    return jnp.concatenate(parts, axis=1)


def half_sums(lines):
    groups = []
    for place in range(2):
        parts = []
        for part in range(4):
            value = lines[pl.ds(place * PER_GROUP * 4 + part, PER_GROUP, stride=4), :]
            parts.append(jnp.sum(value, axis=0, keepdims=True))
        groups.append(jnp.concatenate(parts, axis=1))
    return jnp.concatenate(groups, axis=0)


def all_groups(mine, other):
    core = lax.axis_index("co")
    first, second = jnp.where(core == 0, mine, other), jnp.where(core == 0, other, mine)
    return jnp.concatenate([first[0:1], second[0:1], first[1:2], second[1:2]], axis=0)


def order_body(near_in, pairs, tables, near_out):
    del near_in, pairs, tables, near_out


def own_field(near, pairs, tables, orders, sums, shifted):
    sums[...] = dot(pairs[:, :HALF_SPHERES], load_rows(near))
    return mix(sums, shifted, tables, orders)


def peer_field(near, pairs, tables, orders, sums, shifted):
    sums[...] = dot(pairs[:, SPHERES:], load_rows(near))
    return mix(sums, shifted, tables, orders)


def first_peer_body(near, pairs, tables, orders, field_out, sums, shifted):
    field = peer_field(near, pairs, tables, orders, sums, shifted)
    field_out[...] = jnp.concatenate([field[:OWN], half_sums(near)], axis=0)


def first_own_body(near, pairs, tables, orders, probes, seen, field_out, gradient_out, sums, shifted):
    field_out[...] = own_field(near, pairs, tables, orders, sums, shifted)
    gradient_out[...] = half_gradient(half_sums(near), probes, seen, lax.axis_index("co"))


def second_near_body(near, pairs, probes, seen, sums_out, gradient_out):
    sums_out[...] = dot(pairs[:, :HALF_SPHERES], load_rows(near))
    gradient_out[...] = half_gradient(half_sums(near), probes, seen, lax.axis_index("co"))


def half_gradient(totals, probes, seen, core):
    lane = lax.broadcasted_iota(jnp.int32, totals.shape, 1)
    totals = jnp.where((lane & (WIDE - 1)) < HALF, totals, 0.0)
    first, second = seen[0:2, :], seen[2:4, :]
    mask = jnp.concatenate(
        [jnp.where(core == 0, part[0:1], part[1:2]) for part in (first, second)], axis=0
    )
    return gradient_of(totals, probes, mask)


def by_order(values, bits):
    for bit, mask in zip((16, 8, 4, 2, 1), bits):
        count = TOP + bit
        values = [
            jnp.where(mask, values[j + bit], values[j]) if j + bit < len(values) else values[j]
            for j in range(count)
        ]
    return values


def mix(sums, shifted, tables, orders, dot=dot):
    zeros = jnp.zeros((ROWS, LANES), F32)
    for half in range(2):
        code = orders[:, half * LANES : (half + 1) * LANES] + ORDER
        bits = [(code & bit) != 0 for bit in (16, 8, 4, 2, 1)]
        real = slice(half * LANES, (half + 1) * LANES)
        imag = slice(WIDE + half * LANES, WIDE + (half + 1) * LANES)
        for radial in range(2):

            def load(block, columns):
                at = block * BLOCK + radial * ROWS
                return sums[at : at + ROWS, columns]

            for is_imag, columns, others in ((0, real, imag), (1, imag, real)):
                plus, minus = [load(0, columns)], []
                for k in range(1, TOP + 1):
                    cos_sum, sin_sum = load(k, columns), load(TOP + k, others)
                    plus.append(cos_sum + sin_sum if is_imag else cos_sum - sin_sum)
                    minus.append(cos_sum - sin_sum if is_imag else cos_sum + sin_sum)
                chosen = by_order(minus[::-1] + plus, bits)
                cos_part, sin_part = [], []
                for m in range(ORDER + 1):
                    ahead, behind = chosen[ORDER - m], chosen[ORDER + m]
                    cos_part.append(ahead + behind)
                    sin_part.append(behind - ahead if is_imag else ahead - behind)
                cos_part.append(zeros)
                for m in range(0, ORDER + 1, 2):
                    value = jnp.concatenate(cos_part[m : m + 2], axis=0)
                    shifted[radial, m * ROWS : (m + 2) * ROWS, columns] = value.astype(BF)
                for m in range(1, ORDER + 1, 2):
                    value = jnp.concatenate(sin_part[m : m + 2], axis=0)
                    at = SIN_ROWS + (m - 1) * ROWS
                    shifted[radial, at : at + 2 * ROWS, others] = value.astype(BF)

    back = dot(shifted[0], tables[0]) + dot(shifted[1], tables[1])
    parts_re, parts_im = [], []
    for half in range(2):
        real = slice(half * LANES, (half + 1) * LANES)
        imag = slice(WIDE + half * LANES, WIDE + (half + 1) * LANES)
        order = orders[:, real]
        size = jnp.abs(order)
        sign = jnp.where(order > 0, 1.0, -1.0)
        field_re, field_im = back[0:ROWS, real], back[0:ROWS, imag]
        for m in range(1, ORDER + 1):
            cos_lines = slice(m * ROWS, (m + 1) * ROWS)
            sin_lines = slice(SIN_ROWS + (m - 1) * ROWS, SIN_ROWS + m * ROWS)
            field_re = jnp.where(size == m, back[cos_lines, real] + sign * back[sin_lines, imag], field_re)
            field_im = jnp.where(size == m, back[cos_lines, imag] - sign * back[sin_lines, real], field_im)
        parts_re.append(field_re)
        parts_im.append(field_im)
    return jnp.concatenate(parts_re + parts_im, axis=1)


def scatter(field, tmat, radius):
    real, imag = tmat[0:1, :], tmat[1:2, :]
    field_re, field_im = field[:, :WIDE], field[:, WIDE:]
    wide = jnp.concatenate([radius, radius], axis=1)
    return jnp.concatenate(
        [
            wide * (imag * field_im - real * field_re),
            -wide * (imag * field_re + real * field_im),
        ],
        axis=1,
    )


def first_body(
    field, received, near_gradient, tmat, radius, probes, seen,
    chunk, rows_out, lines,
):
    peer_gradient = half_gradient(received[OWN:, :], probes, seen, 1 - lax.axis_index("co"))
    gradient = all_groups(near_gradient[...], peer_gradient)
    image = scatter(field[...] + received[...], tmat, radius[...])
    rows_out[...] = image
    lane = lax.broadcasted_iota(jnp.int32, (ROWS, FULL), 1)
    marked = jnp.where(lane == PAD + own_group(), jnp.concatenate([radius[...]] * 4, axis=1), image)
    write_chunks(marked, chunk, lines)
    for piece in range(2):
        line = SLICE_LINES[piece]
        chunk[pl.ds(line, FAR, stride=CHUNK), :] = lines[line : line + 1, :] + slices(gradient, piece)


def piece_mask(piece):
    lane = lax.broadcasted_iota(jnp.int32, (FAR, FULL), 1)
    far = lax.broadcasted_iota(jnp.int32, (FAR, FULL), 0)
    return (lane >> 4) == ((far & (FAR // GROUPS - 1)) * 2 + piece)


def slices(gradient, piece):
    rows = [jnp.broadcast_to(gradient[g : g + 1, :], (FAR // GROUPS, FULL)) for g in range(GROUPS)]
    rows = jnp.where(piece_mask(piece), jnp.concatenate(rows, axis=0), 0.0)
    lane = lax.broadcasted_iota(jnp.int32, (FULL, LANES), 1)
    source = lax.broadcasted_iota(jnp.int32, (FULL, LANES), 0)
    fold = jnp.where(lane - (LANES - 16) == (source & 15), 1.0, 0.0).astype(BF)
    return fine_dot(rows, fold, parts=2)


def unslice(parts):
    lane = lax.broadcasted_iota(jnp.int32, (LANES, FULL), 1)
    source = lax.broadcasted_iota(jnp.int32, (LANES, FULL), 0)
    spread = jnp.where(source - (LANES - 16) == (lane & 15), 1.0, 0.0).astype(BF)
    both = fine_dot(jnp.concatenate(parts, axis=0), spread, parts=2)
    total = jnp.where(piece_mask(0), both[:FAR], jnp.where(piece_mask(1), both[FAR:], 0.0))
    each = FAR // GROUPS
    return jnp.concatenate(
        [jnp.sum(total[g * each : (g + 1) * each], axis=0, keepdims=True) for g in range(GROUPS)], axis=0
    )


def gradient_of(totals, probes, seen):
    values = fine_dot(totals, probes[...], parts=2) * seen
    return fine_dot(values, probes[...], dot_t, 2)


def to_lines(rows):
    return jnp.concatenate([rows[:, part * LANES : (part + 1) * LANES] for part in range(4)], axis=0)


def from_lines(lines):
    each = lines.shape[0] // 4
    return jnp.concatenate([lines[part * each : (part + 1) * each, :] for part in range(4)], axis=1)


def second_gradient_body(peer, probes, seen, send):
    send[...] = to_lines(half_gradient(half_sums(peer), probes, seen, 1 - lax.axis_index("co")))


def second_body(
    near, near_sums, near_gradient, peer, pairs, tables, tmat, radius, orders, base, image,
    extra, weights_out, sums, shifted,
):
    sums[...] = near_sums[...] + dot(pairs[:, HALF_SPHERES:SPHERES], load_rows(peer))
    for block in range(BLOCKS):
        k = block if block <= TOP else block - TOP
        at = pl.ds(block * BLOCK, BLOCK)
        value = sums[at, LANES:WIDE]
        weights_out[at, :] = (value if k % 2 == 0 else -value).astype(BF)
    field = mix(sums, shifted, tables, orders)
    last = scatter(field, tmat, radius[...])
    zero, one = base[...], image[...]
    line = lax.broadcasted_iota(jnp.int32, (SHARE, LANES), 0)
    lane = lax.broadcasted_iota(jnp.int32, (SHARE, LANES), 1)
    pairs_of = ((zero, zero), (zero, one), (one, one), (zero, last), (one, last), (last, last))
    sums_of = []
    for a, b in pairs_of:
        product = a * b
        parts = [product[:, part * LANES : (part + 1) * LANES] for part in range(4)]
        sums_of.append(jnp.sum((parts[0] + parts[1]) + (parts[2] + parts[3]), axis=0, keepdims=True))
    stacked = jnp.concatenate(sums_of + [jnp.zeros((SHARE - 6, LANES), F32)], axis=0)
    column = jnp.sum(stacked, axis=1, keepdims=True)
    row = jnp.sum(jnp.where(lane - (PAD - LANES) == line, column, 0.0), axis=0, keepdims=True)
    out = jnp.where(line == SCALAR_LINE, row, 0.0)
    for piece in range(2):
        value = jnp.sum(near[pl.ds(SLICE_LINES[piece], FAR, stride=CHUNK), :], axis=0, keepdims=True)
        out = jnp.where((line == PIECE_LINES[piece]) & (lane >= LANES - 16), value, out)
    extra[...] = out + to_lines(near_gradient[...])


def sum_body(near, out):
    total = near[pl.ds(0, SHARE), :]
    for far in range(1, FAR):
        total = total + near[pl.ds(far * SHARE, SHARE), :]
    out[:SHARE, :] = total
    pieces = [near[pl.ds(PIECE_LINES[piece], FAR, stride=SHARE), :] for piece in range(2)]
    out[SHARE:SCALARS, :] = to_lines(unslice(pieces))
    line = total[SCALAR_LINE : SCALAR_LINE + 1, :]
    for index in range(6):
        at = PAD - LANES + index
        out[SCALARS + index : SCALARS + index + 1, :] = jnp.broadcast_to(line[:, at : at + 1], (1, LANES))


def finish_body(
    near, peer, weights, tables, tmat, orders, incident, image,
    solution_out, sensitivity_out, arnoldi_out, places, sums, shifted,
):
    g00, g01, g11, g02, g12, g22 = [near[at : at + 1, :] + peer[at : at + 1, :] for at in range(SCALARS, SCALARS + 6)]
    scale = 1.0 / g00
    g01, g11, g02, g12, g22 = g01 * scale, g11 * scale, g02 * scale, g12 * scale, g22 * scale
    core = lax.axis_index("co")
    first = from_lines(near[SHARE:SCALARS, :] + peer[SHARE:SCALARS, :])
    mine, other = from_lines(near[:SHARE, :]), from_lines(peer[:SHARE, :])
    even, odd = jnp.where(core == 0, mine, other), jnp.where(core == 0, other, mine)
    second = jnp.concatenate([even[0:1], odd[0:1], even[1:2], odd[1:2]], axis=0)
    diag_first = 1.0 + g01
    below_sq = g11 - g01 * g01
    full = below_sq > 0.0
    below_sq = jnp.where(full, below_sq, 0.0)
    inverse = 1.0 / jnp.where(full, below_sq, 1.0)
    upper = g02 - g01 * g01
    shift = g12 - g01 * (g11 + g02 - g01 * g01)
    norm_sq = g22 - g01 * (2.0 * g12 - g01 * g11)
    cross = diag_first * upper + below_sq + shift
    gram_first = diag_first * diag_first + below_sq
    gram_second = (below_sq + 2.0 * shift + norm_sq) * inverse
    cross_scaled = cross * inverse
    determinant = jnp.where(full, gram_first * gram_second - cross * cross_scaled, 1.0)
    for_image = (upper - diag_first * (1.0 + shift * inverse)) / determinant
    for_base = (diag_first * gram_second - upper * cross_scaled) / determinant - for_image * g01
    for_image = jnp.where(full, for_image, 0.0)
    for_base = jnp.where(full, for_base, diag_first / gram_first)
    below_first = jnp.sqrt(below_sq)
    shift_second = shift * inverse
    diag_second = 1.0 + shift_second
    rest_second = (norm_sq - upper * upper) * inverse - shift_second * shift_second
    arnoldi_out[0] = diag_first[0, 0]
    arnoldi_out[1] = below_first[0, 0]
    arnoldi_out[2] = diag_second[0, 0]
    arnoldi_out[3] = rest_second[0, 0]

    for_base, for_image = [jnp.concatenate([part] * 4, axis=1) for part in (for_base, for_image)]
    factor = COEFF * GROUPS / PROBES / SCALE / float(np.sqrt(np.float32(PER_GROUP)))
    gradient = (for_base * first + for_image * second) * factor
    real, imag = tmat[0:1, :], tmat[1:2, :]
    grad_re, grad_im = gradient[:, :WIDE], gradient[:, WIDE:]
    places[...] = jnp.zeros((LANES, FULL), F32)
    at = pl.ds(PAD - LANES, GROUPS)
    places[at, :WIDE] = real * grad_re + imag * grad_im
    places[at, WIDE:] = real * grad_im - imag * grad_re
    sums[...] = dot(weights[...], places[...].astype(BF))
    field = mix(sums, shifted, tables, orders, dot_t)
    group = own_group()
    own = jnp.zeros((1, FULL), F32)
    for g in range(GROUPS):
        own = jnp.where(group == g, gradient[g : g + 1, :], own)
    lane = lax.broadcasted_iota(jnp.int32, (1, FULL), 1)
    own = jnp.where((lane & (WIDE - 1)) < HALF, own, 0.0)
    image_rows = unpadded(image[...])
    solution_out[...] = for_base[:, :COEFF] * incident[...] + (for_image[:, :COEFF] / SCALE) * image_rows
    sensitivity_out[...] = unpadded(own - field)


def unpadded(rows):
    return jnp.concatenate([rows[:OWN, :HALF], rows[:OWN, WIDE : WIDE + HALF]], axis=1)


def call(body, outs, scratch=(), operands=(), spaces=None, out_spaces=None, cost=None, aliases=None):
    spaces, out_spaces = spaces or {}, out_spaces or {}
    return pl.pallas_call(
        body,
        out_shape=[jax.ShapeDtypeStruct(shape, kind) for shape, kind in outs],
        in_specs=[pl.BlockSpec(memory_space=spaces.get(i, pltpu.VMEM)) for i in range(len(operands))],
        out_specs=[pl.BlockSpec(memory_space=out_spaces.get(i, pltpu.VMEM)) for i in range(len(outs))],
        scratch_shapes=list(scratch),
        compiler_params=pltpu.CompilerParams(vmem_limit_bytes=8 * 1024 * 1024),
        cost_estimate=cost,
        input_output_aliases=aliases or {},
    )(*operands)


def swap_cores(array):
    return lax.ppermute(array, "co", [(0, 1), (1, 0)])


def spread_far(lines):
    parts = lines.reshape(FAR, lines.shape[0] // FAR, LANES)
    return lax.all_to_all(parts, FAR_AXES, 0, 0).reshape(lines.shape)


def on_device(
    incident,
    sphere_site,
    jitter,
    rotation_table,
    axial_tables,
    tmatrix,
    radius_factor,
    probe_field,
    probe_group,
):
    line_scratch = pltpu.VMEM((4 * ROWS, LANES), F32)
    sum_scratch = pltpu.VMEM((BLOCKS * BLOCK, FULL), F32)
    shift_scratch = pltpu.VMEM((2, (ORDER + 1) * BLOCK, FULL), BF)
    rows_shape = ((ROWS, FULL), F32)
    chunk_shape = ((FAR * CHUNK, LANES), F32)
    share_shape = ((SHARE, LANES), F32)
    half_cost = pl.CostEstimate(flops=8_000_000_000, bytes_accessed=4_000_000, transcendentals=0)

    (chunk,) = call(send_body, [chunk_shape], [line_scratch], (incident,))

    def by_core(array):
        lead = array.shape[:-1]
        return jnp.swapaxes(array.reshape(lead + (2, 2, PER_GROUP)), -3, -2).reshape(lead + (SPHERES,))

    pairs, tables, probes, seen, tmat, orders, base, radius = call(
        prepare_body,
        [
            ((BLOCKS * BLOCK, SPHERES + HALF_SPHERES), BF),
            ((2, FULL, FULL), BF),
            ((FULL, PROBES_OWN), BF),
            ((GROUPS, PROBES_OWN), F32),
            ((ROWS, WIDE), F32),
            ((ROWS, WIDE), jnp.int32),
            rows_shape,
            ((ROWS, LANES), F32),
        ],
        operands=(
            by_core(sphere_site[None, :]),
            by_core(jitter),
            rotation_table,
            axial_tables,
            probe_field.T,
            probe_group.reshape(1, PROBES_OWN),
            tmatrix,
            jnp.asarray(_ORDERS),
            incident,
            radius_factor,
        ),
        spaces={9: pltpu.SMEM},
        cost=pl.CostEstimate(flops=8_000_000_000, bytes_accessed=8_000_000, transcendentals=20_000),
    )

    scratch = [sum_scratch, shift_scratch]
    half_shape = ((2, FULL), F32)

    near = spread_far(chunk)
    (near,) = call(
        order_body,
        [chunk_shape],
        operands=(near, pairs, tables),
        spaces={1: pl.ANY, 2: pl.ANY},
        aliases={0: 0},
    )
    (field_peer,) = call(first_peer_body, [rows_shape], scratch, (near, pairs, tables, orders), cost=half_cost)
    field_received = swap_cores(field_peer)
    field, near_gradient = call(
        first_own_body,
        [rows_shape, half_shape],
        scratch,
        (near, pairs, tables, orders, probes, seen),
        cost=half_cost,
    )
    chunk, image = call(
        first_body,
        [chunk_shape, rows_shape],
        [line_scratch],
        (field, field_received, near_gradient, tmat, radius, probes, seen),
    )

    near = spread_far(chunk)
    peer = swap_cores(near)
    near_sums, near_gradient = call(
        second_near_body,
        [((BLOCKS * BLOCK, FULL), F32), half_shape],
        operands=(near, pairs, probes, seen),
        cost=half_cost,
    )
    (send,) = call(second_gradient_body, [share_shape], operands=(peer, probes, seen))
    received = swap_cores(send)
    extra, weights = call(
        second_body,
        [share_shape, ((BLOCKS * BLOCK, LANES), BF)],
        [sum_scratch, shift_scratch],
        (near, near_sums, near_gradient, peer, pairs, tables, tmat, radius, orders, base, image),
        cost=half_cost,
    )
    share = received + extra
    near = spread_far(jnp.broadcast_to(share[None], (FAR, SHARE, LANES)).reshape(FAR * SHARE, LANES))
    (near,) = call(sum_body, [((SCALARS + 8, LANES), F32)], operands=(near,))
    peer = swap_cores(near)
    solution_rows, sensitivity_rows, arnoldi = call(
        finish_body,
        [((OWN, COEFF), F32), ((OWN, COEFF), F32), ((4,), F32)],
        [pltpu.VMEM((LANES, FULL), F32)] + scratch,
        (near, peer, weights, tables, tmat, orders, incident, image),
        out_spaces={2: pltpu.SMEM},
    )
    return solution_rows, sensitivity_rows, arnoldi


def solution(mesh):
    fine = Mesh(mesh.devices.reshape(2, 2, 4, 2, 4), ALL_AXES)
    split_rows = P(ALL_AXES)
    return jax.shard_map(
        on_device,
        mesh=fine,
        in_specs=(
            P(ALL_AXES, None),
            P(),
            P(),
            P(),
            P(),
            P(),
            split_rows,
            P(ALL_AXES, None),
            split_rows,
        ),
        out_specs=(P(ALL_AXES, None), P(ALL_AXES, None), P()),
        check_vma=False,
    )
```

```python
import jax
import jax.numpy as jnp
import numpy as np
from jax import lax
from jax.experimental import pallas as pl
from jax.experimental.pallas import tpu as pltpu
from jax.sharding import Mesh
from jax.sharding import PartitionSpec as P

ORDER = 10
WAVENUMBER = 1.3
LATTICE_STEP = 2.5

SPHERES = 768
COEFF = 480
HALF = 240
GROUPS = 4
PER_GROUP = SPHERES // GROUPS
PROBES = 32768
OWN = 6
PROBES_OWN = 256
LANES = 128
WIDE = 256
FULL = 2 * WIDE
ROWS = 8
BLOCK = 2 * ROWS
BLOCKS = 4 * ORDER + 1
TOP = 2 * ORDER
CHUNK = OWN * FULL // LANES
FAR = 64
SCALE = 2.0**-14
PAD = HALF
SIN_ROWS = (ORDER + 2) * ROWS
SHARE = 2 * FULL // LANES
SCALAR_LINE = 2
SCALARS = SHARE + 4 * GROUPS
PIECE_LINES = (6, 7)
SLICE_LINES = (3, 7)
BF = jnp.bfloat16
F32 = jnp.float32

FAR_AXES = ("xl", "xh", "y", "z")
ALL_AXES = ("xl", "co", "z", "xh", "y")


def order_table(degree_max):
    entries = np.arange(degree_max * (degree_max + 2))
    degree = np.floor(np.sqrt(entries + 1.0) + 1e-09)
    orders = entries + 1 - degree * degree - degree
    return np.concatenate([orders, orders]).astype(np.int32)


_ORDERS = np.zeros((1, WIDE), np.int32)
_ORDERS[0, :HALF] = order_table(ORDER)


def dot(a, b):
    return jnp.dot(a, b, preferred_element_type=F32)


def dot_t(a, b):
    return lax.dot_general(a, b, (((1,), (1,)), ((), ())), preferred_element_type=F32)


def fine_dot(x, y, dot=dot, parts=3):
    rows = x.shape[0]
    padded = -(-rows // 16) * 16
    if padded > rows:
        x = jnp.concatenate([x, jnp.zeros((padded - rows, x.shape[1]), F32)], axis=0)
    terms = []
    for _ in range(parts):
        terms.append(x.astype(BF))
        x = x - terms[-1].astype(F32)
    product = dot(jnp.concatenate(terms, axis=0), y)
    total = product[:rows]
    for part in range(1, parts):
        total = total + product[part * padded : part * padded + rows]
    return total


def padded(x, axis):
    zeros = jnp.zeros((x.shape[0], WIDE - HALF) if axis else (WIDE - HALF, x.shape[1]), x.dtype)
    low, high = (x[:, :HALF], x[:, HALF:]) if axis else (x[:HALF, :], x[HALF:, :])
    return jnp.concatenate([low, zeros, high, zeros], axis=axis)


def own_rows(incident):
    value = jnp.concatenate([incident[...], jnp.zeros((ROWS - OWN, COEFF), F32)], axis=0) * SCALE
    return padded(value, 1)


def own_group():
    return lax.axis_index("xl") * 2 + lax.axis_index("co")


def send_body(incident, chunk, lines):
    write_chunks(own_rows(incident), chunk, lines)


def write_chunks(rows, chunk, lines):
    for part in range(4):
        lines[pl.ds(part, ROWS, stride=4), :] = rows[:, part * LANES : (part + 1) * LANES]
    once = lines[:CHUNK, :]
    for far in range(FAR):
        chunk[far * CHUNK : (far + 1) * CHUNK, :] = once


def prepare_body(
    site, jitter, rotation, axial, probes, probe_group, tmat, orders, incident, radius,
    pairs, tables, probes_out, seen_out, tmat_out, orders_out, base_out, radius_out,
):
    own = (
        lax.axis_index("xl") * PER_GROUP
        + ((lax.axis_index("xh") * 4 + lax.axis_index("y")) * 4 + lax.axis_index("z")) * OWN
    )
    sites = site[...]
    core = lax.axis_index("co")

    def own_core_first(place):
        other = jnp.concatenate([place[:, SPHERES // 2 :], place[:, : SPHERES // 2]], axis=1)
        return jnp.where(core == 0, place, other)

    place_x = own_core_first((sites & 7).astype(F32) * LATTICE_STEP + jitter[0:1, :])
    place_y = own_core_first(((sites >> 3) & 7).astype(F32) * LATTICE_STEP + jitter[1:2, :])
    place_z = own_core_first((sites >> 6).astype(F32) * LATTICE_STEP + jitter[2:3, :])
    lane = lax.broadcasted_iota(jnp.int32, (ROWS, SPHERES), 1)
    line = lax.broadcasted_iota(jnp.int32, (ROWS, SPHERES), 0)
    same = lane == line + own

    def offset(place):
        here = jnp.sum(jnp.where(same, place, 0.0), axis=1, keepdims=True)
        return here - place

    dx, dy, dz = offset(place_x), offset(place_y), offset(place_z)
    distance = jnp.sqrt(jnp.where(same, 1.0, dx * dx + dy * dy + dz * dz))
    phase = WAVENUMBER * distance
    none = same | (line >= OWN)
    radial_cos = jnp.where(none, 0.0, jnp.cos(phase) / phase)
    radial_sin = jnp.where(none, 0.0, jnp.sin(phase) / phase)
    larger = jnp.maximum(jnp.abs(dx), jnp.abs(dy))
    apart = larger > 0.0
    inverse = 1.0 / jnp.where(apart, larger, 1.0)
    ax, ay = dx * inverse, dy * inverse
    length = jnp.sqrt(jnp.where(apart, ax * ax + ay * ay, 1.0))
    cos_one = jnp.where(apart, ax / length, 1.0)
    sin_one = jnp.where(apart, ay / length, 0.0)

    def put(block, factor):
        value = jnp.concatenate([radial_cos * factor, radial_sin * factor], axis=0)
        pairs[block * BLOCK : (block + 1) * BLOCK, :] = value.astype(BF)

    pairs[0:BLOCK, :] = jnp.concatenate([radial_cos, radial_sin], axis=0).astype(BF)
    cos_k, sin_k = cos_one, sin_one
    for k in range(1, TOP + 1):
        put(k, cos_k)
        put(TOP + k, sin_k)
        if k < TOP:
            cos_k, sin_k = (
                cos_k * cos_one - sin_k * sin_one,
                sin_k * cos_one + cos_k * sin_one,
            )

    probes_out[...] = padded(probes[...], 0)
    turned = padded(rotation[...], 0)
    for radial in range(2):
        tables[radial] = fine_dot(0.5 * dot(turned, axial[radial]), turned, dot_t, 2).astype(BF)
    line = lax.broadcasted_iota(jnp.int32, (GROUPS, PROBES_OWN), 0)
    seen_out[...] = jnp.where(line == probe_group[...], 1.0, 0.0)
    tmat_rows = jnp.concatenate([tmat[...], jnp.zeros((2, WIDE - HALF), F32)], axis=1)
    tmat_out[...] = jnp.concatenate([tmat_rows, jnp.zeros((ROWS - 2, WIDE), F32)], axis=0)
    orders_out[...] = jnp.broadcast_to(orders[...], (ROWS, WIDE))
    base_out[...] = own_rows(incident)
    line = lax.broadcasted_iota(jnp.int32, (ROWS, LANES), 0)
    column = jnp.zeros((ROWS, LANES), F32)
    for r in range(OWN):
        column = jnp.where(line == r, radius[r], column)
    radius_out[...] = column


def load_rows(lines):
    parts = [lines[pl.ds(part, SPHERES // 2, stride=4), :].astype(BF) for part in range(4)]
    return jnp.concatenate(parts, axis=1)


def half_sums(lines):
    groups = []
    for place in range(2):
        parts = []
        for part in range(4):
            value = lines[pl.ds(place * PER_GROUP * 4 + part, PER_GROUP, stride=4), :]
            parts.append(jnp.sum(value, axis=0, keepdims=True))
        groups.append(jnp.concatenate(parts, axis=1))
    return jnp.concatenate(groups, axis=0)


def all_groups(mine, other):
    core = lax.axis_index("co")
    first, second = jnp.where(core == 0, mine, other), jnp.where(core == 0, other, mine)
    return jnp.concatenate([first[0:1], second[0:1], first[1:2], second[1:2]], axis=0)


def order_body(near_in, pairs, near_out):
    del near_in, pairs, near_out


def first_near_body(near, pairs, sums_out, totals_out):
    sums_out[...] = dot(pairs[:, : SPHERES // 2], load_rows(near))
    totals_out[...] = half_sums(near)


def second_near_body(near, pairs, probes, seen, sums_out, gradient_out):
    sums_out[...] = dot(pairs[:, : SPHERES // 2], load_rows(near))
    gradient_out[...] = half_gradient(near, probes, seen, lax.axis_index("co"))


def half_gradient(lines, probes, seen, core):
    totals = half_sums(lines)
    lane = lax.broadcasted_iota(jnp.int32, totals.shape, 1)
    totals = jnp.where((lane & (WIDE - 1)) < HALF, totals, 0.0)
    first, second = seen[0:2, :], seen[2:4, :]
    mask = jnp.concatenate(
        [jnp.where(core == 0, part[0:1], part[1:2]) for part in (first, second)], axis=0
    )
    return gradient_of(totals, probes, mask)


def by_order(values, bits):
    for bit, mask in zip((16, 8, 4, 2, 1), bits):
        count = TOP + bit
        values = [
            jnp.where(mask, values[j + bit], values[j]) if j + bit < len(values) else values[j]
            for j in range(count)
        ]
    return values


def mix(sums, shifted, tables, orders, dot=dot):
    zeros = jnp.zeros((ROWS, LANES), F32)
    for half in range(2):
        code = orders[:, half * LANES : (half + 1) * LANES] + ORDER
        bits = [(code & bit) != 0 for bit in (16, 8, 4, 2, 1)]
        real = slice(half * LANES, (half + 1) * LANES)
        imag = slice(WIDE + half * LANES, WIDE + (half + 1) * LANES)
        for radial in range(2):

            def load(block, columns):
                at = block * BLOCK + radial * ROWS
                return sums[at : at + ROWS, columns]

            for is_imag, columns, others in ((0, real, imag), (1, imag, real)):
                plus, minus = [load(0, columns)], []
                for k in range(1, TOP + 1):
                    cos_sum, sin_sum = load(k, columns), load(TOP + k, others)
                    plus.append(cos_sum + sin_sum if is_imag else cos_sum - sin_sum)
                    minus.append(cos_sum - sin_sum if is_imag else cos_sum + sin_sum)
                chosen = by_order(minus[::-1] + plus, bits)
                cos_part, sin_part = [], []
                for m in range(ORDER + 1):
                    ahead, behind = chosen[ORDER - m], chosen[ORDER + m]
                    cos_part.append(ahead + behind)
                    sin_part.append(behind - ahead if is_imag else ahead - behind)
                cos_part.append(zeros)
                for m in range(0, ORDER + 1, 2):
                    value = jnp.concatenate(cos_part[m : m + 2], axis=0)
                    shifted[radial, m * ROWS : (m + 2) * ROWS, columns] = value.astype(BF)
                for m in range(1, ORDER + 1, 2):
                    value = jnp.concatenate(sin_part[m : m + 2], axis=0)
                    at = SIN_ROWS + (m - 1) * ROWS
                    shifted[radial, at : at + 2 * ROWS, others] = value.astype(BF)

    back = dot(shifted[0], tables[0]) + dot(shifted[1], tables[1])
    parts_re, parts_im = [], []
    for half in range(2):
        real = slice(half * LANES, (half + 1) * LANES)
        imag = slice(WIDE + half * LANES, WIDE + (half + 1) * LANES)
        order = orders[:, real]
        size = jnp.abs(order)
        sign = jnp.where(order > 0, 1.0, -1.0)
        field_re, field_im = back[0:ROWS, real], back[0:ROWS, imag]
        for m in range(1, ORDER + 1):
            cos_lines = slice(m * ROWS, (m + 1) * ROWS)
            sin_lines = slice(SIN_ROWS + (m - 1) * ROWS, SIN_ROWS + m * ROWS)
            field_re = jnp.where(size == m, back[cos_lines, real] + sign * back[sin_lines, imag], field_re)
            field_im = jnp.where(size == m, back[cos_lines, imag] - sign * back[sin_lines, real], field_im)
        parts_re.append(field_re)
        parts_im.append(field_im)
    return jnp.concatenate(parts_re + parts_im, axis=1)


def scatter(field, tmat, radius):
    real, imag = tmat[0:1, :], tmat[1:2, :]
    field_re, field_im = field[:, :WIDE], field[:, WIDE:]
    wide = jnp.concatenate([radius, radius], axis=1)
    return jnp.concatenate(
        [
            wide * (imag * field_im - real * field_re),
            -wide * (imag * field_re + real * field_im),
        ],
        axis=1,
    )


def first_body(
    near_sums, near_totals, peer, pairs, tables, tmat, radius, orders, probes, seen,
    chunk, rows_out, sums, shifted, lines,
):
    sums[...] = near_sums[...] + dot(pairs[:, SPHERES // 2 :], load_rows(peer))
    gradient = gradient_of(all_groups(near_totals[...], half_sums(peer)), probes, seen[...])
    field = mix(sums, shifted, tables, orders)
    image = scatter(field, tmat, radius[...])
    rows_out[...] = image
    lane = lax.broadcasted_iota(jnp.int32, (ROWS, FULL), 1)
    marked = jnp.where(lane == PAD + own_group(), jnp.concatenate([radius[...]] * 4, axis=1), image)
    write_chunks(marked, chunk, lines)
    for piece in range(2):
        line = SLICE_LINES[piece]
        chunk[pl.ds(line, FAR, stride=CHUNK), :] = lines[line : line + 1, :] + slices(gradient, piece)


def piece_mask(piece):
    lane = lax.broadcasted_iota(jnp.int32, (FAR, FULL), 1)
    far = lax.broadcasted_iota(jnp.int32, (FAR, FULL), 0)
    return (lane >> 4) == ((far & (FAR // GROUPS - 1)) * 2 + piece)


def slices(gradient, piece):
    rows = [jnp.broadcast_to(gradient[g : g + 1, :], (FAR // GROUPS, FULL)) for g in range(GROUPS)]
    rows = jnp.where(piece_mask(piece), jnp.concatenate(rows, axis=0), 0.0)
    lane = lax.broadcasted_iota(jnp.int32, (FULL, LANES), 1)
    source = lax.broadcasted_iota(jnp.int32, (FULL, LANES), 0)
    fold = jnp.where(lane - (LANES - 16) == (source & 15), 1.0, 0.0).astype(BF)
    return fine_dot(rows, fold, parts=2)


def unslice(parts):
    lane = lax.broadcasted_iota(jnp.int32, (LANES, FULL), 1)
    source = lax.broadcasted_iota(jnp.int32, (LANES, FULL), 0)
    spread = jnp.where(source - (LANES - 16) == (lane & 15), 1.0, 0.0).astype(BF)
    both = fine_dot(jnp.concatenate(parts, axis=0), spread, parts=2)
    total = jnp.where(piece_mask(0), both[:FAR], jnp.where(piece_mask(1), both[FAR:], 0.0))
    each = FAR // GROUPS
    return jnp.concatenate(
        [jnp.sum(total[g * each : (g + 1) * each], axis=0, keepdims=True) for g in range(GROUPS)], axis=0
    )


def gradient_of(totals, probes, seen):
    values = fine_dot(totals, probes[...], parts=2) * seen
    return fine_dot(values, probes[...], dot_t, 2)


def to_lines(rows):
    return jnp.concatenate([rows[:, part * LANES : (part + 1) * LANES] for part in range(4)], axis=0)


def from_lines(lines):
    each = lines.shape[0] // 4
    return jnp.concatenate([lines[part * each : (part + 1) * each, :] for part in range(4)], axis=1)


def second_gradient_body(peer, probes, seen, send):
    send[...] = to_lines(half_gradient(peer, probes, seen, 1 - lax.axis_index("co")))


def second_body(
    near, near_sums, near_gradient, peer, pairs, tables, tmat, radius, orders, base, image,
    extra, weights_out, sums, shifted,
):
    sums[...] = near_sums[...] + dot(pairs[:, SPHERES // 2 :], load_rows(peer))
    for block in range(BLOCKS):
        k = block if block <= TOP else block - TOP
        at = pl.ds(block * BLOCK, BLOCK)
        value = sums[at, LANES:WIDE]
        weights_out[at, :] = (value if k % 2 == 0 else -value).astype(BF)
    field = mix(sums, shifted, tables, orders)
    last = scatter(field, tmat, radius[...])
    zero, one = base[...], image[...]
    line = lax.broadcasted_iota(jnp.int32, (SHARE, LANES), 0)
    lane = lax.broadcasted_iota(jnp.int32, (SHARE, LANES), 1)
    pairs_of = ((zero, zero), (zero, one), (one, one), (zero, last), (one, last), (last, last))
    sums_of = []
    for a, b in pairs_of:
        product = a * b
        parts = [product[:, part * LANES : (part + 1) * LANES] for part in range(4)]
        sums_of.append(jnp.sum((parts[0] + parts[1]) + (parts[2] + parts[3]), axis=0, keepdims=True))
    stacked = jnp.concatenate(sums_of + [jnp.zeros((SHARE - 6, LANES), F32)], axis=0)
    column = jnp.sum(stacked, axis=1, keepdims=True)
    row = jnp.sum(jnp.where(lane - (PAD - LANES) == line, column, 0.0), axis=0, keepdims=True)
    out = jnp.where(line == SCALAR_LINE, row, 0.0)
    for piece in range(2):
        value = jnp.sum(near[pl.ds(SLICE_LINES[piece], FAR, stride=CHUNK), :], axis=0, keepdims=True)
        out = jnp.where((line == PIECE_LINES[piece]) & (lane >= LANES - 16), value, out)
    extra[...] = out + to_lines(near_gradient[...])


def sum_body(near, out):
    total = near[pl.ds(0, SHARE), :]
    for far in range(1, FAR):
        total = total + near[pl.ds(far * SHARE, SHARE), :]
    out[:SHARE, :] = total
    pieces = [near[pl.ds(PIECE_LINES[piece], FAR, stride=SHARE), :] for piece in range(2)]
    out[SHARE:SCALARS, :] = to_lines(unslice(pieces))
    line = total[SCALAR_LINE : SCALAR_LINE + 1, :]
    for index in range(6):
        at = PAD - LANES + index
        out[SCALARS + index : SCALARS + index + 1, :] = jnp.broadcast_to(line[:, at : at + 1], (1, LANES))


def finish_body(
    near, peer, weights, tables, tmat, orders, incident, image,
    solution_out, sensitivity_out, arnoldi_out, places, sums, shifted,
):
    g00, g01, g11, g02, g12, g22 = [near[at : at + 1, :] + peer[at : at + 1, :] for at in range(SCALARS, SCALARS + 6)]
    scale = 1.0 / g00
    g01, g11, g02, g12, g22 = g01 * scale, g11 * scale, g02 * scale, g12 * scale, g22 * scale
    core = lax.axis_index("co")
    first = from_lines(near[SHARE:SCALARS, :] + peer[SHARE:SCALARS, :])
    mine, other = from_lines(near[:SHARE, :]), from_lines(peer[:SHARE, :])
    even, odd = jnp.where(core == 0, mine, other), jnp.where(core == 0, other, mine)
    second = jnp.concatenate([even[0:1], odd[0:1], even[1:2], odd[1:2]], axis=0)
    diag_first = 1.0 + g01
    below_sq = g11 - g01 * g01
    full = below_sq > 0.0
    below_sq = jnp.where(full, below_sq, 0.0)
    inverse = 1.0 / jnp.where(full, below_sq, 1.0)
    upper = g02 - g01 * g01
    shift = g12 - g01 * (g11 + g02 - g01 * g01)
    norm_sq = g22 - g01 * (2.0 * g12 - g01 * g11)
    cross = diag_first * upper + below_sq + shift
    gram_first = diag_first * diag_first + below_sq
    gram_second = (below_sq + 2.0 * shift + norm_sq) * inverse
    cross_scaled = cross * inverse
    determinant = jnp.where(full, gram_first * gram_second - cross * cross_scaled, 1.0)
    for_image = (upper - diag_first * (1.0 + shift * inverse)) / determinant
    for_base = (diag_first * gram_second - upper * cross_scaled) / determinant - for_image * g01
    for_image = jnp.where(full, for_image, 0.0)
    for_base = jnp.where(full, for_base, diag_first / gram_first)
    below_first = jnp.sqrt(below_sq)
    shift_second = shift * inverse
    diag_second = 1.0 + shift_second
    rest_second = (norm_sq - upper * upper) * inverse - shift_second * shift_second
    arnoldi_out[0] = diag_first[0, 0]
    arnoldi_out[1] = below_first[0, 0]
    arnoldi_out[2] = diag_second[0, 0]
    arnoldi_out[3] = rest_second[0, 0]

    for_base, for_image = [jnp.concatenate([part] * 4, axis=1) for part in (for_base, for_image)]
    factor = COEFF * GROUPS / PROBES / SCALE / float(np.sqrt(np.float32(PER_GROUP)))
    gradient = (for_base * first + for_image * second) * factor
    real, imag = tmat[0:1, :], tmat[1:2, :]
    grad_re, grad_im = gradient[:, :WIDE], gradient[:, WIDE:]
    places[...] = jnp.zeros((LANES, FULL), F32)
    at = pl.ds(PAD - LANES, GROUPS)
    places[at, :WIDE] = real * grad_re + imag * grad_im
    places[at, WIDE:] = real * grad_im - imag * grad_re
    sums[...] = dot(weights[...], places[...].astype(BF))
    field = mix(sums, shifted, tables, orders, dot_t)
    group = own_group()
    own = jnp.zeros((1, FULL), F32)
    for g in range(GROUPS):
        own = jnp.where(group == g, gradient[g : g + 1, :], own)
    lane = lax.broadcasted_iota(jnp.int32, (1, FULL), 1)
    own = jnp.where((lane & (WIDE - 1)) < HALF, own, 0.0)
    image_rows = unpadded(image[...])
    solution_out[...] = for_base[:, :COEFF] * incident[...] + (for_image[:, :COEFF] / SCALE) * image_rows
    sensitivity_out[...] = unpadded(own - field)


def unpadded(rows):
    return jnp.concatenate([rows[:OWN, :HALF], rows[:OWN, WIDE : WIDE + HALF]], axis=1)


def call(body, outs, scratch=(), operands=(), spaces=None, out_spaces=None, cost=None, aliases=None):
    spaces, out_spaces = spaces or {}, out_spaces or {}
    return pl.pallas_call(
        body,
        out_shape=[jax.ShapeDtypeStruct(shape, kind) for shape, kind in outs],
        in_specs=[pl.BlockSpec(memory_space=spaces.get(i, pltpu.VMEM)) for i in range(len(operands))],
        out_specs=[pl.BlockSpec(memory_space=out_spaces.get(i, pltpu.VMEM)) for i in range(len(outs))],
        scratch_shapes=list(scratch),
        compiler_params=pltpu.CompilerParams(vmem_limit_bytes=8 * 1024 * 1024),
        cost_estimate=cost,
        input_output_aliases=aliases or {},
    )(*operands)


def swap_cores(array):
    return lax.ppermute(array, "co", [(0, 1), (1, 0)])


def spread_far(lines):
    parts = lines.reshape(FAR, lines.shape[0] // FAR, LANES)
    return lax.all_to_all(parts, FAR_AXES, 0, 0).reshape(lines.shape)


def on_device(
    incident,
    sphere_site,
    jitter,
    rotation_table,
    axial_tables,
    tmatrix,
    radius_factor,
    probe_field,
    probe_group,
):
    line_scratch = pltpu.VMEM((4 * ROWS, LANES), F32)
    sum_scratch = pltpu.VMEM((BLOCKS * BLOCK, FULL), F32)
    shift_scratch = pltpu.VMEM((2, (ORDER + 1) * BLOCK, FULL), BF)
    rows_shape = ((ROWS, FULL), F32)
    chunk_shape = ((FAR * CHUNK, LANES), F32)
    share_shape = ((SHARE, LANES), F32)
    half_cost = pl.CostEstimate(flops=8_000_000_000, bytes_accessed=4_000_000, transcendentals=0)

    (chunk,) = call(send_body, [chunk_shape], [line_scratch], (incident,))

    def by_core(array):
        lead = array.shape[:-1]
        at = len(lead)
        by_device = array.reshape(lead + (2, 2, 4, 2, 4, OWN))
        order = tuple(range(at)) + tuple(at + axis for axis in (1, 0, 3, 4, 2, 5))
        return by_device.transpose(order).reshape(lead + (SPHERES,))

    pairs, tables, probes, seen, tmat, orders, base, radius = call(
        prepare_body,
        [
            ((BLOCKS * BLOCK, SPHERES), BF),
            ((2, FULL, FULL), BF),
            ((FULL, PROBES_OWN), BF),
            ((GROUPS, PROBES_OWN), F32),
            ((ROWS, WIDE), F32),
            ((ROWS, WIDE), jnp.int32),
            rows_shape,
            ((ROWS, LANES), F32),
        ],
        operands=(
            by_core(sphere_site[None, :]),
            by_core(jitter),
            rotation_table,
            axial_tables,
            probe_field.T,
            probe_group.reshape(1, PROBES_OWN),
            tmatrix,
            jnp.asarray(_ORDERS),
            incident,
            radius_factor,
        ),
        spaces={9: pltpu.SMEM},
        cost=pl.CostEstimate(flops=8_000_000_000, bytes_accessed=8_000_000, transcendentals=20_000),
    )

    near = spread_far(chunk)
    (near,) = call(order_body, [chunk_shape], operands=(near, pairs), spaces={1: pl.ANY}, aliases={0: 0})
    sums_shape = ((BLOCKS * BLOCK, FULL), F32)
    near_sums, near_totals = call(
        first_near_body,
        [sums_shape, ((2, FULL), F32)],
        operands=(near, pairs),
        cost=half_cost,
    )
    chunk, image = call(
        first_body,
        [chunk_shape, rows_shape],
        [sum_scratch, shift_scratch, line_scratch],
        (near_sums, near_totals, swap_cores(near), pairs, tables, tmat, radius, orders, probes, seen),
    )

    near = spread_far(chunk)
    peer = swap_cores(near)
    near_sums, near_gradient = call(
        second_near_body,
        [sums_shape, ((2, FULL), F32)],
        operands=(near, pairs, probes, seen),
        cost=half_cost,
    )
    (send,) = call(second_gradient_body, [share_shape], operands=(peer, probes, seen))
    received = swap_cores(send)
    extra, weights = call(
        second_body,
        [share_shape, ((BLOCKS * BLOCK, LANES), BF)],
        [sum_scratch, shift_scratch],
        (near, near_sums, near_gradient, peer, pairs, tables, tmat, radius, orders, base, image),
        cost=half_cost,
    )
    share = received + extra
    near = spread_far(jnp.broadcast_to(share[None], (FAR, SHARE, LANES)).reshape(FAR * SHARE, LANES))
    (near,) = call(sum_body, [((SCALARS + 8, LANES), F32)], operands=(near,))
    peer = swap_cores(near)
    solution_rows, sensitivity_rows, arnoldi = call(
        finish_body,
        [((OWN, COEFF), F32), ((OWN, COEFF), F32), ((4,), F32)],
        [pltpu.VMEM((LANES, FULL), F32), sum_scratch, shift_scratch],
        (near, peer, weights, tables, tmat, orders, incident, image),
        out_spaces={2: pltpu.SMEM},
    )
    return solution_rows, sensitivity_rows, arnoldi


def solution(mesh):
    fine = Mesh(mesh.devices.reshape(2, 2, 4, 2, 4), ALL_AXES)
    split_rows = P(ALL_AXES)
    return jax.shard_map(
        on_device,
        mesh=fine,
        in_specs=(
            P(ALL_AXES, None),
            P(),
            P(),
            P(),
            P(),
            P(),
            split_rows,
            P(ALL_AXES, None),
            split_rows,
        ),
        out_specs=(P(ALL_AXES, None), P(ALL_AXES, None), P()),
        check_vma=False,
    )
```

```python
import jax
import jax.numpy as jnp
import numpy as np
from jax import lax
from jax.experimental import pallas as pl
from jax.experimental.pallas import tpu as pltpu
from jax.sharding import Mesh
from jax.sharding import PartitionSpec as P

ORDER = 10
WAVENUMBER = 1.3
LATTICE_STEP = 2.5

SPHERES = 768
COEFF = 480
HALF = 240
GROUPS = 4
PER_GROUP = SPHERES // GROUPS
PROBES = 32768
OWN = 6
PROBES_OWN = 256
LANES = 128
WIDE = 256
FULL = 2 * WIDE
ROWS = 8
BLOCK = 2 * ROWS
BLOCKS = 4 * ORDER + 1
TOP = 2 * ORDER
CHUNK = OWN * FULL // LANES
FAR = 64
SCALE = 2.0**-14
PAD = HALF
SIN_ROWS = (ORDER + 2) * ROWS
SHARE = 2 * FULL // LANES
SCALAR_LINE = 2
SCALARS = SHARE + 4 * GROUPS
PIECE_LINES = (6, 7)
SLICE_LINES = (3, 7)
BF = jnp.bfloat16
F32 = jnp.float32

FAR_AXES = ("xl", "y", "z", "xh")
ALL_AXES = ("xl", "co", "z", "xh", "y")


def order_table(degree_max):
    entries = np.arange(degree_max * (degree_max + 2))
    degree = np.floor(np.sqrt(entries + 1.0) + 1e-09)
    orders = entries + 1 - degree * degree - degree
    return np.concatenate([orders, orders]).astype(np.int32)


_ORDERS = np.zeros((1, WIDE), np.int32)
_ORDERS[0, :HALF] = order_table(ORDER)


def dot(a, b):
    return jnp.dot(a, b, preferred_element_type=F32)


def dot_t(a, b):
    return lax.dot_general(a, b, (((1,), (1,)), ((), ())), preferred_element_type=F32)


def fine_dot(x, y, dot=dot, parts=3):
    rows = x.shape[0]
    padded = -(-rows // 16) * 16
    if padded > rows:
        x = jnp.concatenate([x, jnp.zeros((padded - rows, x.shape[1]), F32)], axis=0)
    terms = []
    for _ in range(parts):
        terms.append(x.astype(BF))
        x = x - terms[-1].astype(F32)
    product = dot(jnp.concatenate(terms, axis=0), y)
    total = product[:rows]
    for part in range(1, parts):
        total = total + product[part * padded : part * padded + rows]
    return total


def padded(x, axis):
    zeros = jnp.zeros((x.shape[0], WIDE - HALF) if axis else (WIDE - HALF, x.shape[1]), x.dtype)
    low, high = (x[:, :HALF], x[:, HALF:]) if axis else (x[:HALF, :], x[HALF:, :])
    return jnp.concatenate([low, zeros, high, zeros], axis=axis)


def own_rows(incident):
    value = jnp.concatenate([incident[...], jnp.zeros((ROWS - OWN, COEFF), F32)], axis=0) * SCALE
    return padded(value, 1)


def own_group():
    return lax.axis_index("xl") * 2 + lax.axis_index("co")


def send_body(incident, chunk, lines):
    write_chunks(own_rows(incident), chunk, lines)


def write_chunks(rows, chunk, lines):
    for part in range(4):
        lines[pl.ds(part, ROWS, stride=4), :] = rows[:, part * LANES : (part + 1) * LANES]
    once = lines[:CHUNK, :]
    for far in range(FAR):
        chunk[far * CHUNK : (far + 1) * CHUNK, :] = once


def prepare_body(
    site, jitter, rotation, axial, probes, probe_group, tmat, orders, incident, radius,
    pairs, tables, probes_out, seen_out, tmat_out, orders_out, base_out, radius_out,
):
    own = (
        lax.axis_index("xl") * PER_GROUP
        + ((lax.axis_index("y") * 4 + lax.axis_index("z")) * 2 + lax.axis_index("xh")) * OWN
    )
    sites = site[...]
    core = lax.axis_index("co")

    def own_core_first(place):
        other = jnp.concatenate([place[:, SPHERES // 2 :], place[:, : SPHERES // 2]], axis=1)
        return jnp.where(core == 0, place, other)

    place_x = own_core_first((sites & 7).astype(F32) * LATTICE_STEP + jitter[0:1, :])
    place_y = own_core_first(((sites >> 3) & 7).astype(F32) * LATTICE_STEP + jitter[1:2, :])
    place_z = own_core_first((sites >> 6).astype(F32) * LATTICE_STEP + jitter[2:3, :])
    lane = lax.broadcasted_iota(jnp.int32, (ROWS, SPHERES), 1)
    line = lax.broadcasted_iota(jnp.int32, (ROWS, SPHERES), 0)
    same = lane == line + own

    def offset(place):
        here = jnp.sum(jnp.where(same, place, 0.0), axis=1, keepdims=True)
        return here - place

    dx, dy, dz = offset(place_x), offset(place_y), offset(place_z)
    distance = jnp.sqrt(jnp.where(same, 1.0, dx * dx + dy * dy + dz * dz))
    phase = WAVENUMBER * distance
    none = same | (line >= OWN)
    radial_cos = jnp.where(none, 0.0, jnp.cos(phase) / phase)
    radial_sin = jnp.where(none, 0.0, jnp.sin(phase) / phase)
    larger = jnp.maximum(jnp.abs(dx), jnp.abs(dy))
    apart = larger > 0.0
    inverse = 1.0 / jnp.where(apart, larger, 1.0)
    ax, ay = dx * inverse, dy * inverse
    length = jnp.sqrt(jnp.where(apart, ax * ax + ay * ay, 1.0))
    cos_one = jnp.where(apart, ax / length, 1.0)
    sin_one = jnp.where(apart, ay / length, 0.0)

    def put(block, factor):
        value = jnp.concatenate([radial_cos * factor, radial_sin * factor], axis=0)
        pairs[block * BLOCK : (block + 1) * BLOCK, :] = value.astype(BF)

    pairs[0:BLOCK, :] = jnp.concatenate([radial_cos, radial_sin], axis=0).astype(BF)
    cos_k, sin_k = cos_one, sin_one
    for k in range(1, TOP + 1):
        put(k, cos_k)
        put(TOP + k, sin_k)
        if k < TOP:
            cos_k, sin_k = (
                cos_k * cos_one - sin_k * sin_one,
                sin_k * cos_one + cos_k * sin_one,
            )

    probes_out[...] = padded(probes[...], 0)
    turned = padded(rotation[...], 0)
    for radial in range(2):
        tables[radial] = fine_dot(0.5 * dot(turned, axial[radial]), turned, dot_t, 2).astype(BF)
    line = lax.broadcasted_iota(jnp.int32, (GROUPS, PROBES_OWN), 0)
    seen_out[...] = jnp.where(line == probe_group[...], 1.0, 0.0)
    tmat_rows = jnp.concatenate([tmat[...], jnp.zeros((2, WIDE - HALF), F32)], axis=1)
    tmat_out[...] = jnp.concatenate([tmat_rows, jnp.zeros((ROWS - 2, WIDE), F32)], axis=0)
    orders_out[...] = jnp.broadcast_to(orders[...], (ROWS, WIDE))
    base_out[...] = own_rows(incident)
    line = lax.broadcasted_iota(jnp.int32, (ROWS, LANES), 0)
    column = jnp.zeros((ROWS, LANES), F32)
    for r in range(OWN):
        column = jnp.where(line == r, radius[r], column)
    radius_out[...] = column


def load_rows(lines):
    parts = [lines[pl.ds(part, SPHERES // 2, stride=4), :].astype(BF) for part in range(4)]
    return jnp.concatenate(parts, axis=1)


def half_sums(lines):
    groups = []
    for place in range(2):
        parts = []
        for part in range(4):
            value = lines[pl.ds(place * PER_GROUP * 4 + part, PER_GROUP, stride=4), :]
            parts.append(jnp.sum(value, axis=0, keepdims=True))
        groups.append(jnp.concatenate(parts, axis=1))
    return jnp.concatenate(groups, axis=0)


def all_groups(mine, other):
    core = lax.axis_index("co")
    first, second = jnp.where(core == 0, mine, other), jnp.where(core == 0, other, mine)
    return jnp.concatenate([first[0:1], second[0:1], first[1:2], second[1:2]], axis=0)


def order_body(near_in, pairs, near_out):
    del near_in, pairs, near_out


def first_near_body(near, pairs, sums_out, totals_out):
    sums_out[...] = dot(pairs[:, : SPHERES // 2], load_rows(near))
    totals_out[...] = half_sums(near)


def second_near_body(near, pairs, probes, seen, sums_out, gradient_out):
    sums_out[...] = dot(pairs[:, : SPHERES // 2], load_rows(near))
    gradient_out[...] = half_gradient(near, probes, seen, lax.axis_index("co"))


def half_gradient(lines, probes, seen, core):
    totals = half_sums(lines)
    lane = lax.broadcasted_iota(jnp.int32, totals.shape, 1)
    totals = jnp.where((lane & (WIDE - 1)) < HALF, totals, 0.0)
    first, second = seen[0:2, :], seen[2:4, :]
    mask = jnp.concatenate(
        [jnp.where(core == 0, part[0:1], part[1:2]) for part in (first, second)], axis=0
    )
    return gradient_of(totals, probes, mask)


def by_order(values, bits):
    for bit, mask in zip((16, 8, 4, 2, 1), bits):
        count = TOP + bit
        values = [
            jnp.where(mask, values[j + bit], values[j]) if j + bit < len(values) else values[j]
            for j in range(count)
        ]
    return values


def mix(sums, shifted, tables, orders, dot=dot):
    zeros = jnp.zeros((ROWS, LANES), F32)
    for half in range(2):
        code = orders[:, half * LANES : (half + 1) * LANES] + ORDER
        bits = [(code & bit) != 0 for bit in (16, 8, 4, 2, 1)]
        real = slice(half * LANES, (half + 1) * LANES)
        imag = slice(WIDE + half * LANES, WIDE + (half + 1) * LANES)
        for radial in range(2):

            def load(block, columns):
                at = block * BLOCK + radial * ROWS
                return sums[at : at + ROWS, columns]

            for is_imag, columns, others in ((0, real, imag), (1, imag, real)):
                plus, minus = [load(0, columns)], []
                for k in range(1, TOP + 1):
                    cos_sum, sin_sum = load(k, columns), load(TOP + k, others)
                    plus.append(cos_sum + sin_sum if is_imag else cos_sum - sin_sum)
                    minus.append(cos_sum - sin_sum if is_imag else cos_sum + sin_sum)
                chosen = by_order(minus[::-1] + plus, bits)
                cos_part, sin_part = [], []
                for m in range(ORDER + 1):
                    ahead, behind = chosen[ORDER - m], chosen[ORDER + m]
                    cos_part.append(ahead + behind)
                    sin_part.append(behind - ahead if is_imag else ahead - behind)
                cos_part.append(zeros)
                for m in range(0, ORDER + 1, 2):
                    value = jnp.concatenate(cos_part[m : m + 2], axis=0)
                    shifted[radial, m * ROWS : (m + 2) * ROWS, columns] = value.astype(BF)
                for m in range(1, ORDER + 1, 2):
                    value = jnp.concatenate(sin_part[m : m + 2], axis=0)
                    at = SIN_ROWS + (m - 1) * ROWS
                    shifted[radial, at : at + 2 * ROWS, others] = value.astype(BF)

    back = dot(shifted[0], tables[0]) + dot(shifted[1], tables[1])
    parts_re, parts_im = [], []
    for half in range(2):
        real = slice(half * LANES, (half + 1) * LANES)
        imag = slice(WIDE + half * LANES, WIDE + (half + 1) * LANES)
        order = orders[:, real]
        size = jnp.abs(order)
        sign = jnp.where(order > 0, 1.0, -1.0)
        field_re, field_im = back[0:ROWS, real], back[0:ROWS, imag]
        for m in range(1, ORDER + 1):
            cos_lines = slice(m * ROWS, (m + 1) * ROWS)
            sin_lines = slice(SIN_ROWS + (m - 1) * ROWS, SIN_ROWS + m * ROWS)
            field_re = jnp.where(size == m, back[cos_lines, real] + sign * back[sin_lines, imag], field_re)
            field_im = jnp.where(size == m, back[cos_lines, imag] - sign * back[sin_lines, real], field_im)
        parts_re.append(field_re)
        parts_im.append(field_im)
    return jnp.concatenate(parts_re + parts_im, axis=1)


def scatter(field, tmat, radius):
    real, imag = tmat[0:1, :], tmat[1:2, :]
    field_re, field_im = field[:, :WIDE], field[:, WIDE:]
    wide = jnp.concatenate([radius, radius], axis=1)
    return jnp.concatenate(
        [
            wide * (imag * field_im - real * field_re),
            -wide * (imag * field_re + real * field_im),
        ],
        axis=1,
    )


def first_body(
    near_sums, near_totals, peer, pairs, tables, tmat, radius, orders, probes, seen,
    chunk, rows_out, sums, shifted, lines,
):
    sums[...] = near_sums[...] + dot(pairs[:, SPHERES // 2 :], load_rows(peer))
    gradient = gradient_of(all_groups(near_totals[...], half_sums(peer)), probes, seen[...])
    field = mix(sums, shifted, tables, orders)
    image = scatter(field, tmat, radius[...])
    rows_out[...] = image
    lane = lax.broadcasted_iota(jnp.int32, (ROWS, FULL), 1)
    marked = jnp.where(lane == PAD + own_group(), jnp.concatenate([radius[...]] * 4, axis=1), image)
    write_chunks(marked, chunk, lines)
    for piece in range(2):
        line = SLICE_LINES[piece]
        chunk[pl.ds(line, FAR, stride=CHUNK), :] = lines[line : line + 1, :] + slices(gradient, piece)


def piece_mask(piece):
    lane = lax.broadcasted_iota(jnp.int32, (FAR, FULL), 1)
    far = lax.broadcasted_iota(jnp.int32, (FAR, FULL), 0)
    return (lane >> 4) == ((far & (FAR // GROUPS - 1)) * 2 + piece)


def slices(gradient, piece):
    rows = [jnp.broadcast_to(gradient[g : g + 1, :], (FAR // GROUPS, FULL)) for g in range(GROUPS)]
    rows = jnp.where(piece_mask(piece), jnp.concatenate(rows, axis=0), 0.0)
    lane = lax.broadcasted_iota(jnp.int32, (FULL, LANES), 1)
    source = lax.broadcasted_iota(jnp.int32, (FULL, LANES), 0)
    fold = jnp.where(lane - (LANES - 16) == (source & 15), 1.0, 0.0).astype(BF)
    return fine_dot(rows, fold, parts=2)


def unslice(parts):
    lane = lax.broadcasted_iota(jnp.int32, (LANES, FULL), 1)
    source = lax.broadcasted_iota(jnp.int32, (LANES, FULL), 0)
    spread = jnp.where(source - (LANES - 16) == (lane & 15), 1.0, 0.0).astype(BF)
    both = fine_dot(jnp.concatenate(parts, axis=0), spread, parts=2)
    total = jnp.where(piece_mask(0), both[:FAR], jnp.where(piece_mask(1), both[FAR:], 0.0))
    each = FAR // GROUPS
    return jnp.concatenate(
        [jnp.sum(total[g * each : (g + 1) * each], axis=0, keepdims=True) for g in range(GROUPS)], axis=0
    )


def gradient_of(totals, probes, seen):
    values = fine_dot(totals, probes[...], parts=2) * seen
    return fine_dot(values, probes[...], dot_t, 2)


def to_lines(rows):
    return jnp.concatenate([rows[:, part * LANES : (part + 1) * LANES] for part in range(4)], axis=0)


def from_lines(lines):
    each = lines.shape[0] // 4
    return jnp.concatenate([lines[part * each : (part + 1) * each, :] for part in range(4)], axis=1)


def second_gradient_body(peer, probes, seen, send):
    send[...] = to_lines(half_gradient(peer, probes, seen, 1 - lax.axis_index("co")))


def second_body(
    near, near_sums, near_gradient, peer, pairs, tables, tmat, radius, orders, base, image,
    extra, weights_out, sums, shifted,
):
    sums[...] = near_sums[...] + dot(pairs[:, SPHERES // 2 :], load_rows(peer))
    for block in range(BLOCKS):
        k = block if block <= TOP else block - TOP
        at = pl.ds(block * BLOCK, BLOCK)
        value = sums[at, LANES:WIDE]
        weights_out[at, :] = (value if k % 2 == 0 else -value).astype(BF)
    field = mix(sums, shifted, tables, orders)
    last = scatter(field, tmat, radius[...])
    zero, one = base[...], image[...]
    line = lax.broadcasted_iota(jnp.int32, (SHARE, LANES), 0)
    lane = lax.broadcasted_iota(jnp.int32, (SHARE, LANES), 1)
    pairs_of = ((zero, zero), (zero, one), (one, one), (zero, last), (one, last), (last, last))
    sums_of = []
    for a, b in pairs_of:
        product = a * b
        parts = [product[:, part * LANES : (part + 1) * LANES] for part in range(4)]
        sums_of.append(jnp.sum((parts[0] + parts[1]) + (parts[2] + parts[3]), axis=0, keepdims=True))
    stacked = jnp.concatenate(sums_of + [jnp.zeros((SHARE - 6, LANES), F32)], axis=0)
    column = jnp.sum(stacked, axis=1, keepdims=True)
    row = jnp.sum(jnp.where(lane - (PAD - LANES) == line, column, 0.0), axis=0, keepdims=True)
    out = jnp.where(line == SCALAR_LINE, row, 0.0)
    for piece in range(2):
        value = jnp.sum(near[pl.ds(SLICE_LINES[piece], FAR, stride=CHUNK), :], axis=0, keepdims=True)
        out = jnp.where((line == PIECE_LINES[piece]) & (lane >= LANES - 16), value, out)
    extra[...] = out + to_lines(near_gradient[...])


def sum_body(near, out):
    total = near[pl.ds(0, SHARE), :]
    for far in range(1, FAR):
        total = total + near[pl.ds(far * SHARE, SHARE), :]
    out[:SHARE, :] = total
    pieces = [near[pl.ds(PIECE_LINES[piece], FAR, stride=SHARE), :] for piece in range(2)]
    out[SHARE:SCALARS, :] = to_lines(unslice(pieces))
    line = total[SCALAR_LINE : SCALAR_LINE + 1, :]
    for index in range(6):
        at = PAD - LANES + index
        out[SCALARS + index : SCALARS + index + 1, :] = jnp.broadcast_to(line[:, at : at + 1], (1, LANES))


def finish_body(
    near, peer, weights, tables, tmat, orders, incident, image,
    solution_out, sensitivity_out, arnoldi_out, places, sums, shifted,
):
    g00, g01, g11, g02, g12, g22 = [near[at : at + 1, :] + peer[at : at + 1, :] for at in range(SCALARS, SCALARS + 6)]
    scale = 1.0 / g00
    g01, g11, g02, g12, g22 = g01 * scale, g11 * scale, g02 * scale, g12 * scale, g22 * scale
    core = lax.axis_index("co")
    first = from_lines(near[SHARE:SCALARS, :] + peer[SHARE:SCALARS, :])
    mine, other = from_lines(near[:SHARE, :]), from_lines(peer[:SHARE, :])
    even, odd = jnp.where(core == 0, mine, other), jnp.where(core == 0, other, mine)
    second = jnp.concatenate([even[0:1], odd[0:1], even[1:2], odd[1:2]], axis=0)
    diag_first = 1.0 + g01
    below_sq = g11 - g01 * g01
    full = below_sq > 0.0
    below_sq = jnp.where(full, below_sq, 0.0)
    inverse = 1.0 / jnp.where(full, below_sq, 1.0)
    upper = g02 - g01 * g01
    shift = g12 - g01 * (g11 + g02 - g01 * g01)
    norm_sq = g22 - g01 * (2.0 * g12 - g01 * g11)
    cross = diag_first * upper + below_sq + shift
    gram_first = diag_first * diag_first + below_sq
    gram_second = (below_sq + 2.0 * shift + norm_sq) * inverse
    cross_scaled = cross * inverse
    determinant = jnp.where(full, gram_first * gram_second - cross * cross_scaled, 1.0)
    for_image = (upper - diag_first * (1.0 + shift * inverse)) / determinant
    for_base = (diag_first * gram_second - upper * cross_scaled) / determinant - for_image * g01
    for_image = jnp.where(full, for_image, 0.0)
    for_base = jnp.where(full, for_base, diag_first / gram_first)
    below_first = jnp.sqrt(below_sq)
    shift_second = shift * inverse
    diag_second = 1.0 + shift_second
    rest_second = (norm_sq - upper * upper) * inverse - shift_second * shift_second
    arnoldi_out[0] = diag_first[0, 0]
    arnoldi_out[1] = below_first[0, 0]
    arnoldi_out[2] = diag_second[0, 0]
    arnoldi_out[3] = rest_second[0, 0]

    for_base, for_image = [jnp.concatenate([part] * 4, axis=1) for part in (for_base, for_image)]
    factor = COEFF * GROUPS / PROBES / SCALE / float(np.sqrt(np.float32(PER_GROUP)))
    gradient = (for_base * first + for_image * second) * factor
    real, imag = tmat[0:1, :], tmat[1:2, :]
    grad_re, grad_im = gradient[:, :WIDE], gradient[:, WIDE:]
    places[...] = jnp.zeros((LANES, FULL), F32)
    at = pl.ds(PAD - LANES, GROUPS)
    places[at, :WIDE] = real * grad_re + imag * grad_im
    places[at, WIDE:] = real * grad_im - imag * grad_re
    sums[...] = dot(weights[...], places[...].astype(BF))
    field = mix(sums, shifted, tables, orders, dot_t)
    group = own_group()
    own = jnp.zeros((1, FULL), F32)
    for g in range(GROUPS):
        own = jnp.where(group == g, gradient[g : g + 1, :], own)
    lane = lax.broadcasted_iota(jnp.int32, (1, FULL), 1)
    own = jnp.where((lane & (WIDE - 1)) < HALF, own, 0.0)
    image_rows = unpadded(image[...])
    solution_out[...] = for_base[:, :COEFF] * incident[...] + (for_image[:, :COEFF] / SCALE) * image_rows
    sensitivity_out[...] = unpadded(own - field)


def unpadded(rows):
    return jnp.concatenate([rows[:OWN, :HALF], rows[:OWN, WIDE : WIDE + HALF]], axis=1)


def call(body, outs, scratch=(), operands=(), spaces=None, out_spaces=None, cost=None, aliases=None):
    spaces, out_spaces = spaces or {}, out_spaces or {}
    return pl.pallas_call(
        body,
        out_shape=[jax.ShapeDtypeStruct(shape, kind) for shape, kind in outs],
        in_specs=[pl.BlockSpec(memory_space=spaces.get(i, pltpu.VMEM)) for i in range(len(operands))],
        out_specs=[pl.BlockSpec(memory_space=out_spaces.get(i, pltpu.VMEM)) for i in range(len(outs))],
        scratch_shapes=list(scratch),
        compiler_params=pltpu.CompilerParams(vmem_limit_bytes=8 * 1024 * 1024),
        cost_estimate=cost,
        input_output_aliases=aliases or {},
    )(*operands)


def swap_cores(array):
    return lax.ppermute(array, "co", [(0, 1), (1, 0)])


def spread_far(lines):
    parts = lines.reshape(FAR, lines.shape[0] // FAR, LANES)
    return lax.all_to_all(parts, FAR_AXES, 0, 0).reshape(lines.shape)


def on_device(
    incident,
    sphere_site,
    jitter,
    rotation_table,
    axial_tables,
    tmatrix,
    radius_factor,
    probe_field,
    probe_group,
):
    line_scratch = pltpu.VMEM((4 * ROWS, LANES), F32)
    sum_scratch = pltpu.VMEM((BLOCKS * BLOCK, FULL), F32)
    shift_scratch = pltpu.VMEM((2, (ORDER + 1) * BLOCK, FULL), BF)
    rows_shape = ((ROWS, FULL), F32)
    chunk_shape = ((FAR * CHUNK, LANES), F32)
    share_shape = ((SHARE, LANES), F32)
    half_cost = pl.CostEstimate(flops=8_000_000_000, bytes_accessed=4_000_000, transcendentals=0)

    (chunk,) = call(send_body, [chunk_shape], [line_scratch], (incident,))

    def by_core(array):
        lead = array.shape[:-1]
        at = len(lead)
        by_device = array.reshape(lead + (2, 2, 4, 2, 4, OWN))
        order = tuple(range(at)) + tuple(at + axis for axis in (1, 0, 4, 2, 3, 5))
        return by_device.transpose(order).reshape(lead + (SPHERES,))

    pairs, tables, probes, seen, tmat, orders, base, radius = call(
        prepare_body,
        [
            ((BLOCKS * BLOCK, SPHERES), BF),
            ((2, FULL, FULL), BF),
            ((FULL, PROBES_OWN), BF),
            ((GROUPS, PROBES_OWN), F32),
            ((ROWS, WIDE), F32),
            ((ROWS, WIDE), jnp.int32),
            rows_shape,
            ((ROWS, LANES), F32),
        ],
        operands=(
            by_core(sphere_site[None, :]),
            by_core(jitter),
            rotation_table,
            axial_tables,
            probe_field.T,
            probe_group.reshape(1, PROBES_OWN),
            tmatrix,
            jnp.asarray(_ORDERS),
            incident,
            radius_factor,
        ),
        spaces={9: pltpu.SMEM},
        cost=pl.CostEstimate(flops=8_000_000_000, bytes_accessed=8_000_000, transcendentals=20_000),
    )

    near = spread_far(chunk)
    (near,) = call(order_body, [chunk_shape], operands=(near, pairs), spaces={1: pl.ANY}, aliases={0: 0})
    sums_shape = ((BLOCKS * BLOCK, FULL), F32)
    near_sums, near_totals = call(
        first_near_body,
        [sums_shape, ((2, FULL), F32)],
        operands=(near, pairs),
        cost=half_cost,
    )
    chunk, image = call(
        first_body,
        [chunk_shape, rows_shape],
        [sum_scratch, shift_scratch, line_scratch],
        (near_sums, near_totals, swap_cores(near), pairs, tables, tmat, radius, orders, probes, seen),
    )

    near = spread_far(chunk)
    peer = swap_cores(near)
    near_sums, near_gradient = call(
        second_near_body,
        [sums_shape, ((2, FULL), F32)],
        operands=(near, pairs, probes, seen),
        cost=half_cost,
    )
    (send,) = call(second_gradient_body, [share_shape], operands=(peer, probes, seen))
    received = swap_cores(send)
    extra, weights = call(
        second_body,
        [share_shape, ((BLOCKS * BLOCK, LANES), BF)],
        [sum_scratch, shift_scratch],
        (near, near_sums, near_gradient, peer, pairs, tables, tmat, radius, orders, base, image),
        cost=half_cost,
    )
    share = received + extra
    near = spread_far(jnp.broadcast_to(share[None], (FAR, SHARE, LANES)).reshape(FAR * SHARE, LANES))
    (near,) = call(sum_body, [((SCALARS + 8, LANES), F32)], operands=(near,))
    peer = swap_cores(near)
    solution_rows, sensitivity_rows, arnoldi = call(
        finish_body,
        [((OWN, COEFF), F32), ((OWN, COEFF), F32), ((4,), F32)],
        [pltpu.VMEM((LANES, FULL), F32), sum_scratch, shift_scratch],
        (near, peer, weights, tables, tmat, orders, incident, image),
        out_spaces={2: pltpu.SMEM},
    )
    return solution_rows, sensitivity_rows, arnoldi


def solution(mesh):
    fine = Mesh(mesh.devices.reshape(2, 2, 4, 2, 4), ALL_AXES)
    split_rows = P(ALL_AXES)
    return jax.shard_map(
        on_device,
        mesh=fine,
        in_specs=(
            P(ALL_AXES, None),
            P(),
            P(),
            P(),
            P(),
            P(),
            split_rows,
            P(ALL_AXES, None),
            split_rows,
        ),
        out_specs=(P(ALL_AXES, None), P(ALL_AXES, None), P()),
        check_vma=False,
    )
```

```python
import jax
import jax.numpy as jnp
import numpy as np
from jax import lax
from jax.experimental import pallas as pl
from jax.experimental.pallas import tpu as pltpu
from jax.sharding import Mesh
from jax.sharding import PartitionSpec as P

ORDER = 10
WAVENUMBER = 1.3
LATTICE_STEP = 2.5

SPHERES = 768
COEFF = 480
HALF = 240
GROUPS = 4
PER_GROUP = SPHERES // GROUPS
PROBES = 32768
OWN = 6
PROBES_OWN = 256
LANES = 128
WIDE = 256
FULL = 2 * WIDE
ROWS = 8
BLOCK = 2 * ROWS
BLOCKS = 4 * ORDER + 1
TOP = 2 * ORDER
CHUNK = OWN * FULL // LANES
FAR = 64
SCALE = 2.0**-14
PAD = HALF
SIN_ROWS = (ORDER + 2) * ROWS
SHARE = 2 * FULL // LANES
SCALAR_LINE = 2
SCALARS = SHARE + 4 * GROUPS
PIECE_LINES = (6, 7)
SLICE_LINES = (3, 7)
BF = jnp.bfloat16
F32 = jnp.float32

FAR_AXES = ("xl", "y", "z", "xh")
ALL_AXES = ("xl", "co", "z", "xh", "y")


def order_table(degree_max):
    entries = np.arange(degree_max * (degree_max + 2))
    degree = np.floor(np.sqrt(entries + 1.0) + 1e-09)
    orders = entries + 1 - degree * degree - degree
    return np.concatenate([orders, orders]).astype(np.int32)


_ORDERS = np.zeros((1, WIDE), np.int32)
_ORDERS[0, :HALF] = order_table(ORDER)


def dot(a, b):
    return jnp.dot(a, b, preferred_element_type=F32)


def dot_t(a, b):
    return lax.dot_general(a, b, (((1,), (1,)), ((), ())), preferred_element_type=F32)


def fine_dot(x, y, dot=dot, parts=3):
    rows = x.shape[0]
    padded = -(-rows // 16) * 16
    if padded > rows:
        x = jnp.concatenate([x, jnp.zeros((padded - rows, x.shape[1]), F32)], axis=0)
    terms = []
    for _ in range(parts):
        terms.append(x.astype(BF))
        x = x - terms[-1].astype(F32)
    product = dot(jnp.concatenate(terms, axis=0), y)
    total = product[:rows]
    for part in range(1, parts):
        total = total + product[part * padded : part * padded + rows]
    return total


def padded(x, axis):
    zeros = jnp.zeros((x.shape[0], WIDE - HALF) if axis else (WIDE - HALF, x.shape[1]), x.dtype)
    low, high = (x[:, :HALF], x[:, HALF:]) if axis else (x[:HALF, :], x[HALF:, :])
    return jnp.concatenate([low, zeros, high, zeros], axis=axis)


def own_rows(incident):
    value = jnp.concatenate([incident[...], jnp.zeros((ROWS - OWN, COEFF), F32)], axis=0) * SCALE
    return padded(value, 1)


def own_group():
    return lax.axis_index("xl") * 2 + lax.axis_index("co")


def send_body(incident, chunk, lines):
    write_chunks(own_rows(incident), chunk, lines)


def write_chunks(rows, chunk, lines):
    for part in range(4):
        lines[pl.ds(part, ROWS, stride=4), :] = rows[:, part * LANES : (part + 1) * LANES]
    once = lines[:CHUNK, :]
    for far in range(FAR):
        chunk[far * CHUNK : (far + 1) * CHUNK, :] = once


def prepare_body(
    site, jitter, rotation, axial, probes, probe_group, tmat, orders, incident, radius,
    pairs, tables, tables_t, probes_out, seen_out, tmat_out, orders_out, base_out, radius_out,
):
    own = (
        lax.axis_index("xl") * PER_GROUP
        + ((lax.axis_index("y") * 4 + lax.axis_index("z")) * 2 + lax.axis_index("xh")) * OWN
    )
    sites = site[...]
    core = lax.axis_index("co")

    def own_core_first(place):
        other = jnp.concatenate([place[:, SPHERES // 2 :], place[:, : SPHERES // 2]], axis=1)
        return jnp.where(core == 0, place, other)

    place_x = own_core_first((sites & 7).astype(F32) * LATTICE_STEP + jitter[0:1, :])
    place_y = own_core_first(((sites >> 3) & 7).astype(F32) * LATTICE_STEP + jitter[1:2, :])
    place_z = own_core_first((sites >> 6).astype(F32) * LATTICE_STEP + jitter[2:3, :])
    lane = lax.broadcasted_iota(jnp.int32, (ROWS, SPHERES), 1)
    line = lax.broadcasted_iota(jnp.int32, (ROWS, SPHERES), 0)
    same = lane == line + own

    def offset(place):
        here = jnp.sum(jnp.where(same, place, 0.0), axis=1, keepdims=True)
        return here - place

    dx, dy, dz = offset(place_x), offset(place_y), offset(place_z)
    distance = jnp.sqrt(jnp.where(same, 1.0, dx * dx + dy * dy + dz * dz))
    phase = WAVENUMBER * distance
    none = same | (line >= OWN)
    radial_cos = jnp.where(none, 0.0, jnp.cos(phase) / phase)
    radial_sin = jnp.where(none, 0.0, jnp.sin(phase) / phase)
    larger = jnp.maximum(jnp.abs(dx), jnp.abs(dy))
    apart = larger > 0.0
    inverse = 1.0 / jnp.where(apart, larger, 1.0)
    ax, ay = dx * inverse, dy * inverse
    length = jnp.sqrt(jnp.where(apart, ax * ax + ay * ay, 1.0))
    cos_one = jnp.where(apart, ax / length, 1.0)
    sin_one = jnp.where(apart, ay / length, 0.0)

    def put(block, factor):
        value = jnp.concatenate([radial_cos * factor, radial_sin * factor], axis=0)
        pairs[block * BLOCK : (block + 1) * BLOCK, :] = value.astype(BF)

    pairs[0:BLOCK, :] = jnp.concatenate([radial_cos, radial_sin], axis=0).astype(BF)
    cos_k, sin_k = cos_one, sin_one
    for k in range(1, TOP + 1):
        put(k, cos_k)
        put(TOP + k, sin_k)
        if k < TOP:
            cos_k, sin_k = (
                cos_k * cos_one - sin_k * sin_one,
                sin_k * cos_one + cos_k * sin_one,
            )

    probes_out[...] = padded(probes[...], 0)
    turned = padded(rotation[...], 0)
    for radial in range(2):
        tables[radial] = fine_dot(0.5 * dot(turned, axial[radial]), turned, dot_t, 2).astype(BF)
        tables_t[radial] = fine_dot(0.5 * dot_t(turned, axial[radial]), turned, dot_t, 2).astype(BF)
    line = lax.broadcasted_iota(jnp.int32, (GROUPS, PROBES_OWN), 0)
    seen_out[...] = jnp.where(line == probe_group[...], 1.0, 0.0)
    tmat_rows = jnp.concatenate([tmat[...], jnp.zeros((2, WIDE - HALF), F32)], axis=1)
    tmat_out[...] = jnp.concatenate([tmat_rows, jnp.zeros((ROWS - 2, WIDE), F32)], axis=0)
    orders_out[...] = jnp.broadcast_to(orders[...], (ROWS, WIDE))
    base_out[...] = own_rows(incident)
    line = lax.broadcasted_iota(jnp.int32, (ROWS, LANES), 0)
    column = jnp.zeros((ROWS, LANES), F32)
    for r in range(OWN):
        column = jnp.where(line == r, radius[r], column)
    radius_out[...] = column


def load_rows(lines):
    parts = [lines[pl.ds(part, SPHERES // 2, stride=4), :].astype(BF) for part in range(4)]
    return jnp.concatenate(parts, axis=1)


def half_sums(lines):
    groups = []
    for place in range(2):
        parts = []
        for part in range(4):
            value = lines[pl.ds(place * PER_GROUP * 4 + part, PER_GROUP, stride=4), :]
            parts.append(jnp.sum(value, axis=0, keepdims=True))
        groups.append(jnp.concatenate(parts, axis=1))
    return jnp.concatenate(groups, axis=0)


def all_groups(mine, other):
    core = lax.axis_index("co")
    first, second = jnp.where(core == 0, mine, other), jnp.where(core == 0, other, mine)
    return jnp.concatenate([first[0:1], second[0:1], first[1:2], second[1:2]], axis=0)


def order_body(near_in, pairs, near_out):
    del near_in, pairs, near_out


def first_near_body(near, pairs, sums_out, totals_out):
    sums_out[...] = dot(pairs[:, : SPHERES // 2], load_rows(near))
    totals_out[...] = half_sums(near)


def second_near_body(near, pairs, probes, seen, sums_out, gradient_out):
    sums_out[...] = dot(pairs[:, : SPHERES // 2], load_rows(near))
    gradient_out[...] = half_gradient(near, probes, seen, lax.axis_index("co"))


def half_gradient(lines, probes, seen, core):
    totals = half_sums(lines)
    lane = lax.broadcasted_iota(jnp.int32, totals.shape, 1)
    totals = jnp.where((lane & (WIDE - 1)) < HALF, totals, 0.0)
    first, second = seen[0:2, :], seen[2:4, :]
    mask = jnp.concatenate(
        [jnp.where(core == 0, part[0:1], part[1:2]) for part in (first, second)], axis=0
    )
    return gradient_of(totals, probes, mask)


def by_order(values, bits):
    for bit, mask in zip((16, 8, 4, 2, 1), bits):
        count = TOP + bit
        values = [
            jnp.where(mask, values[j + bit], values[j]) if j + bit < len(values) else values[j]
            for j in range(count)
        ]
    return values


def mix(sums, shifted, tables, orders, dot=dot):
    zeros = jnp.zeros((ROWS, LANES), F32)
    for half in range(2):
        code = orders[:, half * LANES : (half + 1) * LANES] + ORDER
        bits = [(code & bit) != 0 for bit in (16, 8, 4, 2, 1)]
        real = slice(half * LANES, (half + 1) * LANES)
        imag = slice(WIDE + half * LANES, WIDE + (half + 1) * LANES)
        for radial in range(2):

            def load(block, columns):
                at = block * BLOCK + radial * ROWS
                return sums[at : at + ROWS, columns]

            for is_imag, columns, others in ((0, real, imag), (1, imag, real)):
                plus, minus = [load(0, columns)], []
                for k in range(1, TOP + 1):
                    cos_sum, sin_sum = load(k, columns), load(TOP + k, others)
                    plus.append(cos_sum + sin_sum if is_imag else cos_sum - sin_sum)
                    minus.append(cos_sum - sin_sum if is_imag else cos_sum + sin_sum)
                chosen = by_order(minus[::-1] + plus, bits)
                cos_part, sin_part = [], []
                for m in range(ORDER + 1):
                    ahead, behind = chosen[ORDER - m], chosen[ORDER + m]
                    cos_part.append(ahead + behind)
                    sin_part.append(behind - ahead if is_imag else ahead - behind)
                cos_part.append(zeros)
                for m in range(0, ORDER + 1, 2):
                    value = jnp.concatenate(cos_part[m : m + 2], axis=0)
                    shifted[radial, m * ROWS : (m + 2) * ROWS, columns] = value.astype(BF)
                for m in range(1, ORDER + 1, 2):
                    value = jnp.concatenate(sin_part[m : m + 2], axis=0)
                    at = SIN_ROWS + (m - 1) * ROWS
                    shifted[radial, at : at + 2 * ROWS, others] = value.astype(BF)

    back = dot(shifted[0], tables[0]) + dot(shifted[1], tables[1])
    parts_re, parts_im = [], []
    for half in range(2):
        real = slice(half * LANES, (half + 1) * LANES)
        imag = slice(WIDE + half * LANES, WIDE + (half + 1) * LANES)
        order = orders[:, real]
        size = jnp.abs(order)
        sign = jnp.where(order > 0, 1.0, -1.0)
        field_re, field_im = back[0:ROWS, real], back[0:ROWS, imag]
        for m in range(1, ORDER + 1):
            cos_lines = slice(m * ROWS, (m + 1) * ROWS)
            sin_lines = slice(SIN_ROWS + (m - 1) * ROWS, SIN_ROWS + m * ROWS)
            field_re = jnp.where(size == m, back[cos_lines, real] + sign * back[sin_lines, imag], field_re)
            field_im = jnp.where(size == m, back[cos_lines, imag] - sign * back[sin_lines, real], field_im)
        parts_re.append(field_re)
        parts_im.append(field_im)
    return jnp.concatenate(parts_re + parts_im, axis=1)


def scatter(field, tmat, radius):
    real, imag = tmat[0:1, :], tmat[1:2, :]
    field_re, field_im = field[:, :WIDE], field[:, WIDE:]
    wide = jnp.concatenate([radius, radius], axis=1)
    return jnp.concatenate(
        [
            wide * (imag * field_im - real * field_re),
            -wide * (imag * field_re + real * field_im),
        ],
        axis=1,
    )


def first_body(
    near_sums, near_totals, peer, pairs, tables, tmat, radius, orders, probes, seen,
    chunk, rows_out, sums, shifted, lines,
):
    sums[...] = near_sums[...] + dot(pairs[:, SPHERES // 2 :], load_rows(peer))
    gradient = gradient_of(all_groups(near_totals[...], half_sums(peer)), probes, seen[...])
    field = mix(sums, shifted, tables, orders)
    image = scatter(field, tmat, radius[...])
    rows_out[...] = image
    lane = lax.broadcasted_iota(jnp.int32, (ROWS, FULL), 1)
    marked = jnp.where(lane == PAD + own_group(), jnp.concatenate([radius[...]] * 4, axis=1), image)
    write_chunks(marked, chunk, lines)
    for piece in range(2):
        line = SLICE_LINES[piece]
        chunk[pl.ds(line, FAR, stride=CHUNK), :] = lines[line : line + 1, :] + slices(gradient, piece)


def piece_mask(piece):
    lane = lax.broadcasted_iota(jnp.int32, (FAR, FULL), 1)
    far = lax.broadcasted_iota(jnp.int32, (FAR, FULL), 0)
    return (lane >> 4) == ((far & (FAR // GROUPS - 1)) * 2 + piece)


def slices(gradient, piece):
    rows = [jnp.broadcast_to(gradient[g : g + 1, :], (FAR // GROUPS, FULL)) for g in range(GROUPS)]
    rows = jnp.where(piece_mask(piece), jnp.concatenate(rows, axis=0), 0.0)
    lane = lax.broadcasted_iota(jnp.int32, (FULL, LANES), 1)
    source = lax.broadcasted_iota(jnp.int32, (FULL, LANES), 0)
    fold = jnp.where(lane - (LANES - 16) == (source & 15), 1.0, 0.0).astype(BF)
    return fine_dot(rows, fold, parts=2)


def unslice(parts):
    lane = lax.broadcasted_iota(jnp.int32, (LANES, FULL), 1)
    source = lax.broadcasted_iota(jnp.int32, (LANES, FULL), 0)
    spread = jnp.where(source - (LANES - 16) == (lane & 15), 1.0, 0.0).astype(BF)
    both = fine_dot(jnp.concatenate(parts, axis=0), spread, parts=2)
    total = jnp.where(piece_mask(0), both[:FAR], jnp.where(piece_mask(1), both[FAR:], 0.0))
    each = FAR // GROUPS
    return jnp.concatenate(
        [jnp.sum(total[g * each : (g + 1) * each], axis=0, keepdims=True) for g in range(GROUPS)], axis=0
    )


def gradient_of(totals, probes, seen):
    values = fine_dot(totals, probes[...], parts=2) * seen
    return fine_dot(values, probes[...], dot_t, 2)


def to_lines(rows):
    return jnp.concatenate([rows[:, part * LANES : (part + 1) * LANES] for part in range(4)], axis=0)


def from_lines(lines):
    each = lines.shape[0] // 4
    return jnp.concatenate([lines[part * each : (part + 1) * each, :] for part in range(4)], axis=1)


def second_gradient_body(peer, probes, seen, send):
    send[...] = to_lines(half_gradient(peer, probes, seen, 1 - lax.axis_index("co")))


def second_body(
    near, near_sums, near_gradient, peer, pairs, tables, tmat, radius, orders, base, image,
    extra, weights_out, sums, shifted,
):
    sums[...] = near_sums[...] + dot(pairs[:, SPHERES // 2 :], load_rows(peer))
    for block in range(BLOCKS):
        k = block if block <= TOP else block - TOP
        at = pl.ds(block * BLOCK, BLOCK)
        value = sums[at, LANES:WIDE]
        weights_out[at, :] = (value if k % 2 == 0 else -value).astype(BF)
    field = mix(sums, shifted, tables, orders)
    last = scatter(field, tmat, radius[...])
    zero, one = base[...], image[...]
    line = lax.broadcasted_iota(jnp.int32, (SHARE, LANES), 0)
    lane = lax.broadcasted_iota(jnp.int32, (SHARE, LANES), 1)
    pairs_of = ((zero, zero), (zero, one), (one, one), (zero, last), (one, last), (last, last))
    sums_of = []
    for a, b in pairs_of:
        product = a * b
        parts = [product[:, part * LANES : (part + 1) * LANES] for part in range(4)]
        sums_of.append(jnp.sum((parts[0] + parts[1]) + (parts[2] + parts[3]), axis=0, keepdims=True))
    stacked = jnp.concatenate(sums_of + [jnp.zeros((SHARE - 6, LANES), F32)], axis=0)
    column = jnp.sum(stacked, axis=1, keepdims=True)
    row = jnp.sum(jnp.where(lane - (PAD - LANES) == line, column, 0.0), axis=0, keepdims=True)
    out = jnp.where(line == SCALAR_LINE, row, 0.0)
    for piece in range(2):
        value = jnp.sum(near[pl.ds(SLICE_LINES[piece], FAR, stride=CHUNK), :], axis=0, keepdims=True)
        out = jnp.where((line == PIECE_LINES[piece]) & (lane >= LANES - 16), value, out)
    extra[...] = out + to_lines(near_gradient[...])


def sum_body(near, out):
    total = near[pl.ds(0, SHARE), :]
    for far in range(1, FAR):
        total = total + near[pl.ds(far * SHARE, SHARE), :]
    out[:SHARE, :] = total
    pieces = [near[pl.ds(PIECE_LINES[piece], FAR, stride=SHARE), :] for piece in range(2)]
    out[SHARE:SCALARS, :] = to_lines(unslice(pieces))
    line = total[SCALAR_LINE : SCALAR_LINE + 1, :]
    for index in range(6):
        at = PAD - LANES + index
        out[SCALARS + index : SCALARS + index + 1, :] = jnp.broadcast_to(line[:, at : at + 1], (1, LANES))


def finish_body(
    near, peer, weights, tables, tmat, orders, incident, image,
    solution_out, sensitivity_out, arnoldi_out, places, sums, shifted,
):
    g00, g01, g11, g02, g12, g22 = [near[at : at + 1, :] + peer[at : at + 1, :] for at in range(SCALARS, SCALARS + 6)]
    scale = 1.0 / g00
    g01, g11, g02, g12, g22 = g01 * scale, g11 * scale, g02 * scale, g12 * scale, g22 * scale
    core = lax.axis_index("co")
    first = from_lines(near[SHARE:SCALARS, :] + peer[SHARE:SCALARS, :])
    mine, other = from_lines(near[:SHARE, :]), from_lines(peer[:SHARE, :])
    even, odd = jnp.where(core == 0, mine, other), jnp.where(core == 0, other, mine)
    second = jnp.concatenate([even[0:1], odd[0:1], even[1:2], odd[1:2]], axis=0)
    diag_first = 1.0 + g01
    below_sq = g11 - g01 * g01
    full = below_sq > 0.0
    below_sq = jnp.where(full, below_sq, 0.0)
    inverse = 1.0 / jnp.where(full, below_sq, 1.0)
    upper = g02 - g01 * g01
    shift = g12 - g01 * (g11 + g02 - g01 * g01)
    norm_sq = g22 - g01 * (2.0 * g12 - g01 * g11)
    cross = diag_first * upper + below_sq + shift
    gram_first = diag_first * diag_first + below_sq
    gram_second = (below_sq + 2.0 * shift + norm_sq) * inverse
    cross_scaled = cross * inverse
    determinant = jnp.where(full, gram_first * gram_second - cross * cross_scaled, 1.0)
    for_image = (upper - diag_first * (1.0 + shift * inverse)) / determinant
    for_base = (diag_first * gram_second - upper * cross_scaled) / determinant - for_image * g01
    for_image = jnp.where(full, for_image, 0.0)
    for_base = jnp.where(full, for_base, diag_first / gram_first)
    below_first = jnp.sqrt(below_sq)
    shift_second = shift * inverse
    diag_second = 1.0 + shift_second
    rest_second = (norm_sq - upper * upper) * inverse - shift_second * shift_second
    arnoldi_out[0] = diag_first[0, 0]
    arnoldi_out[1] = below_first[0, 0]
    arnoldi_out[2] = diag_second[0, 0]
    arnoldi_out[3] = rest_second[0, 0]

    for_base, for_image = [jnp.concatenate([part] * 4, axis=1) for part in (for_base, for_image)]
    factor = COEFF * GROUPS / PROBES / SCALE / float(np.sqrt(np.float32(PER_GROUP)))
    gradient = (for_base * first + for_image * second) * factor
    real, imag = tmat[0:1, :], tmat[1:2, :]
    grad_re, grad_im = gradient[:, :WIDE], gradient[:, WIDE:]
    places[...] = jnp.zeros((LANES, FULL), F32)
    at = pl.ds(PAD - LANES, GROUPS)
    places[at, :WIDE] = real * grad_re + imag * grad_im
    places[at, WIDE:] = real * grad_im - imag * grad_re
    sums[...] = dot(weights[...], places[...].astype(BF))
    field = mix(sums, shifted, tables, orders)
    group = own_group()
    own = jnp.zeros((1, FULL), F32)
    for g in range(GROUPS):
        own = jnp.where(group == g, gradient[g : g + 1, :], own)
    lane = lax.broadcasted_iota(jnp.int32, (1, FULL), 1)
    own = jnp.where((lane & (WIDE - 1)) < HALF, own, 0.0)
    image_rows = unpadded(image[...])
    solution_out[...] = for_base[:, :COEFF] * incident[...] + (for_image[:, :COEFF] / SCALE) * image_rows
    sensitivity_out[...] = unpadded(own - field)


def unpadded(rows):
    return jnp.concatenate([rows[:OWN, :HALF], rows[:OWN, WIDE : WIDE + HALF]], axis=1)


def call(body, outs, scratch=(), operands=(), spaces=None, out_spaces=None, cost=None, aliases=None):
    spaces, out_spaces = spaces or {}, out_spaces or {}
    return pl.pallas_call(
        body,
        out_shape=[jax.ShapeDtypeStruct(shape, kind) for shape, kind in outs],
        in_specs=[pl.BlockSpec(memory_space=spaces.get(i, pltpu.VMEM)) for i in range(len(operands))],
        out_specs=[pl.BlockSpec(memory_space=out_spaces.get(i, pltpu.VMEM)) for i in range(len(outs))],
        scratch_shapes=list(scratch),
        compiler_params=pltpu.CompilerParams(vmem_limit_bytes=8 * 1024 * 1024),
        cost_estimate=cost,
        input_output_aliases=aliases or {},
    )(*operands)


def swap_cores(array):
    return lax.ppermute(array, "co", [(0, 1), (1, 0)])


def spread_far(lines):
    parts = lines.reshape(FAR, lines.shape[0] // FAR, LANES)
    return lax.all_to_all(parts, FAR_AXES, 0, 0).reshape(lines.shape)


def on_device(
    incident,
    sphere_site,
    jitter,
    rotation_table,
    axial_tables,
    tmatrix,
    radius_factor,
    probe_field,
    probe_group,
):
    line_scratch = pltpu.VMEM((4 * ROWS, LANES), F32)
    sum_scratch = pltpu.VMEM((BLOCKS * BLOCK, FULL), F32)
    shift_scratch = pltpu.VMEM((2, (ORDER + 1) * BLOCK, FULL), BF)
    rows_shape = ((ROWS, FULL), F32)
    chunk_shape = ((FAR * CHUNK, LANES), F32)
    share_shape = ((SHARE, LANES), F32)
    half_cost = pl.CostEstimate(flops=8_000_000_000, bytes_accessed=4_000_000, transcendentals=0)

    (chunk,) = call(send_body, [chunk_shape], [line_scratch], (incident,))

    def by_core(array):
        lead = array.shape[:-1]
        at = len(lead)
        by_device = array.reshape(lead + (2, 2, 4, 2, 4, OWN))
        order = tuple(range(at)) + tuple(at + axis for axis in (1, 0, 4, 2, 3, 5))
        return by_device.transpose(order).reshape(lead + (SPHERES,))

    pairs, tables, tables_t, probes, seen, tmat, orders, base, radius = call(
        prepare_body,
        [
            ((BLOCKS * BLOCK, SPHERES), BF),
            ((2, FULL, FULL), BF),
            ((2, FULL, FULL), BF),
            ((FULL, PROBES_OWN), BF),
            ((GROUPS, PROBES_OWN), F32),
            ((ROWS, WIDE), F32),
            ((ROWS, WIDE), jnp.int32),
            rows_shape,
            ((ROWS, LANES), F32),
        ],
        operands=(
            by_core(sphere_site[None, :]),
            by_core(jitter),
            rotation_table,
            axial_tables,
            probe_field.T,
            probe_group.reshape(1, PROBES_OWN),
            tmatrix,
            jnp.asarray(_ORDERS),
            incident,
            radius_factor,
        ),
        spaces={9: pltpu.SMEM},
        cost=pl.CostEstimate(flops=8_000_000_000, bytes_accessed=8_000_000, transcendentals=20_000),
    )

    near = spread_far(chunk)
    (near,) = call(order_body, [chunk_shape], operands=(near, pairs), spaces={1: pl.ANY}, aliases={0: 0})
    sums_shape = ((BLOCKS * BLOCK, FULL), F32)
    near_sums, near_totals = call(
        first_near_body,
        [sums_shape, ((2, FULL), F32)],
        operands=(near, pairs),
        cost=half_cost,
    )
    chunk, image = call(
        first_body,
        [chunk_shape, rows_shape],
        [sum_scratch, shift_scratch, line_scratch],
        (near_sums, near_totals, swap_cores(near), pairs, tables, tmat, radius, orders, probes, seen),
    )

    near = spread_far(chunk)
    peer = swap_cores(near)
    near_sums, near_gradient = call(
        second_near_body,
        [sums_shape, ((2, FULL), F32)],
        operands=(near, pairs, probes, seen),
        cost=half_cost,
    )
    (send,) = call(second_gradient_body, [share_shape], operands=(peer, probes, seen))
    received = swap_cores(send)
    extra, weights = call(
        second_body,
        [share_shape, ((BLOCKS * BLOCK, LANES), BF)],
        [sum_scratch, shift_scratch],
        (near, near_sums, near_gradient, peer, pairs, tables, tmat, radius, orders, base, image),
        cost=half_cost,
    )
    share = received + extra
    near = spread_far(jnp.broadcast_to(share[None], (FAR, SHARE, LANES)).reshape(FAR * SHARE, LANES))
    (near,) = call(sum_body, [((SCALARS + 8, LANES), F32)], operands=(near,))
    peer = swap_cores(near)
    solution_rows, sensitivity_rows, arnoldi = call(
        finish_body,
        [((OWN, COEFF), F32), ((OWN, COEFF), F32), ((4,), F32)],
        [pltpu.VMEM((LANES, FULL), F32), sum_scratch, shift_scratch],
        (near, peer, weights, tables_t, tmat, orders, incident, image),
        out_spaces={2: pltpu.SMEM},
    )
    return solution_rows, sensitivity_rows, arnoldi


def solution(mesh):
    fine = Mesh(mesh.devices.reshape(2, 2, 4, 2, 4), ALL_AXES)
    split_rows = P(ALL_AXES)
    return jax.shard_map(
        on_device,
        mesh=fine,
        in_specs=(
            P(ALL_AXES, None),
            P(),
            P(),
            P(),
            P(),
            P(),
            split_rows,
            P(ALL_AXES, None),
            split_rows,
        ),
        out_specs=(P(ALL_AXES, None), P(ALL_AXES, None), P()),
        check_vma=False,
    )
```
